32 devices in a mesh: rep: 4 (over x, core), fsdp: 8 (over z, y).
Axes of the slice: x: 2, y: 2, z: 4, core: 2. Of those that a mesh axis runs over, the one named last changes fastest.
Arguments:
- decoder_input: bfloat16 [8, 1024, 768], P('fsdp', 'rep'), may hold values from -6 to 6
- memory: bfloat16 [8, 3072, 768], P('fsdp', 'rep'), may hold values from -6 to 6
- memory_lengths: int32 [8], P('fsdp'), may hold values from 2305 to 3072, as said below
- distance_bucket: int32 [1024], replicated, may hold values from 0 to 31, as said below
- cotangent: float32 [8, 1024, 768], P('fsdp', 'rep'), may hold values from -6 to 6
- self_gain: float32 [768], P('fsdp'), may hold values from 0.5 to 1.5
- self_query: float32 [768, 768], P('fsdp'), may hold values from -0.02734375 to 0.02734375
- self_key: float32 [768, 768], P('fsdp'), may hold values from -0.21875 to 0.21875
- self_value: float32 [768, 768], P('fsdp'), may hold values from -0.21875 to 0.21875
- self_output: float32 [768, 768], P('fsdp'), may hold values from -1.75 to 1.75
- bucket_bias: float32 [384], P('fsdp'), may hold values from -3 to 3
- cross_gain: float32 [768], P('fsdp'), may hold values from 0.5 to 1.5
- cross_query: float32 [768, 768], P('fsdp'), may hold values from -0.02734375 to 0.02734375
- cross_key: float32 [768, 768], P('fsdp'), may hold values from -0.21875 to 0.21875
- cross_value: float32 [768, 768], P('fsdp'), may hold values from -0.21875 to 0.21875
- cross_output: float32 [768, 768], P('fsdp'), may hold values from -2.5 to 2.5
- feed_gain: float32 [768], P('fsdp'), may hold values from 0.5 to 1.5
- gate_weight: float32 [768, 2048], P('fsdp'), may hold values from -0.21875 to 0.21875
- up_weight: float32 [768, 2048], P('fsdp'), may hold values from -0.21875 to 0.21875
- down_weight: float32 [2048, 768], P('fsdp'), may hold values from -0.125 to 0.125
Outputs:
- output: float32 [8, 1024, 768], P('fsdp', 'rep')
- input_grad: float32 [8, 1024, 768], P('fsdp', 'rep')
- memory_grad: float32 [8, 3072, 768], P('fsdp', 'rep')
- self_gain_grad: float32 [768], P('fsdp')
- self_query_grad: float32 [768, 768], P('fsdp')
- self_key_grad: float32 [768, 768], P('fsdp')
- self_value_grad: float32 [768, 768], P('fsdp')
- self_output_grad: float32 [768, 768], P('fsdp')
- bucket_bias_grad: float32 [384], P('fsdp')
- cross_gain_grad: float32 [768], P('fsdp')
- cross_query_grad: float32 [768, 768], P('fsdp')
- cross_key_grad: float32 [768, 768], P('fsdp')
- cross_value_grad: float32 [768, 768], P('fsdp')
- cross_output_grad: float32 [768, 768], P('fsdp')
- feed_gain_grad: float32 [768], P('fsdp')
- gate_weight_grad: float32 [768, 2048], P('fsdp')
- up_weight_grad: float32 [768, 2048], P('fsdp')
- down_weight_grad: float32 [2048, 768], P('fsdp')
The draws below stay inside these ranges and needn't reach their ends.
Inputs may be any that keep to these rules, and one draw needn't show every extreme that they name: `memory_lengths`: one sequence of all has exactly 3072. `distance_bucket`: Non-decreasing in the distance, 0 at distance 0 and 31 at distance 1024 - 1.
All inputs are finite; a program needn't handle non-finite values.
Results may differ from the reference program's by a relative error of at most 0.028.
Values may be sent and summed in bfloat16 or wider, within the bound.
No kernel may reach another device: no remote copies, remote signals or barrier semaphores. Data moves between devices by JAX's collectives and lax.ppermute only.
A program may use at most 256 MiB of HBM per device.

```python
import jax
import jax.numpy as jnp
from jax import lax

D = 768
HEADS = 12
HEAD = 64
FF = 2048
BUCKETS = 32
LEN = 1024
MEM = 3072
SEQS = 8
N_REP = 4


def draw_memory_lengths(key, part):
    key = jax.random.fold_in(key, 11)
    first_key, second_key = jax.random.split(key)
    drawn = jax.random.randint(first_key, (SEQS,), MEM - MEM // N_REP + 1, MEM + 1)
    chosen = jax.random.randint(second_key, (), 0, SEQS)
    slots = jnp.arange(SEQS, dtype=jnp.int32)
    return jnp.where(slots == chosen, MEM, drawn).astype(jnp.int32)


def draw_distance_bucket(key, part):
    key = jax.random.fold_in(key, 23)
    shuffled = jax.random.permutation(key, LEN - 1) + 1
    breaks = shuffled[:BUCKETS - 1]
    distance = jnp.arange(LEN, dtype=jnp.int32)
    return jnp.sum((distance[:, None] >= breaks[None, :]).astype(jnp.int32), 1).astype(jnp.int32)


def steps_of(key, dims, cuts, low, largest):
    def one(dim, blocks):
        steps = jax.random.uniform(jax.random.fold_in(jax.random.fold_in(key, 6), dim), (blocks,), jnp.float32, low / len(cuts), largest / len(cuts))
        return jnp.repeat(jnp.exp(steps), dims[dim] // blocks).reshape((-1,) + (1,) * (len(dims) - dim - 1))

    level = one(*cuts[0])
    for cut in cuts[1:]:
        level = level * one(*cut)
    return level


def gaussian(key, extent, width, most, cuts=(), kind=jnp.bfloat16):
    array = width * jax.random.normal(key, extent, jnp.float32)
    if cuts:
        array = array * steps_of(key, extent, cuts, -0.22, 0.18)
    return jnp.clip(array, -most, most).astype(kind)


def setup_inputs(seed: int = 0) -> dict:
    arg_keys = jax.random.split(jax.random.key(seed), 21)
    decoder_input = gaussian(arg_keys[0], (SEQS, LEN, D), 1.0, 6.0, ((0, 8), (1, 4)))
    memory = gaussian(arg_keys[1], (SEQS, MEM, D), 1.0, 6.0, ((0, 8), (1, 4)))
    memory_lengths = draw_memory_lengths(jax.random.fold_in(arg_keys[20], 71), 0)
    distance_bucket = draw_distance_bucket(jax.random.fold_in(arg_keys[20], 71), 0)
    cotangent = gaussian(arg_keys[4], (SEQS, LEN, D), 1.0, 6.0, ((0, 8), (1, 4)), jnp.float32)
    self_gain = jnp.clip(1.0 + 0.1 * jax.random.normal(arg_keys[5], (D,), jnp.float32), 0.5, 1.5)
    self_query = gaussian(arg_keys[6], (D, HEADS * HEAD), (D * HEAD) ** -0.5, 0.02734375, ((0, 8),), jnp.float32)
    self_key = gaussian(arg_keys[7], (D, HEADS * HEAD), D ** -0.5, 0.21875, ((0, 8),), jnp.float32)
    self_value = gaussian(arg_keys[8], (D, HEADS * HEAD), D ** -0.5, 0.21875, ((0, 8),), jnp.float32)
    self_output = gaussian(arg_keys[9], (HEADS * HEAD, D), (max(HEADS * HEAD // 64, 1)) ** -0.5, 1.75, ((0, 8),), jnp.float32)
    bucket_bias = gaussian(arg_keys[10], (HEADS * BUCKETS,), 0.5, 3.0, ((0, 8),), jnp.float32)
    cross_gain = jnp.clip(1.0 + 0.1 * jax.random.normal(arg_keys[11], (D,), jnp.float32), 0.5, 1.5)
    cross_query = gaussian(arg_keys[12], (D, HEADS * HEAD), (D * HEAD) ** -0.5, 0.02734375, ((0, 8),), jnp.float32)
    cross_key = gaussian(arg_keys[13], (D, HEADS * HEAD), D ** -0.5, 0.21875, ((0, 8),), jnp.float32)
    cross_value = gaussian(arg_keys[14], (D, HEADS * HEAD), D ** -0.5, 0.21875, ((0, 8),), jnp.float32)
    cross_output = gaussian(arg_keys[15], (HEADS * HEAD, D), (max(HEADS * HEAD // 128, 1)) ** -0.5, 2.5, ((0, 8),), jnp.float32)
    feed_gain = jnp.clip(1.0 + 0.1 * jax.random.normal(arg_keys[16], (D,), jnp.float32), 0.5, 1.5)
    gate_weight = gaussian(arg_keys[17], (D, FF), D ** -0.5, 0.21875, ((0, 8),), jnp.float32)
    up_weight = gaussian(arg_keys[18], (D, FF), D ** -0.5, 0.21875, ((0, 8),), jnp.float32)
    down_weight = gaussian(arg_keys[19], (FF, D), FF ** -0.5, 0.125, ((0, 8),), jnp.float32)
    return dict(decoder_input=decoder_input, memory=memory, memory_lengths=memory_lengths, distance_bucket=distance_bucket, cotangent=cotangent, self_gain=self_gain, self_query=self_query, self_key=self_key, self_value=self_value, self_output=self_output, bucket_bias=bucket_bias, cross_gain=cross_gain, cross_query=cross_query, cross_key=cross_key, cross_value=cross_value, cross_output=cross_output, feed_gain=feed_gain, gate_weight=gate_weight, up_weight=up_weight, down_weight=down_weight)


@jax.custom_vjp
def low(v):
    return lax.optimization_barrier(v.astype(jnp.bfloat16)).astype(jnp.float32)

@jax.custom_vjp
def low_back(v):
    return v

def low_keep(v):
    return (low(v), None)

def low_pass(kept, grad):
    return (grad,)

def back_keep(v):
    return (v, None)

def back_low(kept, grad):
    return (low(grad),)
low.defvjp(low_keep, low_pass)
low_back.defvjp(back_keep, back_low)
EPS = 1e-06
NEG = -1e+30
HIGH = lax.Precision.HIGHEST

def both_ways(value):
    return low_back(low(value))

def normalize(values, gain):
    inverse = lax.rsqrt(lax.optimization_barrier(jnp.mean(values * values, -1, keepdims=True)) + EPS)
    return values * inverse * gain

def project(inputs, weight):
    return jnp.dot(inputs, weight, precision=HIGH)

def attention_block(queries, keys, values, bias, mask):
    keys = low_back(keys)
    values = low_back(values)
    query_four = queries.reshape(queries.shape[0], HEADS, HEAD)
    key_four = keys.reshape(keys.shape[0], HEADS, HEAD)
    value_four = values.reshape(values.shape[0], HEADS, HEAD)
    scores = low_back(jnp.einsum('ihd,jhd->hij', query_four, key_four, precision=HIGH) + bias)
    scores = jnp.where(mask[None], scores, NEG)
    highest = lax.optimization_barrier(jnp.max(scores, -1, keepdims=True))
    exponent = jnp.exp(scores - highest)
    weights_soft = low(exponent / lax.optimization_barrier(jnp.sum(exponent, -1, keepdims=True)))
    mixed_heads = jnp.einsum('hij,jhd->ihd', weights_soft, value_four, precision=HIGH)
    return mixed_heads.reshape(queries.shape[0], HEADS * HEAD)

def attention(queries, keys, values, bias_blocks, mask_blocks):
    block_rows = queries.shape[0] // N_REP
    query_blocks = queries.reshape(N_REP, block_rows, HEADS * HEAD)

    def one_block(item):
        return attention_block(item[0], keys, values, item[1], item[2])
    mixed = lax.map(jax.checkpoint(one_block), (query_blocks, bias_blocks, mask_blocks))
    return both_ways(mixed.reshape(N_REP * block_rows, HEADS * HEAD))

def layer_one(lowered, bias_blocks, causal_blocks, length, inputs, memory_rows):
    self_gain, self_query, self_key, self_value, self_output, bias_flat, cross_gain, cross_query, cross_key, cross_value, cross_output, feed_gain, gate_weight, up_weight, down_weight = lowered
    normed_one = low(normalize(inputs, self_gain))
    queries_one = both_ways(project(normed_one, self_query))
    keys_one = low(project(normed_one, self_key))
    values_one = low(project(normed_one, self_value))
    mixed_one = attention(queries_one, keys_one, values_one, bias_blocks, causal_blocks)
    middle = inputs + low_back(project(mixed_one, self_output))
    normed_two = low(normalize(middle, cross_gain))
    queries_two = both_ways(project(normed_two, cross_query))
    keys_two = low(project(memory_rows, cross_key))
    values_two = low(project(memory_rows, cross_value))
    reachable = jnp.arange(MEM, dtype=jnp.int32)[None, :] < length
    reach_blocks = jnp.broadcast_to(reachable[None], (N_REP, 1, MEM))
    zero_blocks = jnp.zeros((N_REP, 1, 1, 1), jnp.float32)
    mixed_two = attention(queries_two, keys_two, values_two, zero_blocks, reach_blocks)
    after_cross = middle + low_back(project(mixed_two, cross_output))
    normed_three = low(normalize(after_cross, feed_gain))
    gate_value = low_back(project(normed_three, gate_weight))
    up_value = low_back(project(normed_three, up_weight))
    hidden = low(jax.nn.gelu(gate_value, approximate=True) * up_value)
    return after_cross + low_back(project(hidden, down_weight))

def forward(inputs, memory_all, masters, memory_lengths, distance_bucket):
    lowered = tuple((low(weight) for weight in masters))
    bias_table = lowered[5].reshape(HEADS, BUCKETS)
    places = jnp.arange(LEN, dtype=jnp.int32)
    distance = places[:, None] - places[None, :]
    causal = distance >= 0
    bucket_place = distance_bucket[jnp.clip(distance, 0, LEN - 1).astype(jnp.int32)]
    bias = bias_table[:, bucket_place]
    block_rows = LEN // N_REP
    bias_blocks = bias.reshape(HEADS, N_REP, block_rows, LEN).transpose(1, 0, 2, 3)
    causal_blocks = causal.reshape(N_REP, block_rows, LEN)

    def one_sequence(item):
        return layer_one(lowered, bias_blocks, causal_blocks, item[0], item[1], item[2])
    return lax.map(jax.checkpoint(one_sequence), (memory_lengths, inputs, memory_all))

def reference(decoder_input, memory, memory_lengths, distance_bucket, cotangent, self_gain, self_query, self_key, self_value, self_output, bucket_bias, cross_gain, cross_query, cross_key, cross_value, cross_output, feed_gain, gate_weight, up_weight, down_weight):
    masters = (self_gain, self_query, self_key, self_value, self_output, bucket_bias, cross_gain, cross_query, cross_key, cross_value, cross_output, feed_gain, gate_weight, up_weight, down_weight)

    def whole_layer(inputs, memory_all, weights_all):
        return forward(inputs, memory_all, weights_all, memory_lengths, distance_bucket)
    output, pullback = jax.vjp(whole_layer, decoder_input.astype(jnp.float32), memory.astype(jnp.float32), masters)
    input_grad, memory_grad, weight_grads = pullback(cotangent)
    return (output, input_grad, memory_grad, weight_grads[0], weight_grads[1], weight_grads[2], weight_grads[3], weight_grads[4], weight_grads[5], weight_grads[6], weight_grads[7], weight_grads[8], weight_grads[9], weight_grads[10], weight_grads[11], weight_grads[12], weight_grads[13], weight_grads[14])
```

```python
import functools

import jax
import jax.numpy as jnp
from jax import lax
from jax.experimental import pallas as pl
from jax.experimental.pallas import tpu as pltpu
from jax.sharding import PartitionSpec as P

HEAD = 64
BUCKETS = 32
EPS = 1e-06
NEG = -1e30
BF = jnp.bfloat16
F32 = jnp.float32
NN = (((1,), (0,)), ((), ()))
NT = (((1,), (1,)), ((), ()))
TN = (((0,), (0,)), ((), ()))
TT = (((0,), (1,)), ((), ()))

CORE = [(0, 1), (1, 0), (2, 3), (3, 2)]
FAR = [(0, 2), (2, 0), (1, 3), (3, 1)]


def core_swap(value):
    return lax.ppermute(value, "rep", CORE)


def far_swap(value):
    return lax.ppermute(value, "rep", FAR)


def dot(left, right, dims=NN):
    return lax.dot_general(left, right, dims, preferred_element_type=F32)


def half_rows(pair, head):
    row = lax.broadcasted_iota(jnp.int32, pair.shape, 0)
    keep = (row < HEAD) if head == 0 else (row >= HEAD)
    return jnp.where(keep, pair, jnp.zeros_like(pair))


def three_terms(value):
    first = value.astype(BF)
    rest = value - first.astype(F32)
    second = rest.astype(BF)
    third = (rest - second.astype(F32)).astype(BF)
    return first, second, third


def extra_rows(first_row, vector):
    terms = three_terms(-vector)
    row = lax.broadcasted_iota(jnp.int32, (128, vector.shape[1]), 0)
    out = jnp.where(row == 0, first_row, 0.0)
    for place, term in enumerate(terms):
        out = jnp.where(row == place + 1, term.astype(F32), out)
    return out.astype(BF)


def attend_kernel(chunk, biased, *refs):
    if biased:
        query, key, value, extra, bias, mixed, log_total = refs
    else:
        query, key, value, extra, mixed, log_total = refs
    keys, rows = key.shape[0], query.shape[1]
    pair = query[...]
    row = lax.broadcasted_iota(jnp.int32, (128, rows), 0)
    one = jnp.where(row == 0, 1.0, 0.0).astype(BF)
    wide = [half_rows(pair, h) for h in range(2)]
    if not biased:
        wide = [jnp.concatenate([w, one], 0) for w in wide]

    def score(part, head):
        span = pl.ds(part * chunk, chunk)
        if biased:
            return dot(key[span, :], wide[head]) + bias[head, span, :].astype(F32)
        return dot(jnp.concatenate([key[span, :], extra[span, :]], 1), wide[head])

    highest = [jnp.full((1, rows), NEG, F32)] * 2
    total = [jnp.zeros((1, rows), F32)] * 2
    acc = [jnp.zeros((HEAD, rows), F32)] * 2
    steps = [(part, head) for part in range(keys // chunk) for head in range(2)]
    ahead = score(*steps[0])
    for index, (part, head) in enumerate(steps):
        scores = ahead
        if index + 1 < len(steps):
            ahead = score(*steps[index + 1])
        span = pl.ds(part * chunk, chunk)
        top = jnp.maximum(highest[head], jnp.max(scores, 0, keepdims=True))
        soft = jnp.exp(scores - top)
        scale = jnp.exp(highest[head] - top)
        total[head] = total[head] * scale + jnp.sum(soft, 0, keepdims=True)
        product = dot(value[span, :], soft.astype(BF), TN)[head * HEAD : (head + 1) * HEAD]
        acc[head] = acc[head] * scale + product
        highest[head] = top
    for head in range(2):
        mixed[pl.ds(head * HEAD, HEAD), :] = (acc[head] / total[head]).astype(BF)
        log_total[0, pl.ds(head, 1), :] = highest[head] + jnp.log(total[head])


def attend(query, keyvalue, extra, bias=None, chunk=512):
    width, rows = query.shape
    keys = keyvalue.shape[0]
    pairs = width // 128
    across = pl.BlockSpec((128, rows), lambda p: (p, 0))
    in_specs = [
        across,
        pl.BlockSpec((keys, 128), lambda p: (0, p)),
        pl.BlockSpec((keys, 128), lambda p: (0, p + pairs)),
        pl.BlockSpec((keys, 128), lambda p: (0, 0)),
    ]
    args = [query, keyvalue, keyvalue, extra]
    if bias is not None:
        in_specs.append(pl.BlockSpec((2, keys, rows), lambda p: (p, 0, 0)))
        args.append(bias)
    return pl.pallas_call(
        functools.partial(attend_kernel, chunk, bias is not None),
        grid=(pairs,),
        in_specs=in_specs,
        out_specs=[across, pl.BlockSpec((1, 8, rows), lambda p: (p, 0, 0))],
        out_shape=[
            jax.ShapeDtypeStruct((width, rows), BF),
            jax.ShapeDtypeStruct((pairs, 8, rows), F32),
        ],
        compiler_params=pltpu.CompilerParams(vmem_limit_bytes=56 * 2**20),
        cost_estimate=pl.CostEstimate(
            flops=8 * keys * rows * width,
            bytes_accessed=4 * keys * width,
            transcendentals=keys * rows * width // HEAD,
        ),
    )(*args)


def attend_back_kernel(chunk, biased, *refs):
    if biased:
        query, key, value, extra, mixed, grad, log_total, bias, d_query, d_key, d_value, d_far = refs
    else:
        query, key, value, extra, mixed, grad, log_total, d_query, d_key, d_value = refs
    keys, rows = key.shape[0], query.shape[1]
    pair, grad_pair = query[...], grad[...]
    product = mixed[...].astype(F32) * grad_pair.astype(F32)
    q_half = [half_rows(pair, h) for h in range(2)]
    g_half = [half_rows(grad_pair, h) for h in range(2)]
    q_wide, g_wide = [], []
    for head in range(2):
        inner = jnp.sum(product[head * HEAD : (head + 1) * HEAD], 0, keepdims=True)
        logs = log_total[0, pl.ds(head, 1), :]
        q_wide.append(jnp.concatenate([q_half[head], extra_rows(1.0, logs)], 0))
        g_wide.append(jnp.concatenate([g_half[head], extra_rows(0.0, inner)], 0))
    if biased:
        block = 256
        down = lax.broadcasted_iota(jnp.int32, (block, block), 0)
        over = lax.broadcasted_iota(jnp.int32, (block, block), 1)
        flip = jnp.where(down + over == block - 1, 1.0, 0.0).astype(BF)
    acc = [jnp.zeros((HEAD, rows), F32) for _ in range(2)]
    for part in range(keys // chunk):
        span = pl.ds(part * chunk, chunk)
        key_wide = jnp.concatenate([key[span, :], extra[span, :]], 1)
        value_wide = jnp.concatenate([value[span, :], extra[span, :]], 1)
        dv, dk = 0.0, 0.0
        for head in range(2):
            scores = dot(key_wide, q_wide[head])
            if biased:
                scores = scores + bias[head, span, :].astype(F32)
            soft = jnp.exp(scores)
            d_scores = (soft * dot(value_wide, g_wide[head])).astype(BF)
            dv = dv + dot(soft.astype(BF), g_half[head], NT)
            dk = dk + dot(d_scores, q_half[head], NT)
            step = dot(key[span, :], d_scores, TN)[head * HEAD : (head + 1) * HEAD]
            acc[head] = acc[head] + step
            if biased:
                for j in range(chunk // block):
                    for i in range(rows // block):
                        tile = d_scores[j * block : (j + 1) * block, i * block : (i + 1) * block]
                        tile = jnp.concatenate([dot(flip, tile), jnp.zeros((block, block), F32)], 1)
                        tile = pltpu.roll(tile, 0, 1, stride=1, stride_axis=0)
                        place = (part * (chunk // block) + j) * (rows // block) + i
                        d_far[0, head, pl.ds(place, 1), :] = jnp.sum(tile, 0, keepdims=True)
        d_value[span, :] = dv.astype(BF)
        d_key[span, :] = dk.astype(BF)
    for head in range(2):
        d_query[pl.ds(head * HEAD, HEAD), :] = acc[head].astype(BF)


def attend_back(query, keyvalue, extra, mixed, grad, log_total, bias=None, chunk=512):
    width, rows = query.shape
    keys = keyvalue.shape[0]
    pairs = width // 128
    across = pl.BlockSpec((128, rows), lambda p: (p, 0))
    along = pl.BlockSpec((keys, 128), lambda p: (0, p))
    in_specs = [
        across,
        along,
        pl.BlockSpec((keys, 128), lambda p: (0, p + pairs)),
        pl.BlockSpec((keys, 128), lambda p: (0, 0)),
        across,
        across,
        pl.BlockSpec((1, 8, rows), lambda p: (p, 0, 0)),
    ]
    args = [query, keyvalue, keyvalue, extra, mixed, grad, log_total]
    out_specs = [across, along, along]
    out_shape = [
        jax.ShapeDtypeStruct((width, rows), BF),
        jax.ShapeDtypeStruct((keys, width), BF),
        jax.ShapeDtypeStruct((keys, width), BF),
    ]
    if bias is not None:
        in_specs.append(pl.BlockSpec((2, keys, rows), lambda p: (p, 0, 0)))
        args.append(bias)
        blocks = (keys // 256) * (rows // 256)
        out_specs.append(pl.BlockSpec((1, 2, blocks, 512), lambda p: (p, 0, 0, 0)))
        out_shape.append(jax.ShapeDtypeStruct((pairs, 2, blocks, 512), F32))
    return pl.pallas_call(
        functools.partial(attend_back_kernel, chunk, bias is not None),
        grid=(pairs,),
        in_specs=in_specs,
        out_specs=out_specs,
        out_shape=out_shape,
        compiler_params=pltpu.CompilerParams(vmem_limit_bytes=56 * 2**20),
        cost_estimate=pl.CostEstimate(
            flops=20 * keys * rows * width,
            bytes_accessed=8 * keys * width,
            transcendentals=keys * rows * width // HEAD,
        ),
    )(*args)


def bias_kernel(starts, line, out):
    head = pl.program_id(0)
    block = 256
    for j in range(4):
        for i in range(2):
            start = pl.multiple_of(starts[j * 2 + i], 128)
            row = line[pl.ds(head, 1), pl.ds(start, 2 * block)]
            tile = pltpu.roll(jnp.broadcast_to(row, (block, 2 * block)), 0, 1, stride=1, stride_axis=0)
            out[0, pl.ds(j * block, block), pl.ds(i * block, block)] = tile[:, block:].astype(BF)


def spread_bias(line, gaps, heads):
    return pl.pallas_call(
        bias_kernel,
        grid_spec=pltpu.PrefetchScalarGridSpec(
            num_scalar_prefetch=1,
            grid=(heads,),
            in_specs=[pl.BlockSpec((8, 2048), lambda h, s: (0, 0))],
            out_specs=pl.BlockSpec((1, 1024, 512), lambda h, s: (h, 0, 0)),
        ),
        out_shape=jax.ShapeDtypeStruct((heads, 1024, 512), BF),
    )(gaps * 256 + 768, line)


def inverse_rms(value):
    return lax.rsqrt(jnp.mean(value * value, -1, keepdims=True) + EPS)


def norm_back(value, inverse, gain, grad):
    scaled = grad * gain
    return inverse * (scaled - value * (inverse * inverse) * jnp.mean(scaled * value, -1, keepdims=True))


def gelu_product(gate_value, up_value):
    return jax.nn.gelu(gate_value, approximate=True) * up_value


def turned(received):
    half = received.shape[0] // 2
    return jnp.concatenate([received[half:], received[:half]], 0).astype(F32)


def gather_rows(local):
    return lax.all_gather(local, "fsdp", axis=0, tiled=True)


def scatter_rows(whole):
    return lax.psum_scatter(whole, "fsdp", scatter_dimension=0, tiled=True)


def per_device(
    decoder_input,
    memory,
    memory_lengths,
    distance_bucket,
    cotangent,
    self_gain,
    self_query,
    self_key,
    self_value,
    self_output,
    bucket_bias,
    cross_gain,
    cross_query,
    cross_key,
    cross_value,
    cross_output,
    feed_gain,
    gate_weight,
    up_weight,
    down_weight,
):
    shards = lax.axis_size("fsdp")
    rep = lax.axis_index("rep")
    side, core = rep // 2, rep % 2
    first = core == 0
    rows = decoder_input.shape[1]
    width = decoder_input.shape[2]
    slots = memory.shape[1]
    half = width // 2
    heads = half // HEAD
    shard_rows = self_query.shape[0]
    hidden_all = gate_weight.shape[1]
    hidden_rows = down_weight.shape[0]
    hidden_half = hidden_rows // 2

    def own_columns(weight):
        return lax.dynamic_slice_in_dim(weight, core * half, half, 1).astype(BF)

    def own_hidden(weight):
        parts = weight.reshape(shard_rows, shards, 2, hidden_half)
        own = lax.dynamic_index_in_dim(parts, core, 2, keepdims=False)
        return own.reshape(shard_rows, hidden_all // 2).astype(BF)

    x_own = decoder_input[0]
    x_pair = jnp.concatenate([x_own, far_swap(x_own)], 0)
    x_all = jnp.concatenate([x_pair, core_swap(x_pair)], 0)
    m_own = memory[0]
    m_pair = jnp.concatenate([m_own, far_swap(m_own)], 0)
    m_all = jnp.concatenate([m_pair, core_swap(m_pair)], 0)
    cot_own = cotangent[0]
    cot = jnp.concatenate([cot_own, core_swap(cot_own)], 0)
    places = jnp.stack([rep, 2 * (1 - side) + core, 2 * side + 1 - core, 2 * (1 - side) + 1 - core])

    columns = jnp.stack(
        [self_gain, cross_gain, feed_gain, jnp.pad(bucket_bias, (0, shard_rows - bucket_bias.shape[0]))], 1
    ).astype(BF)
    pack_one = gather_rows(
        jnp.concatenate(
            [own_columns(self_query), own_columns(self_key), own_columns(self_value), jnp.pad(columns, ((0, 0), (0, 124)))], 1
        )
    )
    pack_two = gather_rows(
        jnp.concatenate(
            [
                own_columns(self_output),
                own_columns(cross_query),
                own_columns(cross_key),
                own_columns(cross_value),
                own_columns(cross_output),
            ],
            1,
        )
    )
    pack_three = gather_rows(jnp.concatenate([own_hidden(gate_weight), own_hidden(up_weight)], 1))
    down_half = lax.dynamic_slice_in_dim(down_weight, core * hidden_half, hidden_half, 0).astype(BF)
    down_matrix = gather_rows(down_half)

    query_one = pack_one[:, :half]
    kv_one = pack_one[:, half : 3 * half]
    gains = pack_one[:, 3 * half : 3 * half + 4].astype(F32)
    gain_one, gain_two, gain_three = gains[:, 0][None], gains[:, 1][None], gains[:, 2][None]
    table = gains[:, 3].reshape(shards, shard_rows)[:, : shard_rows // 2].reshape(2, heads, BUCKETS)
    table = lax.dynamic_index_in_dim(table, core, 0, keepdims=False)
    query_two = pack_two[:, half : 2 * half]
    kv_two = pack_two[:, 2 * half : 4 * half]
    outs = jnp.stack([pack_two[:, :half], pack_two[:, 4 * half :]])
    mine = lax.dynamic_slice_in_dim(outs, core * half, half, 1)
    other = core_swap(lax.dynamic_slice_in_dim(outs, (1 - core) * half, half, 1))
    outs = jnp.concatenate([jnp.where(first, mine, other), jnp.where(first, other, mine)], 2)
    output_one, output_two = outs[0], outs[1]
    gate_matrix = pack_three[:, : hidden_all // 2]
    up_matrix = pack_three[:, hidden_all // 2 :]

    slot = (places[:, None] * slots + jnp.arange(slots, dtype=jnp.int32)[None]).reshape(-1)
    lane = jnp.arange(128, dtype=jnp.int32)[None]
    ones = jnp.where((lane >= 1) & (lane <= 3), 1.0, 0.0)
    extra_two = (jnp.where((lane == 0) & (slot >= memory_lengths[0])[:, None], NEG, 0.0) + ones).astype(BF)
    extra_one = jnp.broadcast_to(ones, (4 * rows, 128)).astype(BF)
    codes = jnp.arange(BUCKETS, dtype=jnp.int32)
    hot = (distance_bucket[None, :] == codes[:, None]).astype(BF)
    line = jnp.einsum("hb,bd->hd", table.astype(BF), hot, preferred_element_type=F32)
    line = jnp.concatenate([jnp.full((heads, 4 * rows), NEG, F32), line], 1)
    line = jnp.pad(line, ((0, 8 - heads), (0, 0)))
    query_places = jnp.stack([places[0], places[2]])
    gaps = (query_places[None, :] - places[:, None]).reshape(-1)
    bias = spread_bias(line, gaps, heads)

    inputs_all = x_all.astype(F32)
    normal_all = inputs_all * inverse_rms(inputs_all)
    n1_all = (normal_all * gain_one).astype(BF)
    n1 = jnp.concatenate([n1_all[:rows], n1_all[2 * rows : 3 * rows]], 0)
    inputs = jnp.concatenate([inputs_all[:rows], inputs_all[2 * rows : 3 * rows]], 0)
    q1 = dot(query_one, n1, TT).astype(BF)
    k1v1 = dot(n1_all, kv_one).astype(BF)
    o1, logs_one = attend(q1, k1v1, extra_one, bias)
    part = dot(o1, output_one, TN)
    middle = inputs + part + turned(core_swap(part.astype(BF)))
    inverse_two = inverse_rms(middle)
    n2 = (middle * inverse_two * gain_two).astype(BF)
    q2 = dot(query_two, n2, TT).astype(BF)
    k2v2 = dot(m_all, kv_two).astype(BF)
    o2, logs_two = attend(q2, k2v2, extra_two)
    part = dot(o2, output_two, TN)
    after = middle + part + turned(core_swap(part.astype(BF)))
    inverse_three = inverse_rms(after)
    n3 = (after * inverse_three * gain_three).astype(BF)
    gate_value = dot(n3, gate_matrix)
    up_value = dot(n3, up_matrix)
    hidden = gelu_product(gate_value, up_value).astype(BF)
    part = dot(hidden, down_matrix)
    output = after[:rows] + part[:rows] + core_swap(part[rows:].astype(BF)).astype(F32)

    cot_low = cot.astype(BF)
    d_hidden = dot(cot_low, down_matrix, NT)
    _, gelu_pull = jax.vjp(gelu_product, gate_value, up_value)
    d_gate, d_up = gelu_pull(d_hidden)
    d_gate, d_up = d_gate.astype(BF), d_up.astype(BF)
    d_down_w = dot(hidden, cot_low, TN).astype(BF)
    d_gate_w = dot(n3, d_gate, TN).astype(BF)
    d_up_w = dot(n3, d_up, TN).astype(BF)
    part = dot(d_gate, gate_matrix, NT) + dot(d_up, up_matrix, NT)
    d_gain_three = jnp.sum(part * (after * inverse_three), 0)
    d_n3 = part + turned(core_swap(part.astype(BF)))
    d_after = cot + norm_back(after, inverse_three, gain_three, d_n3)

    d_after_low = d_after.astype(BF)
    d_output_two = dot(o2, d_after_low).astype(BF)
    d_o2 = dot(output_two, d_after_low, NT).astype(BF)
    d_q2, d_k2, d_v2 = attend_back(q2, k2v2, extra_two, o2, d_o2, logs_two)
    part = dot(d_q2, query_two, TT)
    d_gain_two = jnp.sum(part * (middle * inverse_two), 0)
    d_n2 = part + turned(core_swap(part.astype(BF)))
    d_middle = d_after + norm_back(middle, inverse_two, gain_two, d_n2)
    d_query_two = lax.dot_general(n2, d_q2, TT, preferred_element_type=F32).astype(BF)
    d_key_two = dot(m_all, d_k2, TN).astype(BF)
    d_value_two = dot(m_all, d_v2, TN).astype(BF)
    d_memory = dot(d_k2, kv_two[:, :half], NT) + dot(d_v2, kv_two[:, half:], NT)
    d_memory = d_memory[: 2 * slots] + core_swap(d_memory[2 * slots :].astype(BF)).astype(F32)
    d_memory = d_memory[:slots] + far_swap(d_memory[slots:].astype(BF)).astype(F32)

    d_middle_low = d_middle.astype(BF)
    d_output_one = dot(o1, d_middle_low).astype(BF)
    d_o1 = dot(output_one, d_middle_low, NT).astype(BF)
    d_q1, d_k1, d_v1, d_far = attend_back(q1, k1v1, extra_one, o1, d_o1, logs_one, bias)
    part = dot(d_k1, kv_one[:, :half], NT) + dot(d_v1, kv_one[:, half:], NT)
    part_q = dot(d_q1, query_one, TT)
    none = jnp.zeros((rows, width), F32)
    part = part + jnp.concatenate([part_q[:rows], none, part_q[rows:], none], 0)
    d_gain_one = jnp.sum(part * normal_all, 0)
    d_n1 = part[: 2 * rows] + core_swap(part[2 * rows :].astype(BF)).astype(F32)
    d_n1 = d_n1[:rows] + far_swap(d_n1[rows:].astype(BF)).astype(F32)
    own = inputs_all[:rows]
    d_input = d_middle[:rows] + norm_back(own, inverse_rms(own), gain_one, d_n1)
    d_query_one = lax.dot_general(n1, d_q1, TT, preferred_element_type=F32).astype(BF)
    d_key_one = dot(n1_all, d_k1, TN).astype(BF)
    d_value_one = dot(n1_all, d_v1, TN).astype(BF)
    far = (gaps[:, None] * 256 + jnp.arange(512, dtype=jnp.int32)[None] - 255).reshape(-1)
    below = jnp.sum((distance_bucket[None, :] < codes[:, None]).astype(jnp.int32), 1)
    upto = jnp.sum((distance_bucket[None, :] <= codes[:, None]).astype(jnp.int32), 1)
    inside = ((far[None] >= below[:, None]) & (far[None] < upto[:, None])).astype(F32)
    d_table = jnp.einsum("hd,bd->hb", d_far.reshape(heads, -1), inside, precision=lax.Precision.HIGHEST)

    d_outs = jnp.stack([d_output_one, d_output_two])
    mine = lax.dynamic_slice_in_dim(d_outs, core * half, half, 2)
    other = core_swap(lax.dynamic_slice_in_dim(d_outs, (1 - core) * half, half, 2))
    d_outs = jnp.concatenate([jnp.where(first, mine, other), jnp.where(first, other, mine)], 1)

    def owners(value):
        value = scatter_rows(value)
        value = (value.astype(F32) + far_swap(value).astype(F32)).astype(BF)
        return value, core_swap(value)

    def whole(own, other, axis):
        both = [jnp.where(first, own, other), jnp.where(first, other, own)]
        return jnp.concatenate(both, axis).astype(F32)

    def whole_hidden(own, other):
        both = [jnp.where(first, own, other), jnp.where(first, other, own)]
        both = [b.reshape(shard_rows, shards, 1, hidden_half) for b in both]
        return jnp.concatenate(both, 2).reshape(shard_rows, hidden_all).astype(F32)

    down_own, down_other = owners(d_down_w)
    gu_own, gu_other = owners(jnp.concatenate([d_gate_w, d_up_w], 1))
    cross_own, cross_other = owners(jnp.concatenate([d_query_two, d_key_two, d_value_two, d_outs[1]], 1))
    self_own, self_other = owners(jnp.concatenate([d_query_one, d_key_one, d_value_one, d_outs[0]], 1))
    d_self = [whole(self_own[:, i * half : (i + 1) * half], self_other[:, i * half : (i + 1) * half], 1) for i in range(4)]
    d_cross = [whole(cross_own[:, i * half : (i + 1) * half], cross_other[:, i * half : (i + 1) * half], 1) for i in range(4)]
    wide = hidden_all // 2
    d_gate_out = whole_hidden(gu_own[:, :wide], gu_other[:, :wide])
    d_up_out = whole_hidden(gu_own[:, wide:], gu_other[:, wide:])
    d_down_out = whole(down_own, down_other, 0)

    d_table = d_table.reshape(1, -1)
    d_table = jnp.concatenate([jnp.where(first, d_table, 0.0), jnp.where(first, 0.0, d_table)], 1)[0]
    small = lax.psum(jnp.concatenate([d_gain_one, d_gain_two, d_gain_three, d_table]), ("rep", "fsdp"))
    shard = lax.axis_index("fsdp")
    d_gains = [lax.dynamic_slice_in_dim(small, i * width + shard * shard_rows, shard_rows) for i in range(3)]
    d_bucket = lax.dynamic_slice_in_dim(small, 3 * width + shard * (shard_rows // 2), shard_rows // 2)

    return (
        output[None],
        d_input[None],
        d_memory[None],
        d_gains[0],
        d_self[0],
        d_self[1],
        d_self[2],
        d_self[3],
        d_bucket,
        d_gains[1],
        d_cross[0],
        d_cross[1],
        d_cross[2],
        d_cross[3],
        d_gains[2],
        d_gate_out,
        d_up_out,
        d_down_out,
    )


def solution(mesh):
    split = P("fsdp", "rep", None)
    vector, matrix = P("fsdp"), P("fsdp", None)
    weights = (
        (vector,)
        + (matrix,) * 4
        + (vector, vector)
        + (matrix,) * 4
        + (vector,)
        + (matrix,) * 3
    )
    return jax.shard_map(
        per_device,
        mesh=mesh,
        in_specs=(split, split, vector, P(), split) + weights,
        out_specs=(split, split, split) + weights,
        check_vma=False,
    )
```

```python
import functools

import jax
import jax.numpy as jnp
from jax import lax
from jax.experimental import pallas as pl
from jax.experimental.pallas import tpu as pltpu
from jax.sharding import PartitionSpec as P

HEAD = 64
BUCKETS = 32
EPS = 1e-06
NEG = -1e30
BF = jnp.bfloat16
F32 = jnp.float32
NN = (((1,), (0,)), ((), ()))
NT = (((1,), (1,)), ((), ()))
TN = (((0,), (0,)), ((), ()))
TT = (((0,), (1,)), ((), ()))

CORE = [(0, 1), (1, 0), (2, 3), (3, 2)]
FAR = [(0, 2), (2, 0), (1, 3), (3, 1)]


def core_swap(value):
    return lax.ppermute(value, "rep", CORE)


def far_swap(value):
    return lax.ppermute(value, "rep", FAR)


def dot(left, right, dims=NN):
    return lax.dot_general(left, right, dims, preferred_element_type=F32)


def half_rows(pair, head):
    row = lax.broadcasted_iota(jnp.int32, pair.shape, 0)
    keep = (row < HEAD) if head == 0 else (row >= HEAD)
    return jnp.where(keep, pair, jnp.zeros_like(pair))


def three_terms(value):
    first = value.astype(BF)
    rest = value - first.astype(F32)
    second = rest.astype(BF)
    third = (rest - second.astype(F32)).astype(BF)
    return first, second, third


def extra_rows(first_row, vector):
    terms = three_terms(-vector)
    row = lax.broadcasted_iota(jnp.int32, (128, vector.shape[1]), 0)
    out = jnp.where(row == 0, first_row, 0.0)
    for place, term in enumerate(terms):
        out = jnp.where(row == place + 1, term.astype(F32), out)
    return out.astype(BF)


def spread(line, starts, head, part, blocks, lanes):
    block = 256
    rows = []
    for j in range(blocks):
        tiles = []
        for i in range(lanes):
            start = pl.multiple_of(starts[(part * blocks + j) * lanes + i], 128)
            row = line[pl.ds(head, 1), pl.ds(start, 2 * block)]
            tile = pltpu.roll(jnp.broadcast_to(row, (block, 2 * block)), 0, 1, stride=1, stride_axis=0)
            tiles.append(tile[:, block:])
        rows.append(jnp.concatenate(tiles, 1))
    return jnp.concatenate(rows, 0)


def attend_kernel(chunk, biased, base, *refs):
    if biased:
        starts, query, keyvalue, line, mixed, log_total, bias = refs
    else:
        query, keyvalue, extra, mixed, log_total = refs
    keys, rows = keyvalue.shape[0], query.shape[1]
    key, value = keyvalue.at[:, pl.ds(0, 128)], keyvalue.at[:, pl.ds(128, 128)]
    pair = query[...]
    row = lax.broadcasted_iota(jnp.int32, (128, rows), 0)
    one = jnp.where(row == 0, 1.0, 0.0).astype(BF)
    wide = [half_rows(pair, h) for h in range(2)]
    if not biased:
        wide = [jnp.concatenate([w, one], 0) for w in wide]

    def score(part, head):
        span = pl.ds(part * chunk, chunk)
        if not biased:
            return dot(jnp.concatenate([key[span, :], extra[span, :]], 1), wide[head])
        full = 2 * (base + pl.program_id(0)) + head
        tile = spread(line, starts, full, part, chunk // 256, rows // 256)
        bias[head, span, :] = tile.astype(BF)
        return dot(key[span, :], wide[head]) + tile

    highest = [jnp.full((1, rows), NEG, F32)] * 2
    total = [jnp.zeros((1, rows), F32)] * 2
    acc = [jnp.zeros((HEAD, rows), F32)] * 2
    steps = [(part, head) for part in range(keys // chunk) for head in range(2)]
    ahead = score(*steps[0])
    for index, (part, head) in enumerate(steps):
        scores = ahead
        if index + 1 < len(steps):
            ahead = score(*steps[index + 1])
        span = pl.ds(part * chunk, chunk)
        top = jnp.maximum(highest[head], jnp.max(scores, 0, keepdims=True))
        soft = jnp.exp(scores - top)
        scale = jnp.exp(highest[head] - top)
        total[head] = total[head] * scale + jnp.sum(soft, 0, keepdims=True)
        product = dot(value[span, :], soft.astype(BF), TN)[head * HEAD : (head + 1) * HEAD]
        acc[head] = acc[head] * scale + product
        highest[head] = top
    for head in range(2):
        mixed[pl.ds(head * HEAD, HEAD), :] = (acc[head] / total[head]).astype(BF)
        log_total[0, pl.ds(head, 1), :] = highest[head] + jnp.log(total[head])


def attend(query, keyvalue, extra, line=None, starts=None, chunk=512, base=0, pairs=None, modelled=3):
    rows, keys = query.shape[1], keyvalue.shape[0]
    pairs = query.shape[0] // 128 if pairs is None else pairs
    width = pairs * 128
    biased = line is not None
    in_specs = [pl.BlockSpec((128, rows), lambda p, *s: (p + base, 0)), pl.BlockSpec((keys, 256), lambda p, *s: (0, p + base))]
    out_specs = [pl.BlockSpec((128, rows), lambda p, *s: (p, 0)), pl.BlockSpec((1, 8, rows), lambda p, *s: (p, 0, 0))]
    out_shape = [jax.ShapeDtypeStruct((width, rows), BF), jax.ShapeDtypeStruct((pairs, 8, rows), F32)]
    args = [query, keyvalue]
    if biased:
        args = [starts] + args + [line]
        in_specs.append(pl.BlockSpec(line.shape, lambda p, *s: (0, 0)))
        out_specs.append(pl.BlockSpec((2, keys, rows), lambda p, *s: (p, 0, 0)))
        out_shape.append(jax.ShapeDtypeStruct((2 * pairs, keys, rows), BF))
    else:
        args.append(extra)
        in_specs.append(pl.BlockSpec((keys, 128), lambda p, *s: (0, 0)))
    return pl.pallas_call(
        functools.partial(attend_kernel, chunk, biased, base),
        grid_spec=pltpu.PrefetchScalarGridSpec(
            num_scalar_prefetch=int(biased), grid=(pairs,), in_specs=in_specs, out_specs=out_specs
        ),
        out_shape=out_shape,
        compiler_params=pltpu.CompilerParams(vmem_limit_bytes=56 * 2**20),
        cost_estimate=pl.CostEstimate(flops=1, bytes_accessed=int(3.7e6 * modelled), transcendentals=0),
    )(*args)


def attend_back_kernel(chunk, biased, chained, *refs):
    if biased:
        query, keyvalue, extra, mixed, grad, log_total, bias = refs[:7]
        d_query, d_keyvalue, d_far = refs[7 + chained :]
    else:
        query, keyvalue, extra, mixed, grad, log_total = refs[:6]
        d_query, d_keyvalue = refs[6 + chained :]
    keys, rows = keyvalue.shape[0], query.shape[1]
    key, value = keyvalue.at[:, pl.ds(0, 128)], keyvalue.at[:, pl.ds(128, 128)]
    pair, grad_pair = query[...], grad[...]
    product = mixed[...].astype(F32) * grad_pair.astype(F32)
    q_half = [half_rows(pair, h) for h in range(2)]
    g_half = [half_rows(grad_pair, h) for h in range(2)]
    q_wide, g_wide = [], []
    for head in range(2):
        inner = jnp.sum(product[head * HEAD : (head + 1) * HEAD], 0, keepdims=True)
        logs = log_total[0, pl.ds(head, 1), :]
        q_wide.append(jnp.concatenate([q_half[head], extra_rows(1.0, logs)], 0))
        g_wide.append(jnp.concatenate([g_half[head], extra_rows(0.0, inner)], 0))
    if biased:
        block = 256
        down = lax.broadcasted_iota(jnp.int32, (block, block), 0)
        over = lax.broadcasted_iota(jnp.int32, (block, block), 1)
        flip = jnp.where(down + over == block - 1, 1.0, 0.0).astype(BF)
    acc = [jnp.zeros((HEAD, rows), F32) for _ in range(2)]
    for part in range(keys // chunk):
        span = pl.ds(part * chunk, chunk)
        key_wide = jnp.concatenate([key[span, :], extra[span, :]], 1)
        value_wide = jnp.concatenate([value[span, :], extra[span, :]], 1)
        dv, dk = 0.0, 0.0
        for head in range(2):
            scores = dot(key_wide, q_wide[head])
            if biased:
                scores = scores + bias[head, span, :].astype(F32)
            soft = jnp.exp(scores)
            d_scores = (soft * dot(value_wide, g_wide[head])).astype(BF)
            dv = dv + dot(soft.astype(BF), g_half[head], NT)
            dk = dk + dot(d_scores, q_half[head], NT)
            step = dot(key[span, :], d_scores, TN)[head * HEAD : (head + 1) * HEAD]
            acc[head] = acc[head] + step
            if biased:
                for j in range(chunk // block):
                    for i in range(rows // block):
                        tile = d_scores[j * block : (j + 1) * block, i * block : (i + 1) * block]
                        tile = jnp.concatenate([dot(flip, tile), jnp.zeros((block, block), F32)], 1)
                        tile = pltpu.roll(tile, 0, 1, stride=1, stride_axis=0)
                        place = (part * (chunk // block) + j) * (rows // block) + i
                        d_far[0, head, pl.ds(place, 1), :] = jnp.sum(tile, 0, keepdims=True)
        d_keyvalue[span, :] = jnp.concatenate([dk.astype(BF), dv.astype(BF)], 1)
    for head in range(2):
        d_query[pl.ds(head * HEAD, HEAD), :] = acc[head].astype(BF)


def attend_back(
    query, keyvalue, extra, mixed, grad, log_total, bias=None, chunk=512, base=0, pairs=None, earlier=None, modelled=3
):
    rows, keys = query.shape[1], keyvalue.shape[0]
    pairs = query.shape[0] // 128 if pairs is None else pairs
    width = pairs * 128
    across = pl.BlockSpec((128, rows), lambda p: (p + base, 0))
    along = pl.BlockSpec((keys, 256), lambda p: (0, p + base))
    in_specs = [
        across,
        along,
        pl.BlockSpec((keys, 128), lambda p: (0, 0)),
        across,
        across,
        pl.BlockSpec((1, 8, rows), lambda p: (p + base, 0, 0)),
    ]
    args = [query, keyvalue, extra, mixed, grad, log_total]
    out_specs = [pl.BlockSpec((128, rows), lambda p: (p, 0)), along]
    out_shape = [jax.ShapeDtypeStruct((width, rows), BF), jax.ShapeDtypeStruct(keyvalue.shape, BF)]
    if bias is not None:
        in_specs.append(pl.BlockSpec((2, keys, rows), lambda p: (p + base, 0, 0)))
        args.append(bias)
        blocks = (keys // 256) * (rows // 256)
        out_specs.append(pl.BlockSpec((1, 2, blocks, 512), lambda p: (p, 0, 0, 0)))
        out_shape.append(jax.ShapeDtypeStruct((pairs, 2, blocks, 512), F32))
    aliases = {}
    if earlier is not None:
        aliases = {len(args): 1}
        in_specs.append(pl.BlockSpec(memory_space=pl.ANY))
        args.append(earlier)
    return pl.pallas_call(
        functools.partial(attend_back_kernel, chunk, bias is not None, int(earlier is not None)),
        grid=(pairs,),
        in_specs=in_specs,
        out_specs=out_specs,
        out_shape=out_shape,
        input_output_aliases=aliases,
        compiler_params=pltpu.CompilerParams(vmem_limit_bytes=56 * 2**20),
        cost_estimate=pl.CostEstimate(flops=1, bytes_accessed=int(3.7e6 * modelled), transcendentals=0),
    )(*args)


def beside(left, right):
    rows, half = left.shape
    return jnp.stack([left.reshape(rows, -1, 128), right.reshape(rows, -1, 128)], 2).reshape(rows, 2 * half)


def inverse_rms(value):
    return lax.rsqrt(jnp.mean(value * value, -1, keepdims=True) + EPS)


def norm_back(value, inverse, gain, grad):
    scaled = grad * gain
    return inverse * (scaled - value * (inverse * inverse) * jnp.mean(scaled * value, -1, keepdims=True))


def gelu_product(gate_value, up_value):
    return jax.nn.gelu(gate_value, approximate=True) * up_value


def other_lanes(received):
    half = received.shape[1] // 2
    return jnp.concatenate([received[:, half:], received[:, :half]], 1)


def turned(received):
    half = received.shape[0] // 2
    return jnp.concatenate([received[half:], received[:half]], 0).astype(F32)


def gather_plain(local):
    return lax.all_gather(local, "fsdp", axis=0, tiled=True)


def scatter_plain(whole):
    return lax.psum_scatter(whole, "fsdp", scatter_dimension=0, tiled=True)


RING = (0, 2, 4, 6, 7, 5, 3, 1)
FORTH = [(RING[i], RING[(i + 1) % 8]) for i in range(8)]
BACK = [(after, before) for before, after in FORTH]


def forth(value):
    return lax.ppermute(value, "fsdp", FORTH)


def back(value):
    return lax.ppermute(value, "fsdp", BACK)


def ring_places():
    ring = jnp.array(RING, jnp.int32)
    place = jnp.array([RING.index(i) for i in range(8)], jnp.int32)[lax.axis_index("fsdp")]
    return ring[(place + jnp.array([0, -1, 1, -2, 2, -3, 3, 4], jnp.int32)) % 8]


VMEM = pl.BlockSpec(memory_space=pltpu.VMEM)
EXTRA = 16


def vmem_call(kernel, scalars, args, out_shape, mib=32):
    return pl.pallas_call(
        kernel,
        grid_spec=pltpu.PrefetchScalarGridSpec(
            num_scalar_prefetch=1,
            grid=(),
            in_specs=[VMEM] * len(args),
            out_specs=[VMEM] * len(out_shape),
        ),
        out_shape=out_shape,
        compiler_params=pltpu.CompilerParams(vmem_limit_bytes=mib * 2**20),
    )(scalars, *args)


def pack_small_kernel(core, query, key, value, gain_one, gain_two, gain_three, bucket, out):
    rows, half = query.shape
    out[pl.ds(0, rows), pl.ds(0, half)] = query[...].astype(BF)
    for part in range(half // 128):
        lanes = pl.ds(part * 128, 128)
        out[pl.ds(0, rows), pl.ds(half + part * 256, 128)] = key[:, lanes].astype(BF)
        out[pl.ds(0, rows), pl.ds(half + part * 256 + 128, 128)] = value[:, lanes].astype(BF)
    out[pl.ds(rows, EXTRA), :] = jnp.zeros((EXTRA, out.shape[1]), BF)
    for place, vector in enumerate((gain_one, gain_two, gain_three, bucket)):
        out[pl.ds(rows + place, 1), pl.ds(0, vector.shape[1])] = vector[...].astype(BF)


def pack_columns_kernel(core, output_one, output_two, query, key, value, out):
    half = query.shape[1]
    for place, weight in ((0, output_one), (1, output_two), (2, query)):
        out[:, pl.ds(place * half, half)] = weight[...].astype(BF)
    for part in range(half // 128):
        lanes = pl.ds(part * 128, 128)
        out[:, pl.ds(3 * half + part * 256, 128)] = key[:, lanes].astype(BF)
        out[:, pl.ds(3 * half + part * 256 + 128, 128)] = value[:, lanes].astype(BF)


def pack_halves(kernel, core, weights, vectors, rows):
    half = weights[0].shape[1] // 2
    own = pl.BlockSpec((weights[0].shape[0], half), lambda i, c: (0, c[0]))
    columns = len(weights) * half
    return pl.pallas_call(
        kernel,
        grid_spec=pltpu.PrefetchScalarGridSpec(
            num_scalar_prefetch=1,
            grid=(1,),
            in_specs=[own] * len(weights) + [pl.BlockSpec(v.shape, lambda i, c: (0, 0)) for v in vectors],
            out_specs=pl.BlockSpec((rows, columns), lambda i, c: (0, 0)),
        ),
        out_shape=jax.ShapeDtypeStruct((rows, columns), BF),
    )(core, *weights, *vectors)


def pack_feed_kernel(core, gate, up, down, out):
    rows, wide = gate.shape[0], gate.shape[1] // 2
    for place, weight in enumerate((gate, up)):
        for part in range(wide // 128):
            start = pl.multiple_of(part * 256 + core[0] * 128, 128)
            out[:, pl.ds(place * wide + part * 128, 128)] = weight[:, pl.ds(start, 128)].astype(BF)
    half = down.shape[0] // 2
    top = pl.multiple_of(core[0] * half, 16)
    own = jnp.concatenate([down[pl.ds(top, half), pl.ds(j * 128, 128)].astype(BF) for j in range(down.shape[1] // 128)], 0)
    for part in range(wide // 128):
        out[:, pl.ds(2 * wide + part * 128, 128)] = own[part * rows : (part + 1) * rows]


def unfold_down(whole, shards, width):
    rows, wide = whole.shape[0] // shards, whole.shape[1]
    count = rows * wide // width

    def kernel(_, whole, out):
        for f in range(shards):
            tall = jnp.concatenate([whole[pl.ds(f * rows, rows), pl.ds(j * 128, 128)] for j in range(wide // 128)], 0)
            for j in range(width // 128):
                out[pl.ds(f * count, count), pl.ds(j * 128, 128)] = tall[j * count : (j + 1) * count]

    return vmem_call(kernel, jnp.zeros((1,), jnp.int32), [whole], [jax.ShapeDtypeStruct((shards * count, width), whole.dtype)])[0]


def fold_down(whole, shards, wide):
    width = whole.shape[1]
    count = whole.shape[0] // shards
    rows = count * width // wide

    def kernel(_, whole, out):
        for f in range(shards):
            tall = jnp.concatenate([whole[pl.ds(f * count, count), pl.ds(j * 128, 128)] for j in range(width // 128)], 0)
            for j in range(wide // 128):
                out[pl.ds(f * rows, rows), pl.ds(j * 128, 128)] = tall[j * rows : (j + 1) * rows]

    return vmem_call(kernel, jnp.zeros((1,), jnp.int32), [whole], [jax.ShapeDtypeStruct((shards * rows, wide), whole.dtype)])[0]


def put_in_order(scalars, parts, columns, extra=0, turned=(), fold=None):
    rows = parts[0].shape[0] - extra
    skip = parts[7].shape[0]
    total = 8 * rows

    def kernel(scalars, *refs):
        parts, outs = refs[:9], list(refs[9 : 9 + len(columns)])
        sems = refs[-1]
        if fold is not None:
            outs[-1] = refs[-2]
        copies = []
        for index, part in enumerate(parts):
            place = scalars[min(index, 7)]
            offset = skip if index == 8 else 0
            count = min(part.shape[0], rows - offset)
            lane = 0
            for turn, (out, width) in enumerate(zip(outs, columns)):
                start = place * rows
                if turn in turned:
                    start = lax.rem(start + scalars[8] * (total // 2), total)
                start = pl.multiple_of(start + offset, 16)
                copies.append((part.at[pl.ds(0, count), pl.ds(lane, width)], out.at[pl.ds(start, count), :]))
                lane += width
            if extra and index != 7:
                start = pl.multiple_of(place * extra, 16)
                copies.append(
                    (part.at[pl.ds(part.shape[0] - extra, extra), pl.ds(0, 128)], refs[9 + len(columns)].at[pl.ds(start, extra), :])
                )
        copies = [pltpu.make_async_copy(x, y, sems.at[i]) for i, (x, y) in enumerate(copies)]
        for copy in copies:
            copy.start()
        for copy in copies:
            copy.wait()
        if fold is not None:
            folded, out = refs[-2], refs[8 + len(columns)]
            wide, count = columns[-1], rows * columns[-1] // fold
            for f in range(8):
                tall = jnp.concatenate([folded[pl.ds(f * rows, rows), pl.ds(j * 128, 128)] for j in range(wide // 128)], 0)
                for j in range(fold // 128):
                    out[pl.ds(f * count, count), pl.ds(j * 128, 128)] = tall[j * count : (j + 1) * count]

    out_shape = [jax.ShapeDtypeStruct((total, width), BF) for width in columns]
    scratch = []
    if fold is not None:
        out_shape[-1] = jax.ShapeDtypeStruct((total * columns[-1] // fold, fold), BF)
        scratch.append(pltpu.VMEM((total, columns[-1]), BF))
    if extra:
        out_shape.append(jax.ShapeDtypeStruct((8 * extra, 128), BF))
    return pl.pallas_call(
        kernel,
        grid_spec=pltpu.PrefetchScalarGridSpec(
            num_scalar_prefetch=1,
            grid=(),
            in_specs=[pl.BlockSpec(memory_space=pl.ANY)] * 9,
            out_specs=[VMEM] * len(out_shape),
            scratch_shapes=scratch + [pltpu.SemaphoreType.DMA((9 * len(columns) + 9,))],
        ),
        out_shape=out_shape,
        compiler_params=pltpu.CompilerParams(vmem_limit_bytes=32 * 2**20),
    )(scalars, *parts)


def cut_apart(scalars, columns, extras, turned=()):
    rows = columns[0].shape[0] // 8
    extra = 0 if extras is None else EXTRA
    width = sum(c.shape[1] for c in columns)
    half = (rows + extra) // 32 * 16
    counts = [rows + extra] * 7 + [half, rows + extra - half]

    def kernel(scalars, *refs):
        blocks, outs = refs[: len(columns)], refs[len(refs) - 9 :]
        for index, out in enumerate(outs):
            place = scalars[min(index, 7)]
            skip = half if index == 8 else 0
            count = min(out.shape[0], rows - skip)
            lane = 0
            for turn, block in enumerate(blocks):
                start = place * rows
                if turn in turned:
                    start = lax.rem(start + scalars[8] * 4 * rows, 8 * rows)
                start = pl.multiple_of(start + skip, 16)
                out[pl.ds(0, count), pl.ds(lane, block.shape[1])] = block[pl.ds(start, count), :].astype(BF)
                lane += block.shape[1]
            if extra and index != 7:
                out[pl.ds(count, extra), :] = jnp.zeros((extra, width), BF)
                out[pl.ds(count, extra), pl.ds(0, 128)] = refs[len(columns)][pl.ds(pl.multiple_of(place * extra, 16), extra), :]

    args = list(columns) + ([] if extras is None else [extras])
    return vmem_call(kernel, scalars, args, [jax.ShapeDtypeStruct((count, width), BF) for count in counts], 40)


def held(value, *earlier):
    return lax.optimization_barrier((value,) + earlier)[0]


def gather_hops(local, hops):
    ahead, behind, parts = local
    for _ in range(hops):
        ahead, behind = forth(ahead), back(behind)
        parts = parts + [ahead, behind]
    return ahead, behind, parts


def gather_end(state):
    ahead, behind, parts = state
    half = ahead.shape[0] // 32 * 16
    return parts + [forth(ahead[:half]), back(behind[half:])]


def gather_last(scalars, state, columns, hold=None, **options):
    parts = gather_end(state)
    if hold is not None:
        parts[-2:] = [held(part, hold) for part in parts[-2:]]
    return put_in_order(scalars, parts, columns, **options)


def held_hops(state, hold, hops=1):
    return gather_hops((held(state[0], hold), held(state[1], hold), state[2]), hops)


def add(left, right):
    return (left.astype(F32) + right.astype(F32)).astype(left.dtype)


def add_pair(one, two, three, four):
    def kernel(_, one, two, three, four, left, right):
        for whole, part, out, low in ((one, two, left, False), (three, four, right, True)):
            rows, count = whole.shape[0], part.shape[0]
            start = rows - count if low else 0
            out[pl.ds(start, count), :] = add(whole[pl.ds(start, count), :], part[...])
            if count < rows:
                rest = pl.ds(count if not low else 0, rows - count)
                out[rest, :] = whole[rest, :]

    shape = jax.ShapeDtypeStruct(one.shape, one.dtype)
    return vmem_call(kernel, jnp.zeros((1,), jnp.int32), [one, two, three, four], [shape, shape])


class Scatter:
    def __init__(self, pieces):
        self.own, *self.sides, top, low = pieces
        self.ahead, self.behind = forth(top), back(low)
        self.step = 0

    def wait(self, *others):
        self.ahead, self.behind = lax.optimization_barrier((self.ahead, self.behind) + others)[:2]

    def hop(self):
        m1, p1, m2, p2, m3, p3 = self.sides
        up, down = ((p3, m3), (p2, m2), (p1, m1))[self.step]
        ahead, behind = add_pair(up, self.ahead, down, self.behind)
        self.ahead, self.behind = forth(ahead), back(behind)
        self.step += 1

    def total(self):
        return (self.own.astype(F32) + self.ahead.astype(F32) + self.behind.astype(F32)).astype(BF)


def finish(core, own, other, rows, outputs, weights=(), gain=None, down=None):
    widths = [2 * 128 * len(lanes) for lanes, _, _ in outputs]

    def kernel(core, own, other, *refs):
        weights, refs = refs[: len(weights_given)], refs[len(weights_given) :]
        if gain is not None:
            gain_ref, refs = refs[0], refs[1:]
        outs = refs[: len(outputs)]
        for side, source in ((core[0], own), (1 - core[0], other)):
            for out, (lanes, core_step, block_step) in zip(outs, outputs):
                for index, lane in enumerate(lanes):
                    place = pl.multiple_of(side * core_step + index * block_step, 128)
                    out[:, pl.ds(place, 128)] = source[pl.ds(0, rows), pl.ds(lane, 128)].astype(F32)
            if down is not None:
                out = refs[len(outputs)]
                count, width = out.shape[0] // 2, out.shape[1]
                blocks = count * width // (rows * 128)
                tall = jnp.concatenate([source[:, pl.ds(down + j * 128, 128)] for j in range(blocks)], 0)
                start = pl.multiple_of(side * count, 16)
                for j in range(width // 128):
                    out[pl.ds(start, count), pl.ds(j * 128, 128)] = tall[j * count : (j + 1) * count].astype(F32)
        if gain is not None:
            total = jnp.zeros((rows, 1), F32)
            for weight, out in zip(weights, outs):
                total = total + jnp.sum(weight[...].astype(BF).astype(F32) * out[...], 1, keepdims=True)
            refs[-1][...] = jnp.broadcast_to(total / gain_ref[...].astype(BF).astype(F32), (rows, 128))

    weights_given = list(weights)
    args = [own, other] + weights_given + ([] if gain is None else [gain.reshape(rows, 1)])
    out_shape = [jax.ShapeDtypeStruct((rows, width), F32) for width in widths]
    if down is not None:
        out_shape.append(jax.ShapeDtypeStruct(down_shape(rows, own.shape[1] - down), F32))
    if gain is not None:
        out_shape.append(jax.ShapeDtypeStruct((rows, 128), F32))
    return vmem_call(kernel, core, args, out_shape)


def down_shape(rows, folded):
    return 2 * folded // 8, 8 * rows


def per_device(
    decoder_input,
    memory,
    memory_lengths,
    distance_bucket,
    cotangent,
    self_gain,
    self_query,
    self_key,
    self_value,
    self_output,
    bucket_bias,
    cross_gain,
    cross_query,
    cross_key,
    cross_value,
    cross_output,
    feed_gain,
    gate_weight,
    up_weight,
    down_weight,
):
    shards = lax.axis_size("fsdp")
    rep = lax.axis_index("rep")
    side, core = rep // 2, rep % 2
    first = core == 0
    rows = decoder_input.shape[1]
    width = decoder_input.shape[2]
    slots = memory.shape[1]
    half = width // 2
    heads = half // HEAD
    shard_rows = self_query.shape[0]
    hidden_all = gate_weight.shape[1]
    hidden_rows = down_weight.shape[0]
    hidden_half = hidden_rows // 2

    def both_halves(columns):
        other = turned(core_swap(columns.astype(BF)))
        return jnp.concatenate([jnp.where(first, columns, other), jnp.where(first, other, columns)], 1)

    def own_half(value):
        return lax.dynamic_slice_in_dim(value, core * half, half, 1)

    x_own = decoder_input[0]
    x_pair = jnp.concatenate([x_own, far_swap(x_own)], 0)
    x_all = jnp.concatenate([x_pair, core_swap(x_pair)], 0)
    m_own = memory[0]
    m_far = far_swap(m_own)
    cot_own = cotangent[0]
    cot_other = core_swap(cot_own.astype(BF))
    places = jnp.stack([rep, 2 * (1 - side) + core, 2 * side + 1 - core, 2 * (1 - side) + 1 - core])

    ringed = shards == 8 and shard_rows % 32 == 0 and hidden_half % 128 == 0
    wide = hidden_all // 2
    if ringed:
        which = core.reshape(1)
        ring = jnp.concatenate([ring_places(), which])

        def packed(kernel, args, rows, columns):
            return vmem_call(kernel, which, args, [jax.ShapeDtypeStruct((rows, columns), BF)])[0]

        vectors = [v[None] for v in (self_gain, cross_gain, feed_gain, bucket_bias)]
        local = pack_halves(
            pack_small_kernel, which, [self_query, self_key, self_value], vectors, shard_rows + EXTRA
        )
        state = gather_hops((local, local, [local]), 3)
        query_one, kv_one, extras = gather_last(ring, state, (half, 2 * half), extra=EXTRA)
        local = pack_halves(
            pack_columns_kernel,
            which,
            [self_output, cross_output, cross_query, cross_key, cross_value],
            [],
            shard_rows,
        )
        local = held(local, *state[:2])
        second = gather_hops((local, local, [local]), 2)
        feed = packed(pack_feed_kernel, [gate_weight, up_weight, down_weight], shard_rows, 3 * wide)
        extras = extras.reshape(8, EXTRA, 128)[:, :4, :shard_rows].transpose(1, 0, 2).astype(F32)
        gains, table = extras[:3].reshape(3, width), extras[3, :, : shard_rows // 2].reshape(-1)
    else:

        def own_columns(weight):
            return lax.dynamic_slice_in_dim(weight, core * half, half, 1).astype(BF)

        def own_hidden(weight):
            parts = weight.reshape(shard_rows, shards, 2, hidden_half)
            own = lax.dynamic_index_in_dim(parts, core, 2, keepdims=False)
            return own.reshape(shard_rows, wide).astype(BF)

        def own_beside(left, right):
            return beside(own_columns(left), own_columns(right))

        query_one = gather_plain(own_columns(self_query))
        kv_one = gather_plain(own_beside(self_key, self_value))
        outs = gather_plain(jnp.concatenate([own_columns(self_output), own_columns(cross_output)], 1))
        outs = jnp.where(first, outs, jnp.concatenate([outs[half:], outs[:half]], 0))
        query_two = gather_plain(own_columns(cross_query))
        kv_two = gather_plain(own_beside(cross_key, cross_value))
        gate_matrix = gather_plain(own_hidden(gate_weight))
        up_matrix = gather_plain(own_hidden(up_weight))
        down_half = lax.dynamic_slice_in_dim(down_weight, core * hidden_half, hidden_half, 0).astype(BF)
        down_matrix = gather_plain(down_half)
        gains = jnp.stack([gather_plain(g.astype(BF)).astype(F32) for g in (self_gain, cross_gain, feed_gain)])
        table = gather_plain(bucket_bias.astype(BF)).astype(F32)

    gain_one, gain_two, gain_three = gains[0][None], gains[1][None], gains[2][None]
    table = lax.dynamic_index_in_dim(table.reshape(2, heads, BUCKETS), core, 0, keepdims=False)
    slot = (places[:, None] * slots + jnp.arange(slots, dtype=jnp.int32)[None]).reshape(-1)
    lane = jnp.arange(128, dtype=jnp.int32)[None]
    ones = jnp.where((lane >= 1) & (lane <= 3), 1.0, 0.0)
    extra_two = (jnp.where((lane == 0) & (slot >= memory_lengths[0])[:, None], NEG, 0.0) + ones).astype(BF)
    extra_one = jnp.broadcast_to(ones, (4 * rows, 128)).astype(BF)
    codes = jnp.arange(BUCKETS, dtype=jnp.int32)
    hot = (distance_bucket[None, :] == codes[:, None]).astype(BF)
    line = jnp.einsum("hb,bd->hd", table.astype(BF), hot, preferred_element_type=F32)
    line = jnp.concatenate([jnp.full((heads, 4 * rows), NEG, F32), line], 1)
    line = jnp.pad(line, ((0, 8 - heads), (0, 0)))
    query_places = jnp.stack([places[0], places[2]])
    gaps = (query_places[None, :] - places[:, None]).reshape(-1)
    starts = gaps * 256 + 768

    def owners(value):
        value = add(value, far_swap(value))
        return value, core_swap(value)

    inputs_all = x_all.astype(F32)
    normal_all = inputs_all * inverse_rms(inputs_all)
    n1_all = (normal_all * gain_one).astype(BF)
    n1 = jnp.concatenate([n1_all[:rows], n1_all[2 * rows : 3 * rows]], 0)
    inputs = jnp.concatenate([inputs_all[:rows], inputs_all[2 * rows : 3 * rows]], 0)
    q1 = dot(query_one, n1, TT).astype(BF)
    k1v1 = dot(n1_all, kv_one).astype(BF)
    if ringed:
        q1 = held(q1, cot_other, *second[:2])
        second = gather_hops(second, 1)
    o1, logs_one, bias = attend(q1, k1v1, None, line, starts)
    if ringed:
        o1 = held(o1, *second[:2])
    m_pair = jnp.concatenate([m_own, held(m_far, o1)], 0)
    m_all = jnp.concatenate([m_pair, core_swap(m_pair)], 0)
    if ringed:
        second = held_hops(second, o1, 0)
        outs, query_two, kv_two = gather_last(ring, second, (2 * half, half, 2 * half), m_all, turned=(0,))
        feed = held(feed, query_two)
        feed = gather_hops((feed, feed, [feed]), 1)
    o1_all = jnp.concatenate([o1, other_lanes(core_swap(o1))], 0)
    middle = inputs + both_halves(dot(o1_all, outs[:, :half], TN))
    inverse_two = inverse_rms(middle)
    n2 = (middle * inverse_two * gain_two).astype(BF)
    q2 = dot(query_two, n2, TT).astype(BF)
    k2v2 = dot(m_all, kv_two).astype(BF)
    if ringed:
        feed = held_hops(feed, k2v2)
    o2_a, logs_a = attend(q2, k2v2, extra_two, base=0, pairs=1)
    q2_b = held(q2, o2_a)
    if ringed:
        q2_b = held(q2_b, *feed[:2])
        feed = held_hops(feed, o2_a)
    o2_b, logs_b = attend(q2_b, k2v2, extra_two, base=1, pairs=1)
    q2_c = held(q2, o2_b)
    if ringed:
        q2_c = held(q2_c, *feed[:2])
        feed = gather_end(held_hops(feed, o2_b, 0))
    o2_c, logs_c = attend(q2_c, k2v2, extra_two, base=2, pairs=heads // 2 - 2)
    if ringed:
        o2_c = held(o2_c, *feed[-2:])
    o2 = jnp.concatenate([o2_a, o2_b, o2_c], 0)
    logs_two = jnp.concatenate([logs_a, logs_b, logs_c], 0)
    if ringed:
        gate_matrix, up_matrix, down_matrix = put_in_order(ring, feed, (wide, wide, wide), fold=width)
    other = core_swap(outs[half:])
    own_rows = [jnp.concatenate([jnp.where(first, x, y), jnp.where(first, y, x)], 1) for x, y in
                ((outs[:half, :half], other[:, :half]), (outs[:half, half:], other[:, half:]))]
    output_one, output_two = own_rows
    o2_all = jnp.concatenate([o2, other_lanes(core_swap(o2))], 0)
    after = middle + both_halves(dot(o2_all, outs[:, half:], TN))
    inverse_three = inverse_rms(after)
    n3 = (after * inverse_three * gain_three).astype(BF)
    gate_value = dot(n3, gate_matrix)
    up_value = dot(n3, up_matrix)
    hidden = gelu_product(gate_value, up_value).astype(BF)
    part = dot(hidden, down_matrix)
    output = after[:rows] + part[:rows] + core_swap(part[rows:].astype(BF)).astype(F32)

    cot = jnp.concatenate([cot_own, cot_other.astype(F32)], 0)
    cot_low = cot.astype(BF)
    d_hidden = dot(cot_low, down_matrix, NT)
    _, gelu_pull = jax.vjp(gelu_product, gate_value, up_value)
    d_gate, d_up = gelu_pull(d_hidden)
    d_gate, d_up = d_gate.astype(BF), d_up.astype(BF)
    d_down_w = dot(hidden, cot_low, TN).astype(BF)
    d_gate_w = dot(n3, d_gate, TN).astype(BF)
    d_up_w = dot(n3, d_up, TN).astype(BF)
    part = dot(d_gate, gate_matrix, NT) + dot(d_up, up_matrix, NT)
    d_n3 = part + turned(core_swap(part.astype(BF)))
    d_after = cot + norm_back(after, inverse_three, gain_three, d_n3)

    d_after_low = d_after.astype(BF)
    d_output_two = dot(o2_all, own_half(d_after_low)).astype(BF)
    d_o2 = dot(output_two, d_after_low, NT).astype(BF)
    back_two = functools.partial(attend_back, q2, k2v2, extra_two, o2)
    if ringed:
        feed_ring = Scatter(cut_apart(ring, [d_gate_w, d_up_w, fold_down(d_down_w, shards, wide)], None))
        d_o2 = held(d_o2, feed_ring.own)
    d_q2_a, d_kv2 = back_two(d_o2, logs_two, base=0, pairs=1)
    d_o2_b = held(d_o2, d_q2_a)
    if ringed:
        d_o2_b = held(d_o2_b, feed_ring.ahead, feed_ring.behind)
        feed_ring.hop()
        feed_ring.wait(d_q2_a)
    d_q2_b, d_kv2 = back_two(d_o2_b, logs_two, base=1, pairs=1, earlier=d_kv2)
    d_o2_c = held(d_o2, d_q2_b)
    if ringed:
        d_o2_c = held(d_o2_c, feed_ring.ahead, feed_ring.behind)
        feed_ring.hop()
        feed_ring.wait(d_q2_b)
    d_q2_c, d_kv2 = back_two(d_o2_c, logs_two, base=2, pairs=heads // 2 - 2, earlier=d_kv2)
    if ringed:
        d_q2_c = held(d_q2_c, feed_ring.ahead, feed_ring.behind)
        feed_ring.wait(d_q2_c)
        feed_ring.hop()
    d_q2 = jnp.concatenate([d_q2_a, d_q2_b, d_q2_c], 0)
    part = dot(d_q2, query_two, TT)
    d_n2 = part + turned(core_swap(part.astype(BF)))
    d_middle = d_after + norm_back(middle, inverse_two, gain_two, d_n2)
    d_query_two = lax.dot_general(n2, d_q2, TT, preferred_element_type=F32).astype(BF)
    d_kv_two = dot(m_all, d_kv2, TN).astype(BF)
    d_mem_core = core_swap(dot(d_kv2[2 * slots :], kv_two, NT).astype(BF))
    d_memory = dot(d_kv2[: 2 * slots], kv_two, NT)
    d_memory_far = (d_memory[slots:] + d_mem_core[slots:].astype(F32)).astype(BF)
    d_memory = d_memory[:slots] + d_mem_core[:slots].astype(F32)
    d_memory_far_sum = far_swap(d_memory_far)

    d_middle_low = d_middle.astype(BF)
    d_output_one = dot(o1_all, own_half(d_middle_low)).astype(BF)
    d_o1 = dot(output_one, d_middle_low, NT).astype(BF)
    cross_parts = [d_query_two, d_kv_two, d_output_two, d_output_one]
    if ringed:
        feed_ring.wait(d_memory_far)
        feed_own, feed_other = owners(feed_ring.total())
        cross_ring = Scatter(cut_apart(ring, cross_parts, None, (2, 3)))
        d_o1 = held(d_o1, d_memory_far, cross_ring.own)
    back_one = functools.partial(attend_back, q1, k1v1, extra_one, o1)
    d_q1_a, d_kv1, d_far_a = back_one(d_o1, logs_one, bias, base=0, pairs=1)
    d_o1_b = held(d_o1, d_q1_a)
    if ringed:
        d_o1_b = held(d_o1_b, cross_ring.ahead, cross_ring.behind)
        cross_ring.hop()
        cross_ring.wait(d_q1_a)
    d_q1_b, d_kv1, d_far_b = back_one(d_o1_b, logs_one, bias, base=1, pairs=1, earlier=d_kv1)
    d_o1_c = held(d_o1, d_q1_b)
    if ringed:
        d_o1_c = held(d_o1_c, cross_ring.ahead, cross_ring.behind)
        cross_ring.hop()
        cross_ring.wait(d_q1_b)
    d_q1_c, d_kv1, d_far_c = back_one(d_o1_c, logs_one, bias, base=2, pairs=heads // 2 - 2, earlier=d_kv1)
    if ringed:
        d_q1_c = held(d_q1_c, cross_ring.ahead, cross_ring.behind, d_memory_far_sum)
        cross_ring.wait(d_q1_c)
        cross_ring.hop()
    d_q1 = jnp.concatenate([d_q1_a, d_q1_b, d_q1_c], 0)
    d_far = jnp.concatenate([d_far_a, d_far_b, d_far_c], 0)
    d_query_one = lax.dot_general(n1, d_q1, TT, preferred_element_type=F32).astype(BF)
    d_kv_one = dot(n1_all, d_kv1, TN).astype(BF)
    far = (gaps[:, None] * 256 + jnp.arange(512, dtype=jnp.int32)[None] - 255).reshape(-1)
    below = jnp.sum((distance_bucket[None, :] < codes[:, None]).astype(jnp.int32), 1)
    upto = jnp.sum((distance_bucket[None, :] <= codes[:, None]).astype(jnp.int32), 1)
    inside = ((far[None] >= below[:, None]) & (far[None] < upto[:, None])).astype(F32)
    d_table = jnp.einsum("hd,bd->hb", d_far.reshape(heads, -1), inside, precision=lax.Precision.HIGHEST)

    d_table = d_table.reshape(1, -1)
    d_table = jnp.concatenate([jnp.where(first, d_table, 0.0), jnp.where(first, 0.0, d_table)], 1)
    d_table = d_table.reshape(shards, 1, shard_rows // 2)
    self_parts = [d_query_one, d_kv_one]
    if ringed:
        table_rows = jnp.pad(d_table, ((0, 0), (0, EXTRA - 1), (0, 128 - shard_rows // 2))).astype(BF)
        self_ring = Scatter(cut_apart(ring, self_parts, table_rows.reshape(8 * EXTRA, 128)))
        d_q1 = held(d_q1, self_ring.own)
    d_memory = d_memory + d_memory_far_sum.astype(F32)
    part_q = dot(d_q1, query_one, TT)
    d_n1_core = dot(d_kv1[2 * rows :], kv_one, NT)
    d_n1_core = jnp.concatenate([d_n1_core[:rows] + part_q[rows:], d_n1_core[rows:]], 0)
    d_n1_core = core_swap(d_n1_core.astype(BF)).astype(F32)
    d_n1 = dot(d_kv1[: 2 * rows], kv_one, NT) + d_n1_core
    d_n1_far = d_n1[rows:].astype(BF)
    d_n1 = d_n1[:rows] + part_q[:rows] + far_swap(d_n1_far).astype(F32)
    own = inputs_all[:rows]
    d_input = d_middle[:rows] + norm_back(own, inverse_rms(own), gain_one, d_n1)

    blocks = half // 128
    plain = lambda start: ([start + 128 * i for i in range(blocks)], half, 128)
    turns = lambda start: [([start + 256 * i + 128 * t for i in range(blocks)], half, 128) for t in range(2)]
    if ringed:
        self_ring.hop()
        self_ring.wait(d_n1_far)
        self_ring.hop()
        hidden = lambda start: ([start + 128 * i for i in range(wide // 128)], 128, 256)
        d_gate_out, d_up_out, d_down_out, d_gain_three = finish(
            which, feed_own, feed_other, shard_rows, [hidden(0), hidden(wide)], (gate_weight, up_weight), feed_gain, 2 * wide
        )
        cross_own, cross_other = owners(cross_ring.total())
        self_ring.wait(d_down_out)
        self_ring.hop()
        self_ring.wait(cross_own)
        d_cross = finish(
            which,
            cross_own,
            cross_other,
            shard_rows,
            [plain(0), *turns(half), plain(3 * half), plain(4 * half)],
            (cross_query,),
            cross_gain,
        )
        self_own, self_other = owners(self_ring.total())
        d_self = finish(
            which,
            self_own,
            self_other,
            shard_rows,
            [plain(0), *turns(half)],
            (self_query, self_key, self_value),
            self_gain,
        )
        table_own, table_other = [v[shard_rows, : shard_rows // 2].astype(F32) for v in (self_own, self_other)]
        d_gains = [d_self[3][:, 0], d_cross[5][:, 0], d_gain_three[:, 0]]
        d_output_one_out = d_cross[4]
    else:

        def whole(both, axis=1):
            own, other = both
            return jnp.concatenate([jnp.where(first, own, other), jnp.where(first, other, own)], axis).astype(F32)

        def plain_owners(value):
            return owners(scatter_plain(value))

        def kv_whole(both):
            pick = lambda v, turn: v.reshape(shard_rows, -1, 2, 128)[:, :, turn].reshape(shard_rows, half)
            return [whole([pick(v, turn) for v in both]) for turn in range(2)]

        def hidden_whole(both):
            both = [v.reshape(shard_rows, shards, 1, hidden_half) for v in both]
            return whole(both, 2).reshape(shard_rows, hidden_all)

        def in_order(value):
            return jnp.where(first, value, jnp.concatenate([value[half:], value[:half]], 0))

        def gain_grad(gain, *pairs):
            total = sum(jnp.sum(w.astype(BF).astype(F32) * g, 1) for w, g in pairs)
            return total / gain.astype(BF).astype(F32)

        d_gate_out, d_up_out = [hidden_whole(plain_owners(v)) for v in (d_gate_w, d_up_w)]
        d_down_out = whole(plain_owners(d_down_w), 0)
        d_cross = [whole(plain_owners(d_query_two)), *kv_whole(plain_owners(d_kv_two))]
        d_cross.append(whole(plain_owners(in_order(d_output_two))))
        d_output_one_out = whole(plain_owners(in_order(d_output_one)))
        d_self = [whole(plain_owners(d_query_one)), *kv_whole(plain_owners(d_kv_one))]
        table_own, table_other = [v[0].astype(F32) for v in plain_owners(d_table[:, 0].astype(BF))]
        d_gains = [
            gain_grad(self_gain, (self_query, d_self[0]), (self_key, d_self[1]), (self_value, d_self[2])),
            gain_grad(cross_gain, (cross_query, d_cross[0])),
            gain_grad(feed_gain, (gate_weight, d_gate_out), (up_weight, d_up_out)),
        ]
    d_bucket = table_own + table_other

    return (
        output[None],
        d_input[None],
        d_memory[None],
        d_gains[0],
        d_self[0],
        d_self[1],
        d_self[2],
        d_output_one_out,
        d_bucket,
        d_gains[1],
        d_cross[0],
        d_cross[1],
        d_cross[2],
        d_cross[3],
        d_gains[2],
        d_gate_out,
        d_up_out,
        d_down_out,
    )


def solution(mesh):
    split = P("fsdp", "rep", None)
    vector, matrix = P("fsdp"), P("fsdp", None)
    weights = (
        (vector,)
        + (matrix,) * 4
        + (vector, vector)
        + (matrix,) * 4
        + (vector,)
        + (matrix,) * 3
    )
    return jax.shard_map(
        per_device,
        mesh=mesh,
        in_specs=(split, split, vector, P(), split) + weights,
        out_specs=(split, split, split) + weights,
        check_vma=False,
    )
```

```python
import functools

import jax
import jax.numpy as jnp
from jax import lax
from jax.experimental import pallas as pl
from jax.experimental.pallas import tpu as pltpu
from jax.sharding import PartitionSpec as P

HEAD = 64
BUCKETS = 32
EXTRA = 16
EPS = 1e-06
NEG = -1e30
BF = jnp.bfloat16
F32 = jnp.float32
NN = (((1,), (0,)), ((), ()))
NT = (((1,), (1,)), ((), ()))
TN = (((0,), (0,)), ((), ()))
TT = (((0,), (1,)), ((), ()))

CORE = [(0, 1), (1, 0), (2, 3), (3, 2)]
FAR = [(0, 2), (2, 0), (1, 3), (3, 1)]


def core_swap(value):
    return lax.ppermute(value, "rep", CORE)


def far_swap(value):
    return lax.ppermute(value, "rep", FAR)


def dot(left, right, dims=NN):
    return lax.dot_general(left, right, dims, preferred_element_type=F32)


def half_rows(pair, head):
    row = lax.broadcasted_iota(jnp.int32, pair.shape, 0)
    keep = (row < HEAD) if head == 0 else (row >= HEAD)
    return jnp.where(keep, pair, jnp.zeros_like(pair))


def three_terms(value):
    first = value.astype(BF)
    rest = value - first.astype(F32)
    second = rest.astype(BF)
    third = (rest - second.astype(F32)).astype(BF)
    return first, second, third


def extra_rows(first_row, vector):
    terms = three_terms(-vector)
    row = lax.broadcasted_iota(jnp.int32, (128, vector.shape[1]), 0)
    out = jnp.where(row == 0, first_row, 0.0)
    for place, term in enumerate(terms):
        out = jnp.where(row == place + 1, term.astype(F32), out)
    return out.astype(BF)


def spread(line, starts, head, part, blocks, lanes):
    block = 256
    rows = []
    for j in range(blocks):
        tiles = []
        for i in range(lanes):
            start = pl.multiple_of(starts[(part * blocks + j) * lanes + i], 128)
            row = line[pl.ds(head, 1), pl.ds(start, 2 * block)]
            tile = pltpu.roll(jnp.broadcast_to(row, (block, 2 * block)), 0, 1, stride=1, stride_axis=0)
            tiles.append(tile[:, block:])
        rows.append(jnp.concatenate(tiles, 1))
    return jnp.concatenate(rows, 0)


def attend_kernel(chunk, biased, base, *refs):
    if biased:
        starts, query, keyvalue, line, mixed, log_total = refs
    else:
        query, keyvalue, extra, mixed, log_total = refs
    keys, rows = keyvalue.shape[0], query.shape[1]
    key, value = keyvalue.at[:, pl.ds(0, 128)], keyvalue.at[:, pl.ds(128, 128)]
    pair = query[...]
    row = lax.broadcasted_iota(jnp.int32, (128, rows), 0)
    one = jnp.where(row == 0, 1.0, 0.0).astype(BF)
    wide = [half_rows(pair, h) for h in range(2)]
    if not biased:
        wide = [jnp.concatenate([w, one], 0) for w in wide]

    def score(part, head):
        span = pl.ds(part * chunk, chunk)
        if not biased:
            return dot(jnp.concatenate([key[span, :], extra[span, :]], 1), wide[head])
        full = 2 * (base + pl.program_id(0)) + head
        return dot(key[span, :], wide[head]) + spread(line, starts, full, part, chunk // 256, rows // 256)

    highest = [jnp.full((1, rows), NEG, F32)] * 2
    total = [jnp.zeros((1, rows), F32)] * 2
    acc = [jnp.zeros((HEAD, rows), F32)] * 2
    steps = [(part, head) for part in range(keys // chunk) for head in range(2)]
    ahead = score(*steps[0])
    for index, (part, head) in enumerate(steps):
        scores = ahead
        if index + 1 < len(steps):
            ahead = score(*steps[index + 1])
        span = pl.ds(part * chunk, chunk)
        top = jnp.maximum(highest[head], jnp.max(scores, 0, keepdims=True))
        soft = jnp.exp(scores - top)
        scale = jnp.exp(highest[head] - top)
        total[head] = total[head] * scale + jnp.sum(soft, 0, keepdims=True)
        product = dot(value[span, :], soft.astype(BF), TN)[head * HEAD : (head + 1) * HEAD]
        acc[head] = acc[head] * scale + product
        highest[head] = top
    for head in range(2):
        mixed[pl.ds(head * HEAD, HEAD), :] = (acc[head] / total[head]).astype(BF)
        log_total[0, pl.ds(head, 1), :] = highest[head] + jnp.log(total[head])


def attend(query, keyvalue, extra, line=None, starts=None, chunk=512, base=0, pairs=None, modelled=3):
    rows, keys = query.shape[1], keyvalue.shape[0]
    pairs = query.shape[0] // 128 if pairs is None else pairs
    width = pairs * 128
    biased = line is not None
    in_specs = [pl.BlockSpec((128, rows), lambda p, *s: (p + base, 0)), pl.BlockSpec((keys, 256), lambda p, *s: (0, p + base))]
    out_specs = [pl.BlockSpec((128, rows), lambda p, *s: (p, 0)), pl.BlockSpec((1, 8, rows), lambda p, *s: (p, 0, 0))]
    out_shape = [jax.ShapeDtypeStruct((width, rows), BF), jax.ShapeDtypeStruct((pairs, 8, rows), F32)]
    args = [query, keyvalue]
    if biased:
        args = [starts] + args + [line]
        in_specs.append(pl.BlockSpec(line.shape, lambda p, *s: (0, 0)))
    else:
        args.append(extra)
        in_specs.append(pl.BlockSpec((keys, 128), lambda p, *s: (0, 0)))
    return pl.pallas_call(
        functools.partial(attend_kernel, chunk, biased, base),
        grid_spec=pltpu.PrefetchScalarGridSpec(
            num_scalar_prefetch=int(biased), grid=(pairs,), in_specs=in_specs, out_specs=out_specs
        ),
        out_shape=out_shape,
        compiler_params=pltpu.CompilerParams(vmem_limit_bytes=12 * 2**20),
        cost_estimate=pl.CostEstimate(flops=1, bytes_accessed=int(3.7e6 * modelled), transcendentals=0),
    )(*args)


def attend_back_kernel(chunk, biased, chained, base, *refs):
    if biased:
        starts, query, keyvalue, extra, mixed, grad, log_total, line = refs[:8]
        d_query, d_keyvalue, d_far = refs[8 + chained :]
    else:
        query, keyvalue, extra, mixed, grad, log_total = refs[:6]
        d_query, d_keyvalue = refs[6 + chained :]
    keys, rows = keyvalue.shape[0], query.shape[1]
    key, value = keyvalue.at[:, pl.ds(0, 128)], keyvalue.at[:, pl.ds(128, 128)]
    pair, grad_pair = query[...], grad[...]
    product = mixed[...].astype(F32) * grad_pair.astype(F32)
    q_half = [half_rows(pair, h) for h in range(2)]
    g_half = [half_rows(grad_pair, h) for h in range(2)]
    q_wide, g_wide = [], []
    for head in range(2):
        inner = jnp.sum(product[head * HEAD : (head + 1) * HEAD], 0, keepdims=True)
        logs = log_total[0, pl.ds(head, 1), :]
        q_wide.append(jnp.concatenate([q_half[head], extra_rows(1.0, logs)], 0))
        g_wide.append(jnp.concatenate([g_half[head], extra_rows(0.0, inner)], 0))
    if biased:
        block = 256
        down = lax.broadcasted_iota(jnp.int32, (block, block), 0)
        over = lax.broadcasted_iota(jnp.int32, (block, block), 1)
        flip = jnp.where(down + over == block - 1, 1.0, 0.0).astype(BF)
    acc = [jnp.zeros((HEAD, rows), F32) for _ in range(2)]
    for part in range(keys // chunk):
        span = pl.ds(part * chunk, chunk)
        key_wide = jnp.concatenate([key[span, :], extra[span, :]], 1)
        value_wide = jnp.concatenate([value[span, :], extra[span, :]], 1)
        dv, dk = 0.0, 0.0
        for head in range(2):
            scores = dot(key_wide, q_wide[head])
            if biased:
                full = 2 * (base + pl.program_id(0)) + head
                scores = scores + spread(line, starts, full, part, chunk // 256, rows // 256)
            soft = jnp.exp(scores)
            d_scores = (soft * dot(value_wide, g_wide[head])).astype(BF)
            dv = dv + dot(soft.astype(BF), g_half[head], NT)
            dk = dk + dot(d_scores, q_half[head], NT)
            step = dot(key[span, :], d_scores, TN)[head * HEAD : (head + 1) * HEAD]
            acc[head] = acc[head] + step
            if biased:
                for j in range(chunk // block):
                    for i in range(rows // block):
                        tile = d_scores[j * block : (j + 1) * block, i * block : (i + 1) * block]
                        tile = jnp.concatenate([dot(flip, tile), jnp.zeros((block, block), F32)], 1)
                        tile = pltpu.roll(tile, 0, 1, stride=1, stride_axis=0)
                        place = (part * (chunk // block) + j) * (rows // block) + i
                        d_far[0, head, pl.ds(place, 1), :] = jnp.sum(tile, 0, keepdims=True)
        d_keyvalue[span, :] = jnp.concatenate([dk.astype(BF), dv.astype(BF)], 1)
    for head in range(2):
        d_query[pl.ds(head * HEAD, HEAD), :] = acc[head].astype(BF)


def attend_back(
    query, keyvalue, extra, mixed, grad, log_total, line=None, starts=None, chunk=512, base=0, pairs=None, earlier=None, modelled=3
):
    rows, keys = query.shape[1], keyvalue.shape[0]
    pairs = query.shape[0] // 128 if pairs is None else pairs
    width = pairs * 128
    biased = line is not None
    across = pl.BlockSpec((128, rows), lambda p, *s: (p + base, 0))
    along = pl.BlockSpec((keys, 256), lambda p, *s: (0, p + base))
    in_specs = [
        across,
        along,
        pl.BlockSpec((keys, 128), lambda p, *s: (0, 0)),
        across,
        across,
        pl.BlockSpec((1, 8, rows), lambda p, *s: (p + base, 0, 0)),
    ]
    args = [query, keyvalue, extra, mixed, grad, log_total]
    out_specs = [pl.BlockSpec((128, rows), lambda p, *s: (p, 0)), along]
    out_shape = [jax.ShapeDtypeStruct((width, rows), BF), jax.ShapeDtypeStruct(keyvalue.shape, BF)]
    if biased:
        in_specs.append(pl.BlockSpec(line.shape, lambda p, *s: (0, 0)))
        args = [starts] + args + [line]
        blocks = (keys // 256) * (rows // 256)
        out_specs.append(pl.BlockSpec((1, 2, blocks, 512), lambda p, *s: (p, 0, 0, 0)))
        out_shape.append(jax.ShapeDtypeStruct((pairs, 2, blocks, 512), F32))
    aliases = {}
    if earlier is not None:
        aliases = {len(args): 1}
        in_specs.append(pl.BlockSpec(memory_space=pl.ANY))
        args.append(earlier)
    return pl.pallas_call(
        functools.partial(attend_back_kernel, chunk, biased, int(earlier is not None), base),
        grid_spec=pltpu.PrefetchScalarGridSpec(
            num_scalar_prefetch=int(biased), grid=(pairs,), in_specs=in_specs, out_specs=out_specs
        ),
        out_shape=out_shape,
        input_output_aliases=aliases,
        compiler_params=pltpu.CompilerParams(vmem_limit_bytes=10 * 2**20),
        cost_estimate=pl.CostEstimate(flops=1, bytes_accessed=int(3.7e6 * modelled), transcendentals=0),
    )(*args)


def project_blocks(blocks, weight):
    def kernel(*refs):
        weight, out = refs[-2:]
        row = 0
        for block in refs[:-2]:
            for part in range(block.shape[0] // blocks[0].shape[0]):
                count = blocks[0].shape[0]
                out[pl.ds(row, count), :] = dot(block[pl.ds(part * count, count), :], weight[...]).astype(BF)
                row += count

    rows = sum(block.shape[0] for block in blocks)
    return pl.pallas_call(
        kernel,
        in_specs=[pl.BlockSpec(block.shape, lambda: (0, 0)) for block in blocks] + [pl.BlockSpec(memory_space=pltpu.VMEM)],
        out_specs=pl.BlockSpec(memory_space=pltpu.VMEM),
        out_shape=jax.ShapeDtypeStruct((rows, weight.shape[1]), BF),
        compiler_params=pltpu.CompilerParams(vmem_limit_bytes=12 * 2**20),
        cost_estimate=pl.CostEstimate(flops=1, bytes_accessed=1, transcendentals=0),
    )(*blocks, weight)


def beside(left, right):
    rows, half = left.shape
    return jnp.stack([left.reshape(rows, -1, 128), right.reshape(rows, -1, 128)], 2).reshape(rows, 2 * half)


VMEM = pl.BlockSpec(memory_space=pltpu.VMEM)


def whole_block(shape):
    return pl.BlockSpec(shape, lambda *i: (0,) * len(shape), pipeline_mode=pl.Buffered(1))


def step(kernel, core, args, shapes, mib=10, near=(), scratch=()):
    scalars = core if isinstance(core, tuple) else (core,)
    return pl.pallas_call(
        kernel,
        grid_spec=pltpu.PrefetchScalarGridSpec(
            num_scalar_prefetch=len(scalars),
            grid=(1,),
            in_specs=[VMEM if i in near else whole_block(arg.shape) for i, arg in enumerate(args)],
            out_specs=[VMEM] * len(shapes),
            scratch_shapes=list(scratch),
        ),
        out_shape=[jax.ShapeDtypeStruct(shape, kind) for shape, kind in shapes],
        compiler_params=pltpu.CompilerParams(vmem_limit_bytes=mib * 2**20),
        cost_estimate=pl.CostEstimate(flops=1, bytes_accessed=1, transcendentals=0),
    )(*scalars, *args)


def inverse_rms(value):
    return lax.rsqrt(jnp.mean(value * value, -1, keepdims=True) + EPS)


def norm_back(value, inverse, gain, grad):
    scaled = grad * gain
    return inverse * (scaled - value * (inverse * inverse) * jnp.mean(scaled * value, -1, keepdims=True))


def rows_turned(ref):
    half = ref.shape[0] // 2
    return jnp.concatenate([ref[pl.ds(half, half), :], ref[pl.ds(0, half), :]], 0)


def lanes_turned(ref):
    half = ref.shape[1] // 2
    return jnp.concatenate([ref[:, pl.ds(half, half)], ref[:, pl.ds(0, half)]], 1)


def halves(core, half):
    return pl.ds(pl.multiple_of(core[0] * half, 128), half), pl.ds(pl.multiple_of((1 - core[0]) * half, 128), half)


def first_kernel(core, own, far, near, diagonal, gain, w_query, w_keyvalue, query, keyvalue, normed_t, normed):
    rows = own.shape[0]
    for place, block in enumerate((own, far, near, diagonal)):
        value = block[...].astype(F32)
        value = value * inverse_rms(value) * gain[pl.ds(0, 1), :]
        normed[pl.ds(place * rows, rows), :] = value.astype(BF)
        normed_t[:, pl.ds(place * rows, rows)] = value.T.astype(BF)
    keyvalue[...] = dot(normed[...], w_keyvalue[...]).astype(BF)
    mine = jnp.concatenate([normed[pl.ds(0, rows), :], normed[pl.ds(2 * rows, rows), :]], 0)
    query[...] = dot(mine, w_query[...]).T.astype(BF)


def prepare_kernel(core, extras, buckets, gains, line):
    shards, count = 8, gains.shape[1] // 8
    pieces = [extras[pl.ds(f * EXTRA, 8), :].astype(F32) for f in range(shards)]
    gains[...] = jnp.concatenate([piece[:, :count] for piece in pieces], 1)
    table = jnp.concatenate([piece[3:4, : count // 2] for piece in pieces], 1)
    entries = table.shape[1]
    heads = entries // BUCKETS // 2
    head = lax.broadcasted_iota(jnp.int32, (8, entries), 0)
    entry = lax.broadcasted_iota(jnp.int32, (8, entries), 1)
    first = (core[0] * heads + head) * BUCKETS
    mine = (entry >= first) & (entry < first + BUCKETS) & (head < heads)
    rows = jnp.where(mine, jnp.broadcast_to(table, (8, entries)), 0.0).astype(BF)
    length = buckets.shape[1]
    code = lax.broadcasted_iota(jnp.int32, (entries, length), 0) & (BUCKETS - 1)
    hot = jnp.where(code == buckets[...], 1.0, 0.0).astype(BF)
    line[:, pl.ds(0, length)] = jnp.full((8, length), NEG, F32)
    line[:, pl.ds(length, length)] = dot(rows, hot)


def table_kernel(core, starts, below, upto, far_a, far_b, out):
    heads = 2 * (far_a.shape[0] + far_b.shape[0])
    total = jnp.zeros((8, BUCKETS), F32)
    for block in range(8):
        rows = [far[p, h, pl.ds(block, 1), :] for far in (far_a, far_b) for p in range(far.shape[0]) for h in range(2)]
        rows = jnp.concatenate(rows + [jnp.zeros((8 - heads, 512), F32)], 0)
        distance = lax.broadcasted_iota(jnp.int32, (512, BUCKETS), 0) + (starts[block] - 1023)
        hot = jnp.where((distance >= below[...]) & (distance < upto[...]), 1.0, 0.0).astype(BF)
        for term in three_terms(rows):
            total = total + dot(term, hot)
    entries = 2 * heads * BUCKETS
    spot = lax.broadcasted_iota(jnp.int32, (BUCKETS, entries), 1) - lax.broadcasted_iota(jnp.int32, (BUCKETS, entries), 0)
    line = jnp.zeros((1, entries), F32)
    for head in range(heads):
        pick = jnp.where(spot == (core[0] * heads + head) * BUCKETS, 1.0, 0.0).astype(BF)
        line = line + dot(total[head : head + 1].astype(BF), pick)
    out[...] = jnp.zeros(out.shape, BF)
    count = entries // 8
    for f in range(8):
        out[pl.ds(f * EXTRA, 1), pl.ds(0, count)] = line[:, f * count : (f + 1) * count].astype(BF)


def mix_kernel(core, mixed, other, weight, columns, low):
    half = mixed.shape[0]
    total = dot(mixed[...], weight[pl.ds(0, half), :], TN) + dot(lanes_turned(other), weight[pl.ds(half, half), :], TN)
    columns[...] = total
    low[...] = total.astype(BF)


def stacked(refs):
    blocks = [ref[...].astype(F32) for ref in refs]
    return blocks[0] if len(blocks) == 1 else jnp.concatenate(blocks, 0)


def norm_kernel(parts, projected, which, core, *refs):
    base, (columns, other, gain) = refs[:parts], refs[parts : parts + 3]
    value, normed, normed_t = refs[parts + 3 + projected : parts + 6 + projected]
    mine, theirs = halves(core, columns.shape[1])
    value[...] = stacked(base)
    value[:, mine] += columns[...]
    value[:, theirs] += rows_turned(other).astype(F32)
    whole = value[...]
    whole = whole * inverse_rms(whole) * gain[pl.ds(which, 1), :]
    normed[...] = whole.astype(BF)
    normed_t[...] = whole.T.astype(BF)
    if projected:
        refs[-1][...] = dot(normed[...], refs[parts + 3][...]).T.astype(BF)


def feed_kernel(core, normed, normed_t, gate, up, down, cot_own, cot_other, part, grads, d_down, d_normed, d_low):
    wide = gate.shape[1]
    scale, cubic = 0.7978845608028654, 0.044715
    grad_out = jnp.concatenate([cot_own[...], cot_other[...]], 0)
    total, back_total = 0.0, 0.0
    for start in range(0, wide, 256):
        span = pl.ds(start, 256)
        g = dot(normed[...], gate[:, span])
        u = dot(normed[...], up[:, span])
        square = g * g
        t = jnp.tanh(scale * (g + cubic * square * g))
        act = 0.5 * g * (1.0 + t)
        slope = 0.5 * (1.0 + t) + 0.5 * g * (1.0 - t * t) * (scale * (1.0 + 3.0 * cubic * square))
        hidden = (act * u).astype(BF)
        d_hidden = dot(grad_out, down[span, :], NT)
        d_gate = (d_hidden * u * slope).astype(BF)
        d_up = (d_hidden * act).astype(BF)
        total = total + dot(hidden, down[span, :])
        back_total = back_total + dot(d_gate, gate[:, span], NT) + dot(d_up, up[:, span], NT)
        grads[:, span] = dot(normed_t[...], d_gate).astype(BF)
        grads[:, pl.ds(wide + start, 256)] = dot(normed_t[...], d_up).astype(BF)
        d_down[span, :] = dot(hidden, grad_out, TN).astype(BF)
    part[...] = total.astype(BF)
    d_normed[...] = back_total
    d_low[...] = back_total.astype(BF)


def back_kernel(parts, which, core, *refs):
    part, other, value, gain = refs[:4]
    base = refs[4 : 4 + parts]
    weight, w_theirs, mixed, mixed_other = refs[4 + parts : 8 + parts]
    d_value, d_mixed, d_weight = refs[8 + parts :]
    half = weight.shape[1]
    grad = part[...] + rows_turned(other).astype(F32)
    whole = value[...]
    d_value[...] = stacked(base) + norm_back(whole, inverse_rms(whole), gain[pl.ds(which, 1), :], grad)
    mine, theirs = halves(core, half)
    d_mine, d_theirs = d_value[:, mine].astype(BF), d_value[:, theirs].astype(BF)
    d_mixed[...] = (dot(weight[pl.ds(0, half), :], d_mine, NT) + dot(w_theirs[pl.ds(half, half), :], d_theirs, NT)).astype(BF)
    d_weight[pl.ds(0, half), :] = dot(mixed[...], d_mine).astype(BF)
    d_weight[pl.ds(half, half), :] = dot(lanes_turned(mixed_other), d_mine).astype(BF)


def query_kernel(core, d_query, weight, normed_t, part, low, d_weight):
    grad = d_query[...].astype(F32).T.astype(BF)
    total = dot(grad, weight[...], NT)
    part[...] = total
    low[...] = total.astype(BF)
    d_weight[...] = dot(normed_t[...], d_query[...], NT).astype(BF)


def first_weights_kernel(core, d_query, d_keyvalue, normed_t, d_w_query, d_w_keyvalue):
    rows = d_query.shape[1] // 2
    d_w_query[...] = (
        dot(normed_t[:, pl.ds(0, rows)], d_query[:, pl.ds(0, rows)], NT)
        + dot(normed_t[:, pl.ds(2 * rows, rows)], d_query[:, pl.ds(rows, rows)], NT)
    ).astype(BF)
    d_w_keyvalue[...] = dot(normed_t[...], d_keyvalue[...]).astype(BF)


def first_back_kernel(core, d_query, d_keyvalue, w_query, w_keyvalue, near, low):
    rows = d_query.shape[1] // 2
    grad = d_query[...].astype(F32).T.astype(BF)
    near[...] = dot(d_keyvalue[pl.ds(0, 2 * rows), :], w_keyvalue[...], NT)
    near[pl.ds(0, rows), :] += dot(grad[:rows], w_query[...], NT)
    total = dot(d_keyvalue[pl.ds(2 * rows, 2 * rows), :], w_keyvalue[...], NT)
    low[pl.ds(0, rows), :] = (total[:rows] + dot(grad[rows:], w_query[...], NT)).astype(BF)
    low[pl.ds(rows, rows), :] = total[rows:].astype(BF)


def first_sum_kernel(core, near, other, own, far):
    rows = own.shape[0]
    own[...] = near[pl.ds(0, rows), :] + other[pl.ds(0, rows), :].astype(F32)
    far[...] = (near[pl.ds(rows, rows), :] + other[pl.ds(rows, rows), :].astype(F32)).astype(BF)


def input_kernel(core, value, gain, own, far, base, out):
    whole = value[...].astype(F32)
    grad = own[...] + far[...].astype(F32)
    out[...] = base[...] + norm_back(whole, inverse_rms(whole), gain[pl.ds(0, 1), :], grad)


def gather_plain(local):
    return lax.all_gather(local, "fsdp", axis=0, tiled=True)


def scatter_plain(whole):
    return lax.psum_scatter(whole, "fsdp", scatter_dimension=0, tiled=True)


RING = (0, 2, 4, 6, 7, 5, 3, 1)
FORTH = [(RING[i], RING[(i + 1) % 8]) for i in range(8)]
BACK = [(after, before) for before, after in FORTH]


def forth(value):
    return lax.ppermute(value, "fsdp", FORTH)


def back(value):
    return lax.ppermute(value, "fsdp", BACK)


def ring_places():
    shard = lax.axis_index("fsdp")
    place = jnp.where(shard % 2 == 0, shard // 2, 7 - shard // 2)
    places = (place + jnp.array([0, -1, 1, -2, 2, -3, 3, 4], jnp.int32)) % 8
    return jnp.where(places < 4, 2 * places, 15 - 2 * places)


def vmem_call(kernel, scalars, args, out_shape, mib=10):
    return pl.pallas_call(
        kernel,
        grid_spec=pltpu.PrefetchScalarGridSpec(
            num_scalar_prefetch=1,
            grid=(1,),
            in_specs=[whole_block(arg.shape) for arg in args],
            out_specs=[whole_block(out.shape) for out in out_shape],
        ),
        out_shape=out_shape,
        compiler_params=pltpu.CompilerParams(vmem_limit_bytes=mib * 2**20),
    )(scalars, *args)


def pack_small_kernel(core, query, key, value, gain_one, gain_two, gain_three, bucket, out):
    rows, half = query.shape
    out[pl.ds(0, rows), pl.ds(0, half)] = query[...].astype(BF)
    for part in range(half // 128):
        lanes = pl.ds(part * 128, 128)
        out[pl.ds(0, rows), pl.ds(half + part * 256, 128)] = key[:, lanes].astype(BF)
        out[pl.ds(0, rows), pl.ds(half + part * 256 + 128, 128)] = value[:, lanes].astype(BF)
    out[pl.ds(rows, EXTRA), :] = jnp.zeros((EXTRA, out.shape[1]), BF)
    for place, vector in enumerate((gain_one, gain_two, gain_three, bucket)):
        out[pl.ds(rows + place, 1), pl.ds(0, vector.shape[1])] = vector[...].astype(BF)


def pack_columns_kernel(core, output_one, output_two, query, key, value, out):
    half = query.shape[1]
    for place, weight in ((0, output_one), (1, output_two), (2, query)):
        out[:, pl.ds(place * half, half)] = weight[...].astype(BF)
    for part in range(half // 128):
        lanes = pl.ds(part * 128, 128)
        out[:, pl.ds(3 * half + part * 256, 128)] = key[:, lanes].astype(BF)
        out[:, pl.ds(3 * half + part * 256 + 128, 128)] = value[:, lanes].astype(BF)


def pack_halves(kernel, core, weights, vectors, rows, mib):
    half = weights[0].shape[1] // 2
    own = pl.BlockSpec((weights[0].shape[0], half), lambda i, c: (0, c[0]))
    columns = len(weights) * half
    return pl.pallas_call(
        kernel,
        grid_spec=pltpu.PrefetchScalarGridSpec(
            num_scalar_prefetch=1,
            grid=(1,),
            in_specs=[own] * len(weights) + [pl.BlockSpec(v.shape, lambda i, c: (0, 0)) for v in vectors],
            out_specs=pl.BlockSpec((rows, columns), lambda i, c: (0, 0)),
        ),
        out_shape=jax.ShapeDtypeStruct((rows, columns), BF),
        compiler_params=pltpu.CompilerParams(vmem_limit_bytes=mib * 2**20),
    )(core, *weights, *vectors)


def pack_feed_kernel(core, gate, up, down, out):
    rows, wide = gate.shape[0], gate.shape[1] // 2
    for place, weight in enumerate((gate, up)):
        for part in range(wide // 128):
            start = pl.multiple_of(part * 256 + core[0] * 128, 128)
            out[:, pl.ds(place * wide + part * 128, 128)] = weight[:, pl.ds(start, 128)].astype(BF)
    half = down.shape[0] // 2
    top = pl.multiple_of(core[0] * half, 16)
    own = jnp.concatenate([down[pl.ds(top, half), pl.ds(j * 128, 128)].astype(BF) for j in range(down.shape[1] // 128)], 0)
    for part in range(wide // 128):
        out[:, pl.ds(2 * wide + part * 128, 128)] = own[part * rows : (part + 1) * rows]


def unfold_down(whole, shards, width):
    rows, wide = whole.shape[0] // shards, whole.shape[1]
    count = rows * wide // width

    def kernel(_, whole, out):
        for f in range(shards):
            tall = jnp.concatenate([whole[pl.ds(f * rows, rows), pl.ds(j * 128, 128)] for j in range(wide // 128)], 0)
            for j in range(width // 128):
                out[pl.ds(f * count, count), pl.ds(j * 128, 128)] = tall[j * count : (j + 1) * count]

    return vmem_call(kernel, jnp.zeros((1,), jnp.int32), [whole], [jax.ShapeDtypeStruct((shards * count, width), whole.dtype)])[0]


def fold_down(whole, shards, wide):
    width = whole.shape[1]
    count = whole.shape[0] // shards
    rows = count * width // wide

    def kernel(_, whole, out):
        for f in range(shards):
            tall = jnp.concatenate([whole[pl.ds(f * count, count), pl.ds(j * 128, 128)] for j in range(width // 128)], 0)
            for j in range(wide // 128):
                out[pl.ds(f * rows, rows), pl.ds(j * 128, 128)] = tall[j * rows : (j + 1) * rows]

    return vmem_call(kernel, jnp.zeros((1,), jnp.int32), [whole], [jax.ShapeDtypeStruct((shards * rows, wide), whole.dtype)])[0]


def put_in_order(scalars, parts, columns, extra=0, turned=(), fold=None):
    rows = parts[0].shape[0] - extra
    skip = parts[7].shape[0]
    total = 8 * rows

    def kernel(scalars, *refs):
        parts, outs = refs[:9], list(refs[9 : 9 + len(columns)])
        sems = refs[-1]
        if fold is not None:
            outs[-1] = refs[-2]
        copies = []
        for index, part in enumerate(parts):
            place = scalars[min(index, 7)]
            offset = skip if index == 8 else 0
            count = min(part.shape[0], rows - offset)
            lane = 0
            for turn, (out, width) in enumerate(zip(outs, columns)):
                start = place * rows
                if turn in turned:
                    start = lax.rem(start + scalars[8] * (total // 2), total)
                start = pl.multiple_of(start + offset, 16)
                copies.append((part.at[pl.ds(0, count), pl.ds(lane, width)], out.at[pl.ds(start, count), :]))
                lane += width
            if extra and index != 7:
                start = pl.multiple_of(place * extra, 16)
                copies.append(
                    (part.at[pl.ds(part.shape[0] - extra, extra), pl.ds(0, 128)], refs[9 + len(columns)].at[pl.ds(start, extra), :])
                )
        copies = [pltpu.make_async_copy(x, y, sems.at[i]) for i, (x, y) in enumerate(copies)]
        for copy in copies:
            copy.start()
        for copy in copies:
            copy.wait()
        if fold is not None:
            folded, out = refs[-2], refs[8 + len(columns)]
            wide, count = columns[-1], rows * columns[-1] // fold
            for f in range(8):
                tall = jnp.concatenate([folded[pl.ds(f * rows, rows), pl.ds(j * 128, 128)] for j in range(wide // 128)], 0)
                for j in range(fold // 128):
                    out[pl.ds(f * count, count), pl.ds(j * 128, 128)] = tall[j * count : (j + 1) * count]

    out_shape = [jax.ShapeDtypeStruct((total, width), BF) for width in columns]
    scratch = []
    if fold is not None:
        out_shape[-1] = jax.ShapeDtypeStruct((total * columns[-1] // fold, fold), BF)
        scratch.append(pltpu.VMEM((total, columns[-1]), BF))
    if extra:
        out_shape.append(jax.ShapeDtypeStruct((8 * extra, 128), BF))
    return pl.pallas_call(
        kernel,
        grid_spec=pltpu.PrefetchScalarGridSpec(
            num_scalar_prefetch=1,
            grid=(),
            in_specs=[pl.BlockSpec(memory_space=pltpu.HBM)] * 9,
            out_specs=[VMEM] * len(out_shape),
            scratch_shapes=scratch + [pltpu.SemaphoreType.DMA((9 * len(columns) + 9,))],
        ),
        out_shape=out_shape,
        compiler_params=pltpu.CompilerParams(vmem_limit_bytes=4 * 2**20),
    )(scalars, *parts)


def cut_apart(scalars, columns, extras, turned=()):
    rows = columns[0].shape[0] // 8
    extra = 0 if extras is None else EXTRA
    width = sum(c.shape[1] for c in columns)
    half = (rows + extra) // 32 * 16
    counts = [rows + extra] * 7 + [half, rows + extra - half]

    def kernel(scalars, *refs):
        blocks, outs, sems = refs[: len(columns)], refs[len(refs) - 10 : -1], refs[-1]
        copies = []
        for index, out in enumerate(outs):
            place = scalars[min(index, 7)]
            skip = half if index == 8 else 0
            count = min(out.shape[0], rows - skip)
            lane = 0
            for turn, block in enumerate(blocks):
                start = place * rows
                if turn in turned:
                    start = lax.rem(start + scalars[8] * 4 * rows, 8 * rows)
                start = pl.multiple_of(start + skip, 16)
                copies.append((block.at[pl.ds(start, count), :], out.at[pl.ds(0, count), pl.ds(lane, block.shape[1])]))
                lane += block.shape[1]
            if extra and index != 7:
                start = pl.multiple_of(place * extra, 16)
                copies.append((refs[len(columns)].at[pl.ds(start, extra), :], out.at[pl.ds(count, extra), :]))
        copies = [pltpu.make_async_copy(x, y, sems.at[i]) for i, (x, y) in enumerate(copies)]
        for copy in copies:
            copy.start()
        for copy in copies:
            copy.wait()

    args = list(columns) + ([] if extras is None else [extras])
    out_shape = [jax.ShapeDtypeStruct((count, width), BF) for count in counts]
    return pl.pallas_call(
        kernel,
        grid_spec=pltpu.PrefetchScalarGridSpec(
            num_scalar_prefetch=1,
            grid=(),
            in_specs=[VMEM] * len(args),
            out_specs=[pl.BlockSpec(memory_space=pl.ANY)] * 9,
            scratch_shapes=[pltpu.SemaphoreType.DMA((9 * len(columns) + 9,))],
        ),
        out_shape=out_shape,
        compiler_params=pltpu.CompilerParams(vmem_limit_bytes=4 * 2**20),
    )(scalars, *args)


def held(value, *earlier):
    return lax.optimization_barrier((value,) + earlier)[0]


def gather_hops(local, hops):
    ahead, behind, parts = local
    for _ in range(hops):
        ahead, behind = forth(ahead), back(behind)
        parts = parts + [ahead, behind]
    return ahead, behind, parts


def gather_end(state):
    ahead, behind, parts = state
    half = ahead.shape[0] // 32 * 16
    return parts + [forth(ahead[:half]), back(behind[half:])]


def gather_last(scalars, state, columns, hold=None, **options):
    parts = gather_end(state)
    if hold is not None:
        parts[-2:] = [held(part, hold) for part in parts[-2:]]
    return put_in_order(scalars, parts, columns, **options)


def held_hops(state, hold, hops=1):
    return gather_hops((held(state[0], hold), held(state[1], hold), state[2]), hops)


def add(left, right):
    return (left.astype(F32) + right.astype(F32)).astype(left.dtype)


def add_pair(one, two, three, four):
    def kernel(*refs):
        parts, (left, right), held_parts, sems = refs[:4], refs[4:6], refs[6:10], refs[10]
        copies = [pltpu.make_async_copy(x, y, sems.at[i]) for i, (x, y) in enumerate(zip(parts, held_parts))]
        for copy in copies:
            copy.start()
        for copy in copies:
            copy.wait()
        for whole, part, out, low in ((*held_parts[:2], left, False), (*held_parts[2:], right, True)):
            rows, count = whole.shape[0], part.shape[0]
            start = rows - count if low else 0
            out[pl.ds(start, count), :] = add(whole[pl.ds(start, count), :], part[...])
            if count < rows:
                rest = pl.ds(count if not low else 0, rows - count)
                out[rest, :] = whole[rest, :]

    shape = jax.ShapeDtypeStruct(one.shape, one.dtype)
    args = [one, two, three, four]
    return pl.pallas_call(
        kernel,
        in_specs=[pl.BlockSpec(memory_space=pl.ANY)] * 4,
        out_specs=[pl.BlockSpec(memory_space=pltpu.VMEM)] * 2,
        out_shape=[shape, shape],
        scratch_shapes=[pltpu.VMEM(arg.shape, arg.dtype) for arg in args] + [pltpu.SemaphoreType.DMA((4,))],
        compiler_params=pltpu.CompilerParams(vmem_limit_bytes=8 * 2**20),
        cost_estimate=pl.CostEstimate(flops=1, bytes_accessed=1, transcendentals=0),
    )(*args)


class Scatter:
    def __init__(self, pieces):
        self.own, *self.sides, top, low = pieces
        self.ahead, self.behind = forth(top), back(low)
        self.step = 0

    def wait(self, *others):
        self.ahead, self.behind = lax.optimization_barrier((self.ahead, self.behind) + others)[:2]

    def hop(self):
        m1, p1, m2, p2, m3, p3 = self.sides
        up, down = ((p3, m3), (p2, m2), (p1, m1))[self.step]
        ahead, behind = add_pair(up, self.ahead, down, self.behind)
        self.ahead, self.behind = forth(ahead), back(behind)
        self.step += 1

    def total(self):
        return (self.own.astype(F32) + self.ahead.astype(F32) + self.behind.astype(F32)).astype(BF)


def finish(core, own, other, rows, outputs, weights=(), gain=None, down=None):
    widths = [2 * 128 * len(lanes) for lanes, _, _ in outputs]

    def kernel(core, own, other, *refs):
        weights, refs = refs[: len(weights_given)], refs[len(weights_given) :]
        if gain is not None:
            gain_ref, refs = refs[0], refs[1:]
        outs = refs[: len(outputs)]
        for side, source in ((core[0], own), (1 - core[0], other)):
            for out, (lanes, core_step, block_step) in zip(outs, outputs):
                for index, lane in enumerate(lanes):
                    place = pl.multiple_of(side * core_step + index * block_step, 128)
                    out[:, pl.ds(place, 128)] = source[pl.ds(0, rows), pl.ds(lane, 128)].astype(F32)
            if down is not None:
                out = refs[len(outputs)]
                count, width = out.shape[0] // 2, out.shape[1]
                blocks = count * width // (rows * 128)
                tall = jnp.concatenate([source[:, pl.ds(down + j * 128, 128)] for j in range(blocks)], 0)
                start = pl.multiple_of(side * count, 16)
                for j in range(width // 128):
                    out[pl.ds(start, count), pl.ds(j * 128, 128)] = tall[j * count : (j + 1) * count].astype(F32)
        if gain is not None:
            total = jnp.zeros((rows, 1), F32)
            for weight, out in zip(weights, outs):
                total = total + jnp.sum(weight[...].astype(BF).astype(F32) * out[...], 1, keepdims=True)
            refs[-1][...] = jnp.broadcast_to(total / gain_ref[...].astype(BF).astype(F32), (rows, 128))

    weights_given = list(weights)
    args = [own, other] + weights_given + ([] if gain is None else [gain])
    out_shape = [jax.ShapeDtypeStruct((rows, width), F32) for width in widths]
    if down is not None:
        out_shape.append(jax.ShapeDtypeStruct(down_shape(rows, own.shape[1] - down), F32))
    if gain is not None:
        out_shape.append(jax.ShapeDtypeStruct((rows, 128), F32))
    return vmem_call(kernel, core, args, out_shape)


def down_shape(rows, folded):
    return 2 * folded // 8, 8 * rows


def per_device(
    decoder_input,
    memory,
    memory_lengths,
    distance_bucket,
    cotangent,
    self_gain,
    self_query,
    self_key,
    self_value,
    self_output,
    bucket_bias,
    cross_gain,
    cross_query,
    cross_key,
    cross_value,
    cross_output,
    feed_gain,
    gate_weight,
    up_weight,
    down_weight,
):
    shards = lax.axis_size("fsdp")
    rep = lax.axis_index("rep")
    side, core = rep // 2, rep % 2
    first = core == 0
    rows = decoder_input.shape[1]
    width = decoder_input.shape[2]
    slots = memory.shape[1]
    half = width // 2
    heads = half // HEAD
    shard_rows = self_query.shape[0]
    hidden_all = gate_weight.shape[1]
    hidden_rows = down_weight.shape[0]
    hidden_half = hidden_rows // 2

    which = core.reshape(1)
    cot_own = cotangent[0]
    cot_low = cot_own.astype(BF)
    cot_other = core_swap(cot_low)
    places = jnp.stack([rep, 2 * (1 - side) + core, 2 * side + 1 - core, 2 * (1 - side) + 1 - core])

    slot = (places[:, None] * slots + jnp.arange(slots, dtype=jnp.int32)[None]).reshape(-1)
    lane = jnp.arange(128, dtype=jnp.int32)[None]
    ones = jnp.where((lane >= 1) & (lane <= 3), 1.0, 0.0)
    extra_two = (jnp.where((lane == 0) & (slot >= memory_lengths[0])[:, None], NEG, 0.0) + ones).astype(BF)
    extra_one = jnp.broadcast_to(ones, (4 * rows, 128)).astype(BF)
    codes = jnp.arange(BUCKETS, dtype=jnp.int32)
    gaps = (jnp.stack([places[0], places[2]])[None, :] - places[:, None]).reshape(-1)
    starts = gaps * 256 + 768
    below = jnp.sum((distance_bucket[None, :] < codes[:, None]).astype(jnp.int32), 1)[None]
    upto = jnp.sum((distance_bucket[None, :] <= codes[:, None]).astype(jnp.int32), 1)[None]

    ringed = shards == 8 and shard_rows % 32 == 0 and hidden_half % 128 == 0
    wide = hidden_all // 2
    if ringed:
        ring = jnp.concatenate([ring_places(), which])
        gain_columns = [gain.reshape(shard_rows, 1) for gain in (self_gain, cross_gain, feed_gain)]
        which, ring, starts, below, upto, extra_two, gain_columns = lax.optimization_barrier(
            (which, ring, starts, below, upto, extra_two, gain_columns)
        )

        def packed(kernel, args, rows, columns):
            return vmem_call(kernel, which, args, [jax.ShapeDtypeStruct((rows, columns), BF)])[0]

        vectors = [v[None] for v in (self_gain, cross_gain, feed_gain, bucket_bias)]
        local = pack_halves(
            pack_small_kernel, which, [self_query, self_key, self_value], vectors, shard_rows + EXTRA, 60
        )
        state = gather_hops((local, local, [local]), 2)
    x_own, m_own = decoder_input[0], memory[0]
    x_far, m_far = far_swap(x_own), far_swap(m_own)
    if ringed:
        state = gather_hops(state, 1)
        x_far = held(x_far, *state[:2])
    x_core, x_diagonal = core_swap(x_own), core_swap(x_far)
    if ringed:
        state = gather_end(state)
        query_one, kv_one, extras = put_in_order(ring, state, (half, 2 * half), extra=EXTRA)
        local = pack_halves(
            pack_columns_kernel,
            which,
            [self_output, cross_output, cross_query, cross_key, cross_value],
            [],
            shard_rows,
            8,
        )
        local = held(local, *state[-2:])
        second = gather_hops((local, local, [local]), 1)
        feed = packed(pack_feed_kernel, [gate_weight, up_weight, down_weight], shard_rows, 3 * wide)
        gains, line = step(
            prepare_kernel, which, [extras, distance_bucket[None]], [((8, width), F32), ((8, 8 * rows), F32)], near=(0,)
        )
    else:

        def own_columns(weight):
            return lax.dynamic_slice_in_dim(weight, core * half, half, 1).astype(BF)

        def own_hidden(weight):
            parts = weight.reshape(shard_rows, shards, 2, hidden_half)
            own = lax.dynamic_index_in_dim(parts, core, 2, keepdims=False)
            return own.reshape(shard_rows, wide).astype(BF)

        def own_beside(left, right):
            return beside(own_columns(left), own_columns(right))

        query_one = gather_plain(own_columns(self_query))
        kv_one = gather_plain(own_beside(self_key, self_value))
        outs = [gather_plain(own_columns(w)) for w in (self_output, cross_output)]
        out_one, out_two = [jnp.where(first, w, jnp.concatenate([w[half:], w[:half]], 0)) for w in outs]
        query_two = gather_plain(own_columns(cross_query))
        kv_two = gather_plain(own_beside(cross_key, cross_value))
        gate_matrix = gather_plain(own_hidden(gate_weight))
        up_matrix = gather_plain(own_hidden(up_weight))
        down_half = lax.dynamic_slice_in_dim(down_weight, core * hidden_half, hidden_half, 0).astype(BF)
        down_matrix = gather_plain(down_half)
        gains = jnp.stack([gather_plain(g.astype(BF)).astype(F32) for g in (self_gain, cross_gain, feed_gain)])
        table = gather_plain(bucket_bias.astype(BF)).astype(F32)
        table = lax.dynamic_index_in_dim(table.reshape(2, heads, BUCKETS), core, 0, keepdims=False)
        hot = (distance_bucket[None, :] == codes[:, None]).astype(BF)
        line = jnp.einsum("hb,bd->hd", table.astype(BF), hot, preferred_element_type=F32)
        line = jnp.concatenate([jnp.full((heads, 4 * rows), NEG, F32), line], 1)
        line = jnp.pad(line, ((0, 8 - heads), (0, 0)))

    def owners(value):
        value = add(value, far_swap(value))
        return value, core_swap(value)

    pair = 2 * rows
    f32, b16 = (lambda *shape: (shape, F32)), (lambda *shape: (shape, BF))
    blocks = [x_own, x_far, x_core, x_diagonal]
    if ringed:
        blocks[0] = held(x_own, cot_other, extra_two, feed, *second[:2])
    q1, k1v1, n1_t = step(
        first_kernel,
        which,
        [*blocks, gains, query_one, kv_one],
        [b16(half, pair), b16(4 * rows, 2 * half), b16(width, 4 * rows)],
        near=(5, 6),
        scratch=[pltpu.VMEM((4 * rows, width), BF)],
    )
    if ringed:
        second = gather_hops(second, 1)
        q1 = held(q1, *second[:2])
        second = held_hops(second, q1, 1)
    o1, logs_one = attend(q1, k1v1, None, line, starts)
    if ringed:
        o1 = held(o1, *second[:2])
        second = gather_end(held_hops(second, o1, 0))
        m_far = held(m_far, o1)
    o1_other = core_swap(o1)
    m_core, m_diagonal = core_swap(m_own), core_swap(m_far)
    if ringed:
        out_one, out_two, query_two, kv_two = put_in_order(ring, second, (half, half, half, 2 * half), turned=(0, 1))
        feed = held(feed, *second[-2:])
        feed = gather_hops((feed, feed, [feed]), 1)
    columns, low = step(mix_kernel, which, [o1, o1_other, out_one], [f32(pair, half), b16(pair, half)], near=(0, 2))
    middle, n2, n2_t, q2 = step(
        functools.partial(norm_kernel, 2, 1, 1),
        which,
        [x_own, x_core, columns, core_swap(low), gains, query_two],
        [f32(pair, width), b16(pair, width), b16(width, pair), b16(half, pair)],
        near=(2, 5),
    )
    out_one_other, out_two_other = core_swap(out_one), core_swap(out_two)
    if ringed:
        q2 = held(q2, *feed[:2])
        feed = held_hops(feed, q2, 1)
        m_own = held(m_own, q2, out_one_other, out_two_other)
    k2v2 = project_blocks([m_own, m_far, m_core, m_diagonal], kv_two)
    if ringed:
        q2 = held(q2, *feed[:2])
        feed = held_hops(feed, k2v2, 1)
    o2, logs_two = attend(q2, k2v2, extra_two)
    if ringed:
        o2 = held(o2, *feed[:2])
        feed = gather_end(held_hops(feed, o2, 0))
        m_own = held(m_own, o2)
    m_all = jnp.concatenate([m_own, m_far, m_core, m_diagonal], 0)
    o2_other = core_swap(o2)
    columns, low = step(mix_kernel, which, [o2, o2_other, out_two], [f32(pair, half), b16(pair, half)], near=(0,))
    after, n3, n3_t = step(
        functools.partial(norm_kernel, 1, 0, 2),
        which,
        [middle, columns, core_swap(low), gains],
        [f32(pair, width), b16(pair, width), b16(width, pair)],
        near=(1,),
    )
    if ringed:
        feed[-2:] = [held(part, m_all) for part in feed[-2:]]
        gate_matrix, up_matrix, down_matrix = put_in_order(ring, feed, (wide, wide, wide), fold=width)

    part_low, d_gate_up_w, d_down_w, d_n3, d_low = step(
        feed_kernel,
        which,
        [n3, n3_t, gate_matrix, up_matrix, down_matrix, cot_low, cot_other],
        [b16(pair, width), b16(width, 2 * wide), b16(wide, width), f32(pair, width), b16(pair, width)],
        10,
        near=(0, 1, 2, 3, 4),
    )
    d_after, d_o2, d_out_two = step(
        functools.partial(back_kernel, 2, 2),
        which,
        [d_n3, core_swap(d_low), after, gains, cot_own, cot_other, out_two, out_two_other, o2, o2_other],
        [f32(pair, width), b16(half, pair), b16(width, half)],
    )

    back_two = functools.partial(attend_back, q2, k2v2, extra_two, o2)
    if ringed:
        feed_ring = Scatter(cut_apart(ring, [d_gate_up_w, fold_down(d_down_w, shards, wide)], None))
        d_o2 = held(d_o2, feed_ring.ahead, feed_ring.behind)
        feed_ring.hop()
    d_q2_a, d_kv2 = back_two(d_o2, logs_two, base=0, pairs=1)
    d_o2_b = held(d_o2, d_q2_a)
    if ringed:
        d_o2_b = held(d_o2_b, feed_ring.ahead, feed_ring.behind)
        feed_ring.wait(d_q2_a)
        feed_ring.hop()
    d_q2_b, d_kv2 = back_two(d_o2_b, logs_two, base=1, pairs=1, earlier=d_kv2)
    d_q2_c, d_kv2 = back_two(held(d_o2, d_q2_b), logs_two, base=2, pairs=heads // 2 - 2, earlier=d_kv2)
    d_q2 = jnp.concatenate([d_q2_a, d_q2_b, d_q2_c], 0)
    d_kv2_held = d_kv2
    if ringed:
        d_kv2_held = held(d_kv2, feed_ring.ahead, feed_ring.behind)
        feed_ring.wait(d_q2_c)
        feed_ring.hop()
    part, low, d_query_two = step(
        query_kernel, which, [d_q2, query_two, n2_t], [f32(pair, width), b16(pair, width), b16(width, half)]
    )
    low = core_swap(low)
    d_middle, d_o1, d_out_one = step(
        functools.partial(back_kernel, 1, 1),
        which,
        [part, low, middle, gains, d_after, out_one, out_one_other, o1, o1_other],
        [f32(pair, width), b16(half, pair), b16(width, half)],
    )
    d_kv_two = dot(m_all, d_kv2_held, TN).astype(BF)
    d_mem_core = core_swap(dot(d_kv2[2 * slots :], kv_two, NT).astype(BF))
    d_memory = dot(d_kv2[: 2 * slots], kv_two, NT)
    d_memory_far = (d_memory[slots:] + d_mem_core[slots:].astype(F32)).astype(BF)
    d_memory = d_memory[:slots] + d_mem_core[:slots].astype(F32)
    d_memory_far_sum = far_swap(d_memory_far)

    cross_parts = [d_query_two, d_kv_two, d_out_two, d_out_one]
    if ringed:
        cross_ring = Scatter(cut_apart(ring, cross_parts, None, (2, 3)))
        feed_ring.wait(d_memory_far)
        feed_own, feed_other = owners(feed_ring.total())
        d_o1 = held(d_o1, d_memory_far, cross_ring.ahead, cross_ring.behind)
        cross_ring.hop()
    back_one = functools.partial(attend_back, q1, k1v1, extra_one, o1)
    d_q1_a, d_kv1, d_far_a = back_one(d_o1, logs_one, line, starts, base=0, pairs=heads // 2 - 1)
    d_o1_c = held(d_o1, d_q1_a)
    if ringed:
        d_o1_c = held(d_o1_c, cross_ring.ahead, cross_ring.behind)
        cross_ring.wait(d_q1_a)
        cross_ring.hop()
    d_q1_c, d_kv1, d_far_c = back_one(d_o1_c, logs_one, line, starts, base=heads // 2 - 1, pairs=1, earlier=d_kv1)
    if ringed:
        d_q1_c, d_kv1, d_far_c = lax.optimization_barrier((d_q1_c, d_kv1, d_far_c, cross_ring.ahead, cross_ring.behind))[:3]
    d_q1 = jnp.concatenate([d_q1_a, d_q1_c], 0)
    if ringed:
        (table_rows,) = step(
            table_kernel, (which, starts), [below, upto, d_far_a, d_far_c], [b16(8 * EXTRA, 3 * half)]
        )
        d_kv1 = held(d_kv1, table_rows, d_memory_far_sum)
        d_query_one, d_kv_one = step(
            first_weights_kernel, which, [d_q1, d_kv1, n1_t], [b16(width, half), b16(width, 2 * half)]
        )
        self_ring = Scatter(cut_apart(ring, [d_query_one, d_kv_one], table_rows))
        d_q1 = held(d_q1, self_ring.own)
        cross_ring.wait(self_ring.own)
        cross_ring.hop()
    after_own, output_other = after[:rows], core_swap(part_low[rows:])
    if ringed:
        after_own, d_memory = held(after_own, self_ring.own), held(d_memory, self_ring.own)
    output = after_own + part_low[:rows].astype(F32) + output_other.astype(F32)
    d_memory = d_memory + d_memory_far_sum.astype(F32)
    near, low = step(
        first_back_kernel, which, [d_q1, d_kv1, query_one, kv_one], [f32(pair, width), b16(pair, width)]
    )
    low = core_swap(low)
    if ringed:
        low = held(low, self_ring.ahead, self_ring.behind)
    d_n1, d_n1_far = step(first_sum_kernel, which, [near, low], [f32(rows, width), b16(rows, width)])
    d_n1_other = far_swap(d_n1_far)
    (d_input,) = step(
        input_kernel, which, [x_own, gains, d_n1, d_n1_other, d_middle[:rows]], [f32(rows, width)]
    )

    blocks = half // 128
    plain = lambda start: ([start + 128 * i for i in range(blocks)], half, 128)
    turns = lambda start: [([start + 256 * i + 128 * t for i in range(blocks)], half, 128) for t in range(2)]
    if ringed:
        self_ring.wait(d_n1_far)
        self_ring.hop()
        self_ring.hop()
        hidden = lambda start: ([start + 128 * i for i in range(wide // 128)], 128, 256)
        d_gate_out, d_up_out, d_down_out, d_gain_three = finish(
            which, feed_own, feed_other, shard_rows, [hidden(0), hidden(wide)], (gate_weight, up_weight), gain_columns[2], 2 * wide
        )
        cross_sum = cross_ring.total()
        cross_own, cross_other = owners(cross_sum)
        self_ring.wait(d_down_out, cross_sum)
        self_ring.hop()
        self_ring.wait(d_n1_other)
        d_cross = finish(
            which,
            cross_own,
            cross_other,
            shard_rows,
            [plain(0), *turns(half), plain(3 * half), plain(4 * half)],
            (cross_query,),
            gain_columns[1],
        )
        self_own, self_other = owners(self_ring.total())
        d_self = finish(
            which,
            self_own,
            self_other,
            shard_rows,
            [plain(0), *turns(half)],
            (self_query, self_key, self_value),
            gain_columns[0],
        )
        table_own, table_other = [v[shard_rows, : shard_rows // 2].astype(F32) for v in (self_own, self_other)]
        d_gains = [d_self[3][:, 0], d_cross[5][:, 0], d_gain_three[:, 0]]
        d_output_one_out = d_cross[4]
    else:
        d_query_one, d_kv_one = step(
            first_weights_kernel, which, [d_q1, d_kv1, n1_t], [b16(width, half), b16(width, 2 * half)]
        )

        def whole(both, axis=1):
            own, other = both
            return jnp.concatenate([jnp.where(first, own, other), jnp.where(first, other, own)], axis).astype(F32)

        def plain_owners(value):
            return owners(scatter_plain(value))

        def kv_whole(both):
            pick = lambda v, turn: v.reshape(shard_rows, -1, 2, 128)[:, :, turn].reshape(shard_rows, half)
            return [whole([pick(v, turn) for v in both]) for turn in range(2)]

        def hidden_whole(both):
            both = [v.reshape(shard_rows, shards, 1, hidden_half) for v in both]
            return whole(both, 2).reshape(shard_rows, hidden_all)

        def in_order(value):
            return jnp.where(first, value, jnp.concatenate([value[half:], value[:half]], 0))

        far = (gaps[:, None] * 256 + jnp.arange(512, dtype=jnp.int32)[None] - 255).reshape(-1)
        inside = ((far[None] >= below[0][:, None]) & (far[None] < upto[0][:, None])).astype(F32)
        d_far = jnp.concatenate([d_far_a, d_far_c], 0).reshape(heads, -1)
        d_table = jnp.einsum("hd,bd->hb", d_far, inside, precision=lax.Precision.HIGHEST).reshape(1, -1)
        d_table = jnp.concatenate([jnp.where(first, d_table, 0.0), jnp.where(first, 0.0, d_table)], 1)
        d_table = d_table.reshape(shards, shard_rows // 2).astype(BF)

        def gain_grad(gain, *pairs):
            total = sum(jnp.sum(w.astype(BF).astype(F32) * g, 1) for w, g in pairs)
            return total / gain.astype(BF).astype(F32)

        d_gate_out, d_up_out = [hidden_whole(plain_owners(v)) for v in (d_gate_up_w[:, :wide], d_gate_up_w[:, wide:])]
        d_down_out = whole(plain_owners(d_down_w), 0)
        d_cross = [whole(plain_owners(d_query_two)), *kv_whole(plain_owners(d_kv_two))]
        d_cross.append(whole(plain_owners(in_order(d_out_two))))
        d_output_one_out = whole(plain_owners(in_order(d_out_one)))
        d_self = [whole(plain_owners(d_query_one)), *kv_whole(plain_owners(d_kv_one))]
        table_own, table_other = [v[0].astype(F32) for v in plain_owners(d_table)]
        d_gains = [
            gain_grad(self_gain, (self_query, d_self[0]), (self_key, d_self[1]), (self_value, d_self[2])),
            gain_grad(cross_gain, (cross_query, d_cross[0])),
            gain_grad(feed_gain, (gate_weight, d_gate_out), (up_weight, d_up_out)),
        ]
    d_bucket = table_own + table_other

    return (
        output[None],
        d_input[None],
        d_memory[None],
        d_gains[0],
        d_self[0],
        d_self[1],
        d_self[2],
        d_output_one_out,
        d_bucket,
        d_gains[1],
        d_cross[0],
        d_cross[1],
        d_cross[2],
        d_cross[3],
        d_gains[2],
        d_gate_out,
        d_up_out,
        d_down_out,
    )


def solution(mesh):
    split = P("fsdp", "rep", None)
    vector, matrix = P("fsdp"), P("fsdp", None)
    weights = (
        (vector,)
        + (matrix,) * 4
        + (vector, vector)
        + (matrix,) * 4
        + (vector,)
        + (matrix,) * 3
    )
    return jax.shard_map(
        per_device,
        mesh=mesh,
        in_specs=(split, split, vector, P(), split) + weights,
        out_specs=(split, split, split) + weights,
        check_vma=False,
    )
```

```python
import functools

import jax
import jax.numpy as jnp
from jax import lax
from jax.experimental import pallas as pl
from jax.experimental.pallas import tpu as pltpu
from jax.sharding import PartitionSpec as P

HEAD = 64
BUCKETS = 32
EXTRA = 16
EPS = 1e-06
NEG = -1e30
BF = jnp.bfloat16
F32 = jnp.float32
NN = (((1,), (0,)), ((), ()))
NT = (((1,), (1,)), ((), ()))
TN = (((0,), (0,)), ((), ()))
TT = (((0,), (1,)), ((), ()))

CORE = [(0, 1), (1, 0), (2, 3), (3, 2)]
FAR = [(0, 2), (2, 0), (1, 3), (3, 1)]


def core_swap(value):
    return lax.ppermute(value, "rep", CORE)


def far_swap(value):
    return lax.ppermute(value, "rep", FAR)


def dot(left, right, dims=NN):
    return lax.dot_general(left, right, dims, preferred_element_type=F32)


def half_rows(pair, head):
    row = lax.broadcasted_iota(jnp.int32, pair.shape, 0)
    keep = (row < HEAD) if head == 0 else (row >= HEAD)
    return jnp.where(keep, pair, jnp.zeros_like(pair))


def three_terms(value):
    first = value.astype(BF)
    rest = value - first.astype(F32)
    second = rest.astype(BF)
    third = (rest - second.astype(F32)).astype(BF)
    return first, second, third


def extra_rows(first_row, vector):
    terms = three_terms(-vector)
    row = lax.broadcasted_iota(jnp.int32, (128, vector.shape[1]), 0)
    out = jnp.where(row == 0, first_row, 0.0)
    for place, term in enumerate(terms):
        out = jnp.where(row == place + 1, term.astype(F32), out)
    return out.astype(BF)


def spread(line, starts, head, part, blocks, lanes):
    block = 256
    rows = []
    for j in range(blocks):
        tiles = []
        for i in range(lanes):
            start = pl.multiple_of(starts[(part * blocks + j) * lanes + i], 128)
            row = line[pl.ds(head, 1), pl.ds(start, 2 * block)]
            tile = pltpu.roll(jnp.broadcast_to(row, (block, 2 * block)), 0, 1, stride=1, stride_axis=0)
            tiles.append(tile[:, block:])
        rows.append(jnp.concatenate(tiles, 1))
    return jnp.concatenate(rows, 0)


def attend_kernel(chunk, biased, base, *refs):
    if biased:
        starts, query, keyvalue, line, mixed, log_total = refs
    else:
        query, keyvalue, extra, mixed, log_total = refs
    keys, rows = keyvalue.shape[0], query.shape[1]
    key, value = keyvalue.at[:, pl.ds(0, 128)], keyvalue.at[:, pl.ds(128, 128)]
    pair = query[...]
    row = lax.broadcasted_iota(jnp.int32, (128, rows), 0)
    one = jnp.where(row == 0, 1.0, 0.0).astype(BF)
    wide = [half_rows(pair, h) for h in range(2)]
    if not biased:
        wide = [jnp.concatenate([w, one], 0) for w in wide]

    def score(part, head):
        span = pl.ds(part * chunk, chunk)
        if not biased:
            return dot(jnp.concatenate([key[span, :], extra[span, :]], 1), wide[head])
        full = 2 * (base + pl.program_id(0)) + head
        return dot(key[span, :], wide[head]) + spread(line, starts, full, part, chunk // 256, rows // 256)

    highest = [jnp.full((1, rows), NEG, F32)] * 2
    total = [jnp.zeros((1, rows), F32)] * 2
    acc = [jnp.zeros((HEAD, rows), F32)] * 2
    steps = [(part, head) for part in range(keys // chunk) for head in range(2)]
    ahead = score(*steps[0])
    for index, (part, head) in enumerate(steps):
        scores = ahead
        if index + 1 < len(steps):
            ahead = score(*steps[index + 1])
        span = pl.ds(part * chunk, chunk)
        top = jnp.maximum(highest[head], jnp.max(scores, 0, keepdims=True))
        soft = jnp.exp(scores - top)
        scale = jnp.exp(highest[head] - top)
        total[head] = total[head] * scale + jnp.sum(soft, 0, keepdims=True)
        product = dot(value[span, :], soft.astype(BF), TN)[head * HEAD : (head + 1) * HEAD]
        acc[head] = acc[head] * scale + product
        highest[head] = top
    for head in range(2):
        mixed[pl.ds(head * HEAD, HEAD), :] = (acc[head] / total[head]).astype(BF)
        log_total[0, pl.ds(head, 1), :] = highest[head] + jnp.log(total[head])


def attend(query, keyvalue, extra, line=None, starts=None, chunk=512, base=0, pairs=None, modelled=0.3):
    rows, keys = query.shape[1], keyvalue.shape[0]
    pairs = query.shape[0] // 128 if pairs is None else pairs
    width = pairs * 128
    biased = line is not None
    in_specs = [pl.BlockSpec((128, rows), lambda p, *s: (p + base, 0)), pl.BlockSpec((keys, 256), lambda p, *s: (0, p + base))]
    out_specs = [pl.BlockSpec((128, rows), lambda p, *s: (p, 0)), pl.BlockSpec((1, 8, rows), lambda p, *s: (p, 0, 0))]
    out_shape = [jax.ShapeDtypeStruct((width, rows), BF), jax.ShapeDtypeStruct((pairs, 8, rows), F32)]
    args = [query, keyvalue]
    if biased:
        args = [starts] + args + [line]
        in_specs.append(pl.BlockSpec(line.shape, lambda p, *s: (0, 0)))
    else:
        args.append(extra)
        in_specs.append(pl.BlockSpec((keys, 128), lambda p, *s: (0, 0)))
    return pl.pallas_call(
        functools.partial(attend_kernel, chunk, biased, base),
        grid_spec=pltpu.PrefetchScalarGridSpec(
            num_scalar_prefetch=int(biased), grid=(pairs,), in_specs=in_specs, out_specs=out_specs
        ),
        out_shape=out_shape,
        compiler_params=pltpu.CompilerParams(vmem_limit_bytes=12 * 2**20),
        cost_estimate=pl.CostEstimate(flops=1, bytes_accessed=int(3.7e6 * modelled), transcendentals=0),
    )(*args)


def attend_back_kernel(chunk, biased, chained, base, *refs):
    if biased:
        starts, query, keyvalue, extra, mixed, grad, log_total, line = refs[:8]
        d_query, d_keyvalue, d_far = refs[8 + chained :]
    else:
        query, keyvalue, extra, mixed, grad, log_total = refs[:6]
        d_query, d_keyvalue = refs[6 + chained :]
    keys, rows = keyvalue.shape[0], query.shape[1]
    key, value = keyvalue.at[:, pl.ds(0, 128)], keyvalue.at[:, pl.ds(128, 128)]
    pair, grad_pair = query[...], grad[...]
    product = mixed[...].astype(F32) * grad_pair.astype(F32)
    q_half = [half_rows(pair, h) for h in range(2)]
    g_half = [half_rows(grad_pair, h) for h in range(2)]
    q_wide, g_wide = [], []
    for head in range(2):
        inner = jnp.sum(product[head * HEAD : (head + 1) * HEAD], 0, keepdims=True)
        logs = log_total[0, pl.ds(head, 1), :]
        q_wide.append(jnp.concatenate([q_half[head], extra_rows(1.0, logs)], 0))
        g_wide.append(jnp.concatenate([g_half[head], extra_rows(0.0, inner)], 0))
    if biased:
        block = 256
        down = lax.broadcasted_iota(jnp.int32, (block, block), 0)
        over = lax.broadcasted_iota(jnp.int32, (block, block), 1)
        flip = jnp.where(down + over == block - 1, 1.0, 0.0).astype(BF)
    acc = [jnp.zeros((HEAD, rows), F32) for _ in range(2)]
    for part in range(keys // chunk):
        span = pl.ds(part * chunk, chunk)
        key_wide = jnp.concatenate([key[span, :], extra[span, :]], 1)
        value_wide = jnp.concatenate([value[span, :], extra[span, :]], 1)
        dv, dk = 0.0, 0.0
        for head in range(2):
            scores = dot(key_wide, q_wide[head])
            if biased:
                full = 2 * (base + pl.program_id(0)) + head
                scores = scores + spread(line, starts, full, part, chunk // 256, rows // 256)
            soft = jnp.exp(scores)
            d_scores = (soft * dot(value_wide, g_wide[head])).astype(BF)
            dv = dv + dot(soft.astype(BF), g_half[head], NT)
            dk = dk + dot(d_scores, q_half[head], NT)
            step = dot(key[span, :], d_scores, TN)[head * HEAD : (head + 1) * HEAD]
            acc[head] = acc[head] + step
            if biased:
                for j in range(chunk // block):
                    for i in range(rows // block):
                        tile = d_scores[j * block : (j + 1) * block, i * block : (i + 1) * block]
                        tile = jnp.concatenate([dot(flip, tile), jnp.zeros((block, block), F32)], 1)
                        tile = pltpu.roll(tile, 0, 1, stride=1, stride_axis=0)
                        place = (part * (chunk // block) + j) * (rows // block) + i
                        d_far[0, head, pl.ds(place, 1), :] = jnp.sum(tile, 0, keepdims=True)
        d_keyvalue[span, :] = jnp.concatenate([dk.astype(BF), dv.astype(BF)], 1)
    for head in range(2):
        d_query[pl.ds(head * HEAD, HEAD), :] = acc[head].astype(BF)


def attend_back(
    query, keyvalue, extra, mixed, grad, log_total, line=None, starts=None, chunk=512, base=0, pairs=None, earlier=None, modelled=0.3
):
    rows, keys = query.shape[1], keyvalue.shape[0]
    pairs = query.shape[0] // 128 if pairs is None else pairs
    width = pairs * 128
    biased = line is not None
    across = pl.BlockSpec((128, rows), lambda p, *s: (p + base, 0))
    along = pl.BlockSpec((keys, 256), lambda p, *s: (0, p + base))
    in_specs = [
        across,
        along,
        pl.BlockSpec((keys, 128), lambda p, *s: (0, 0)),
        across,
        across,
        pl.BlockSpec((1, 8, rows), lambda p, *s: (p + base, 0, 0)),
    ]
    args = [query, keyvalue, extra, mixed, grad, log_total]
    out_specs = [pl.BlockSpec((128, rows), lambda p, *s: (p, 0)), along]
    out_shape = [jax.ShapeDtypeStruct((width, rows), BF), jax.ShapeDtypeStruct(keyvalue.shape, BF)]
    if biased:
        in_specs.append(pl.BlockSpec(line.shape, lambda p, *s: (0, 0)))
        args = [starts] + args + [line]
        blocks = (keys // 256) * (rows // 256)
        out_specs.append(pl.BlockSpec((1, 2, blocks, 512), lambda p, *s: (p, 0, 0, 0)))
        out_shape.append(jax.ShapeDtypeStruct((pairs, 2, blocks, 512), F32))
    aliases = {}
    if earlier is not None:
        aliases = {len(args): 1}
        in_specs.append(pl.BlockSpec(memory_space=pl.ANY))
        args.append(earlier)
    return pl.pallas_call(
        functools.partial(attend_back_kernel, chunk, biased, int(earlier is not None), base),
        grid_spec=pltpu.PrefetchScalarGridSpec(
            num_scalar_prefetch=int(biased), grid=(pairs,), in_specs=in_specs, out_specs=out_specs
        ),
        out_shape=out_shape,
        input_output_aliases=aliases,
        compiler_params=pltpu.CompilerParams(vmem_limit_bytes=10 * 2**20),
        cost_estimate=pl.CostEstimate(flops=1, bytes_accessed=int(3.7e6 * modelled), transcendentals=0),
    )(*args)


def project_blocks(blocks, weight):
    def kernel(*refs):
        weight, out = refs[-2:]
        row = 0
        for block in refs[:-2]:
            for part in range(block.shape[0] // blocks[0].shape[0]):
                count = blocks[0].shape[0]
                out[pl.ds(row, count), :] = dot(block[pl.ds(part * count, count), :], weight[...]).astype(BF)
                row += count

    rows = sum(block.shape[0] for block in blocks)
    return pl.pallas_call(
        kernel,
        in_specs=[pl.BlockSpec(block.shape, lambda: (0, 0)) for block in blocks] + [pl.BlockSpec(memory_space=pltpu.VMEM)],
        out_specs=pl.BlockSpec(memory_space=pltpu.VMEM),
        out_shape=jax.ShapeDtypeStruct((rows, weight.shape[1]), BF),
        compiler_params=pltpu.CompilerParams(vmem_limit_bytes=12 * 2**20),
        cost_estimate=pl.CostEstimate(flops=1, bytes_accessed=1, transcendentals=0),
    )(*blocks, weight)


def beside(left, right):
    rows, half = left.shape
    return jnp.stack([left.reshape(rows, -1, 128), right.reshape(rows, -1, 128)], 2).reshape(rows, 2 * half)


VMEM = pl.BlockSpec(memory_space=pltpu.VMEM)


def whole_block(shape):
    return pl.BlockSpec(shape, lambda *i: (0,) * len(shape), pipeline_mode=pl.Buffered(1))


def step(kernel, core, args, shapes, mib=10, near=(), scratch=()):
    scalars = core if isinstance(core, tuple) else (core,)
    return pl.pallas_call(
        kernel,
        grid_spec=pltpu.PrefetchScalarGridSpec(
            num_scalar_prefetch=len(scalars),
            grid=(1,),
            in_specs=[VMEM if i in near else whole_block(arg.shape) for i, arg in enumerate(args)],
            out_specs=[VMEM] * len(shapes),
            scratch_shapes=list(scratch),
        ),
        out_shape=[jax.ShapeDtypeStruct(shape, kind) for shape, kind in shapes],
        compiler_params=pltpu.CompilerParams(vmem_limit_bytes=mib * 2**20),
        cost_estimate=pl.CostEstimate(flops=1, bytes_accessed=1, transcendentals=0),
    )(*scalars, *args)


def inverse_rms(value):
    return lax.rsqrt(jnp.mean(value * value, -1, keepdims=True) + EPS)


def norm_back(value, inverse, gain, grad):
    scaled = grad * gain
    return inverse * (scaled - value * (inverse * inverse) * jnp.mean(scaled * value, -1, keepdims=True))


def rows_turned(ref):
    half = ref.shape[0] // 2
    return jnp.concatenate([ref[pl.ds(half, half), :], ref[pl.ds(0, half), :]], 0)


def lanes_turned(ref):
    half = ref.shape[1] // 2
    return jnp.concatenate([ref[:, pl.ds(half, half)], ref[:, pl.ds(0, half)]], 1)


def halves(core, half):
    return pl.ds(pl.multiple_of(core[0] * half, 128), half), pl.ds(pl.multiple_of((1 - core[0]) * half, 128), half)


def first_kernel(core, own, far, near, diagonal, gain, w_query, w_keyvalue, query, keyvalue, normed_t, normed):
    rows = own.shape[0]
    for place, block in enumerate((own, far, near, diagonal)):
        value = block[...].astype(F32)
        value = value * inverse_rms(value) * gain[pl.ds(0, 1), :]
        normed[pl.ds(place * rows, rows), :] = value.astype(BF)
        normed_t[:, pl.ds(place * rows, rows)] = value.T.astype(BF)
    keyvalue[...] = dot(normed[...], w_keyvalue[...]).astype(BF)
    mine = jnp.concatenate([normed[pl.ds(0, rows), :], normed[pl.ds(2 * rows, rows), :]], 0)
    query[...] = dot(mine, w_query[...]).T.astype(BF)


def prepare_kernel(core, extras, buckets, gains, line):
    count = gains.shape[1] // 8
    lines = extras[...].astype(F32).T
    gains[...] = lines[:8]
    table = jnp.concatenate([lines[3:4, f * count : f * count + count // 2] for f in range(8)], 1)
    entries = table.shape[1]
    heads = entries // BUCKETS // 2
    head = lax.broadcasted_iota(jnp.int32, (8, entries), 0)
    entry = lax.broadcasted_iota(jnp.int32, (8, entries), 1)
    first = (core[0] * heads + head) * BUCKETS
    mine = (entry >= first) & (entry < first + BUCKETS) & (head < heads)
    rows = jnp.where(mine, jnp.broadcast_to(table, (8, entries)), 0.0).astype(BF)
    length = buckets.shape[1]
    code = lax.broadcasted_iota(jnp.int32, (entries, length), 0) & (BUCKETS - 1)
    hot = jnp.where(code == buckets[...], 1.0, 0.0).astype(BF)
    line[:, pl.ds(0, length)] = jnp.full((8, length), NEG, F32)
    line[:, pl.ds(length, length)] = dot(rows, hot)


def table_kernel(core, starts, below, upto, *refs):
    parts, out = refs[:-1], refs[-1]
    heads = sum(2 * far.shape[0] for far in parts)
    total = jnp.zeros((8, BUCKETS), F32)
    for block in range(8):
        rows = [far[p, h, pl.ds(block, 1), :] for far in parts for p in range(far.shape[0]) for h in range(2)]
        rows = jnp.concatenate(rows + [jnp.zeros((8 - heads, 512), F32)], 0)
        distance = lax.broadcasted_iota(jnp.int32, (512, BUCKETS), 0) + (starts[block] - 1023)
        hot = jnp.where((distance >= below[...]) & (distance < upto[...]), 1.0, 0.0).astype(BF)
        for term in three_terms(rows):
            total = total + dot(term, hot)
    entries = 2 * heads * BUCKETS
    spot = lax.broadcasted_iota(jnp.int32, (BUCKETS, entries), 1) - lax.broadcasted_iota(jnp.int32, (BUCKETS, entries), 0)
    line = jnp.zeros((1, entries), F32)
    for head in range(heads):
        pick = jnp.where(spot == (core[0] * heads + head) * BUCKETS, 1.0, 0.0).astype(BF)
        line = line + dot(total[head : head + 1].astype(BF), pick)
    out[...] = jnp.zeros(out.shape, BF)
    count = entries // 8
    for f in range(8):
        out[pl.ds(f * EXTRA, 1), pl.ds(0, count)] = line[:, f * count : (f + 1) * count].astype(BF)


def mix_kernel(core, mixed, weight, w_theirs, part, low_own, low_other):
    half = mixed.shape[0]
    mine, theirs = halves(core, half)
    part[:, mine] = dot(mixed[...], weight[pl.ds(0, half), :], TN)
    part[:, theirs] = dot(mixed[...], w_theirs[pl.ds(half, half), :], TN)
    rows = low_own.shape[0]
    low_own[...] = part[pl.ds(0, rows), :].astype(BF)
    low_other[...] = part[pl.ds(rows, rows), :].astype(BF)


def stacked(refs):
    blocks = [ref[...].astype(F32) for ref in refs]
    return blocks[0] if len(blocks) == 1 else jnp.concatenate(blocks, 0)


def norm_kernel(parts, projected, which, core, *refs):
    base, (part, own, other, gain) = refs[:parts], refs[parts : parts + 4]
    value, normed, normed_t = refs[parts + 4 + projected : parts + 7 + projected]
    whole = stacked(base) + part[...] + stacked((own, other))
    value[...] = whole
    whole = whole * inverse_rms(whole) * gain[pl.ds(which, 1), :]
    normed[...] = whole.astype(BF)
    normed_t[...] = whole.T.astype(BF)
    if projected:
        refs[-1][...] = dot(normed[...], refs[parts + 4][...]).T.astype(BF)


def feed_kernel(core, normed, normed_t, gate, up, down, cot_own, cot_other, part, grads, d_down, d_normed, d_low):
    wide = gate.shape[1]
    scale, cubic = 0.7978845608028654, 0.044715
    grad_out = jnp.concatenate([cot_own[...], cot_other[...]], 0)
    total, back_total = 0.0, 0.0
    for start in range(0, wide, 256):
        span = pl.ds(start, 256)
        g = dot(normed[...], gate[:, span])
        u = dot(normed[...], up[:, span])
        square = g * g
        t = jnp.tanh(scale * (g + cubic * square * g))
        act = 0.5 * g * (1.0 + t)
        slope = 0.5 * (1.0 + t) + 0.5 * g * (1.0 - t * t) * (scale * (1.0 + 3.0 * cubic * square))
        hidden = (act * u).astype(BF)
        d_hidden = dot(grad_out, down[span, :], NT)
        d_gate = (d_hidden * u * slope).astype(BF)
        d_up = (d_hidden * act).astype(BF)
        total = total + dot(hidden, down[span, :])
        back_total = back_total + dot(d_gate, gate[:, span], NT) + dot(d_up, up[:, span], NT)
        grads[:, span] = dot(normed_t[...], d_gate).astype(BF)
        grads[:, pl.ds(wide + start, 256)] = dot(normed_t[...], d_up).astype(BF)
        d_down[span, :] = dot(hidden, grad_out, TN).astype(BF)
    part[...] = total.astype(BF)
    d_normed[...] = back_total
    d_low[...] = back_total.astype(BF)


def back_kernel(parts, which, core, *refs):
    part, other, value, gain = refs[:4]
    base = refs[4 : 4 + parts]
    weight, w_theirs, mixed, mixed_other = refs[4 + parts : 8 + parts]
    d_value, d_mixed, d_weight = refs[8 + parts :]
    half = weight.shape[1]
    grad = part[...] + rows_turned(other).astype(F32)
    whole = value[...]
    d_value[...] = stacked(base) + norm_back(whole, inverse_rms(whole), gain[pl.ds(which, 1), :], grad)
    mine, theirs = halves(core, half)
    d_mine, d_theirs = d_value[:, mine].astype(BF), d_value[:, theirs].astype(BF)
    d_mixed[...] = (dot(weight[pl.ds(0, half), :], d_mine, NT) + dot(w_theirs[pl.ds(half, half), :], d_theirs, NT)).astype(BF)
    d_weight[pl.ds(0, half), :] = dot(mixed[...], d_mine).astype(BF)
    d_weight[pl.ds(half, half), :] = dot(lanes_turned(mixed_other), d_mine).astype(BF)


def query_kernel(core, d_query, weight, normed_t, part, low, d_weight):
    grad = d_query[...].astype(F32).T.astype(BF)
    total = dot(grad, weight[...], NT)
    part[...] = total
    low[...] = total.astype(BF)
    d_weight[...] = dot(normed_t[...], d_query[...], NT).astype(BF)


def memory_core_kernel(core, d_keyvalue, weight, out):
    rows = out.shape[0]
    out[...] = dot(d_keyvalue[pl.ds(rows, rows), :], weight[...], NT).astype(BF)


def memory_weight_kernel(core, memory_t, d_keyvalue, out):
    out[...] = dot(memory_t[...], d_keyvalue[...]).astype(BF)


def memory_near_kernel(core, d_keyvalue, weight, other, own, far):
    rows = own.shape[0]
    own[...] = dot(d_keyvalue[pl.ds(0, rows), :], weight[...], NT) + other[pl.ds(0, rows), :].astype(F32)
    total = dot(d_keyvalue[pl.ds(rows, rows), :], weight[...], NT) + other[pl.ds(rows, rows), :].astype(F32)
    far[...] = total.astype(BF)


def turn_kernel(core, *refs):
    blocks, out = refs[:-1], refs[-1]
    for place, block in enumerate(blocks):
        rows = block.shape[0]
        out[:, pl.ds(place * rows, rows)] = block[...].astype(F32).T.astype(BF)


def first_weights_kernel(core, d_query, d_keyvalue, normed_t, d_w_query, d_w_keyvalue):
    rows = d_query.shape[1] // 2
    d_w_query[...] = (
        dot(normed_t[:, pl.ds(0, rows)], d_query[:, pl.ds(0, rows)], NT)
        + dot(normed_t[:, pl.ds(2 * rows, rows)], d_query[:, pl.ds(rows, rows)], NT)
    ).astype(BF)
    d_w_keyvalue[...] = dot(normed_t[...], d_keyvalue[...]).astype(BF)


def first_back_kernel(core, d_query, d_keyvalue, w_query, w_keyvalue, near, low):
    rows = d_query.shape[1] // 2
    grad = d_query[...].astype(F32).T.astype(BF)
    near[...] = dot(d_keyvalue[pl.ds(0, 2 * rows), :], w_keyvalue[...], NT)
    near[pl.ds(0, rows), :] += dot(grad[:rows], w_query[...], NT)
    total = dot(d_keyvalue[pl.ds(2 * rows, 2 * rows), :], w_keyvalue[...], NT)
    low[pl.ds(0, rows), :] = (total[:rows] + dot(grad[rows:], w_query[...], NT)).astype(BF)
    low[pl.ds(rows, rows), :] = total[rows:].astype(BF)


def first_sum_kernel(core, near, other, own, far):
    rows = own.shape[0]
    own[...] = near[pl.ds(0, rows), :] + other[pl.ds(0, rows), :].astype(F32)
    far[...] = (near[pl.ds(rows, rows), :] + other[pl.ds(rows, rows), :].astype(F32)).astype(BF)


def input_kernel(core, value, gain, own, far, base, out):
    whole = value[...].astype(F32)
    grad = own[...] + far[...].astype(F32)
    out[...] = base[...] + norm_back(whole, inverse_rms(whole), gain[pl.ds(0, 1), :], grad)


def gather_plain(local):
    return lax.all_gather(local, "fsdp", axis=0, tiled=True)


def scatter_plain(whole):
    return lax.psum_scatter(whole, "fsdp", scatter_dimension=0, tiled=True)


RING = (0, 2, 4, 6, 7, 5, 3, 1)
FORTH = [(RING[i], RING[(i + 1) % 8]) for i in range(8)]
BACK = [(after, before) for before, after in FORTH]


def forth(value):
    return lax.ppermute(value, "fsdp", FORTH)


def back(value):
    return lax.ppermute(value, "fsdp", BACK)


def ring_places():
    shard = lax.axis_index("fsdp")
    place = jnp.where(shard % 2 == 0, shard // 2, 7 - shard // 2)
    places = (place + jnp.array([0, -1, 1, -2, 2, -3, 3, 4], jnp.int32)) % 8
    return jnp.where(places < 4, 2 * places, 15 - 2 * places)


def vmem_call(kernel, scalars, args, out_shape, mib=10):
    return pl.pallas_call(
        kernel,
        grid_spec=pltpu.PrefetchScalarGridSpec(
            num_scalar_prefetch=1,
            grid=(1,),
            in_specs=[whole_block(arg.shape) for arg in args],
            out_specs=[whole_block(out.shape) for out in out_shape],
        ),
        out_shape=out_shape,
        compiler_params=pltpu.CompilerParams(vmem_limit_bytes=mib * 2**20),
    )(scalars, *args)


def pack_kernel(core, query, key, value, output_one, output_two, query_two, key_two, value_two, *refs):
    vectors, out = refs[:4], refs[4]
    rows, half = query.shape
    for place, weight in ((0, query), (3, output_one), (4, output_two), (5, query_two)):
        out[:, pl.ds(place * half, half)] = weight[...].astype(BF)
    for place, pair in ((1, (key, value)), (6, (key_two, value_two))):
        for part in range(half // 128):
            for turn, weight in enumerate(pair):
                lane = place * half + part * 256 + turn * 128
                out[:, pl.ds(lane, 128)] = weight[:, pl.ds(part * 128, 128)].astype(BF)
    table = jnp.concatenate([vectors[3][...], jnp.zeros((1, rows - vectors[3].shape[1]), F32)], 1)
    lines = [vector[...] for vector in vectors[:3]] + [table, jnp.zeros((4, rows), F32)]
    lines = jnp.concatenate(lines, 0).astype(BF)
    place = lax.broadcasted_iota(jnp.int32, (8, 128), 0) == lax.broadcasted_iota(jnp.int32, (8, 128), 1)
    out[:, pl.ds(8 * half, 128)] = dot(lines, jnp.where(place, 1.0, 0.0).astype(BF), TN).astype(BF)


def pack_halves(kernel, core, weights, vectors, rows, mib):
    half = weights[0].shape[1] // 2
    own = pl.BlockSpec((weights[0].shape[0], half), lambda i, c: (0, c[0]))
    columns = len(weights) * half + 128
    return pl.pallas_call(
        kernel,
        grid_spec=pltpu.PrefetchScalarGridSpec(
            num_scalar_prefetch=1,
            grid=(1,),
            in_specs=[own] * len(weights) + [pl.BlockSpec(v.shape, lambda i, c: (0, 0)) for v in vectors],
            out_specs=pl.BlockSpec((rows, columns), lambda i, c: (0, 0)),
        ),
        out_shape=jax.ShapeDtypeStruct((rows, columns), BF),
        compiler_params=pltpu.CompilerParams(vmem_limit_bytes=mib * 2**20),
    )(core, *weights, *vectors)


def pack_feed_kernel(core, gate, up, down, out):
    rows, wide = gate.shape[0], gate.shape[1] // 2
    for place, weight in enumerate((gate, up)):
        for part in range(wide // 128):
            start = pl.multiple_of(part * 256 + core[0] * 128, 128)
            out[:, pl.ds(place * wide + part * 128, 128)] = weight[:, pl.ds(start, 128)].astype(BF)
    half = down.shape[0] // 2
    top = pl.multiple_of(core[0] * half, 16)
    own = jnp.concatenate([down[pl.ds(top, half), pl.ds(j * 128, 128)].astype(BF) for j in range(down.shape[1] // 128)], 0)
    for part in range(wide // 128):
        out[:, pl.ds(2 * wide + part * 128, 128)] = own[part * rows : (part + 1) * rows]


def unfold_down(whole, shards, width):
    rows, wide = whole.shape[0] // shards, whole.shape[1]
    count = rows * wide // width

    def kernel(_, whole, out):
        for f in range(shards):
            tall = jnp.concatenate([whole[pl.ds(f * rows, rows), pl.ds(j * 128, 128)] for j in range(wide // 128)], 0)
            for j in range(width // 128):
                out[pl.ds(f * count, count), pl.ds(j * 128, 128)] = tall[j * count : (j + 1) * count]

    return vmem_call(kernel, jnp.zeros((1,), jnp.int32), [whole], [jax.ShapeDtypeStruct((shards * count, width), whole.dtype)])[0]


def fold_down(whole, shards, wide):
    width = whole.shape[1]
    count = whole.shape[0] // shards
    rows = count * width // wide

    def kernel(_, whole, out):
        for f in range(shards):
            tall = jnp.concatenate([whole[pl.ds(f * count, count), pl.ds(j * 128, 128)] for j in range(width // 128)], 0)
            for j in range(wide // 128):
                out[pl.ds(f * rows, rows), pl.ds(j * 128, 128)] = tall[j * rows : (j + 1) * rows]

    return vmem_call(kernel, jnp.zeros((1,), jnp.int32), [whole], [jax.ShapeDtypeStruct((shards * rows, wide), whole.dtype)])[0]


def put_in_order(scalars, parts, columns, extra=0, turned=(), fold=None):
    rows = parts[0].shape[0] - extra
    skip = parts[7].shape[0]
    total = 8 * rows

    def kernel(scalars, *refs):
        parts, outs = refs[:9], list(refs[9 : 9 + len(columns)])
        sems = refs[-1]
        if fold is not None:
            outs[-1] = refs[-2]
        copies = []
        for index, part in enumerate(parts):
            place = scalars[min(index, 7)]
            offset = skip if index == 8 else 0
            count = min(part.shape[0], rows - offset)
            lane = 0
            for turn, (out, width) in enumerate(zip(outs, columns)):
                start = place * rows
                if turn in turned:
                    start = lax.rem(start + scalars[8] * (total // 2), total)
                start = pl.multiple_of(start + offset, 16)
                copies.append((part.at[pl.ds(0, count), pl.ds(lane, width)], out.at[pl.ds(start, count), :]))
                lane += width
            if extra and index != 7:
                start = pl.multiple_of(place * extra, 16)
                copies.append(
                    (part.at[pl.ds(part.shape[0] - extra, extra), pl.ds(0, 128)], refs[9 + len(columns)].at[pl.ds(start, extra), :])
                )
        copies = [pltpu.make_async_copy(x, y, sems.at[i]) for i, (x, y) in enumerate(copies)]
        for copy in copies:
            copy.start()
        for copy in copies:
            copy.wait()
        if fold is not None:
            folded, out = refs[-2], refs[8 + len(columns)]
            wide, count = columns[-1], rows * columns[-1] // fold
            for f in range(8):
                tall = jnp.concatenate([folded[pl.ds(f * rows, rows), pl.ds(j * 128, 128)] for j in range(wide // 128)], 0)
                for j in range(fold // 128):
                    out[pl.ds(f * count, count), pl.ds(j * 128, 128)] = tall[j * count : (j + 1) * count]

    out_shape = [jax.ShapeDtypeStruct((total, width), BF) for width in columns]
    scratch = []
    if fold is not None:
        out_shape[-1] = jax.ShapeDtypeStruct((total * columns[-1] // fold, fold), BF)
        scratch.append(pltpu.VMEM((total, columns[-1]), BF))
    if extra:
        out_shape.append(jax.ShapeDtypeStruct((8 * extra, 128), BF))
    return pl.pallas_call(
        kernel,
        grid_spec=pltpu.PrefetchScalarGridSpec(
            num_scalar_prefetch=1,
            grid=(),
            in_specs=[pl.BlockSpec(memory_space=pltpu.HBM)] * 9,
            out_specs=[VMEM] * len(out_shape),
            scratch_shapes=scratch + [pltpu.SemaphoreType.DMA((9 * len(columns) + 9,))],
        ),
        out_shape=out_shape,
        compiler_params=pltpu.CompilerParams(vmem_limit_bytes=4 * 2**20),
    )(scalars, *parts)


def cut_apart(scalars, columns, extras, turned=()):
    rows = columns[0].shape[0] // 8
    extra = 0 if extras is None else EXTRA
    width = sum(c.shape[1] for c in columns)
    half = (rows + extra) // 32 * 16
    counts = [rows + extra] * 7 + [half, rows + extra - half]

    def kernel(scalars, *refs):
        blocks, outs, sems = refs[: len(columns)], refs[len(refs) - 10 : -1], refs[-1]
        copies = []
        for index, out in enumerate(outs):
            place = scalars[min(index, 7)]
            skip = half if index == 8 else 0
            count = min(out.shape[0], rows - skip)
            lane = 0
            for turn, block in enumerate(blocks):
                start = place * rows
                if turn in turned:
                    start = lax.rem(start + scalars[8] * 4 * rows, 8 * rows)
                start = pl.multiple_of(start + skip, 16)
                copies.append((block.at[pl.ds(start, count), :], out.at[pl.ds(0, count), pl.ds(lane, block.shape[1])]))
                lane += block.shape[1]
            if extra and index != 7:
                start = pl.multiple_of(place * extra, 16)
                copies.append((refs[len(columns)].at[pl.ds(start, extra), :], out.at[pl.ds(count, extra), :]))
        copies = [pltpu.make_async_copy(x, y, sems.at[i]) for i, (x, y) in enumerate(copies)]
        for copy in copies:
            copy.start()
        for copy in copies:
            copy.wait()

    args = list(columns) + ([] if extras is None else [extras])
    out_shape = [jax.ShapeDtypeStruct((count, width), BF) for count in counts]
    return pl.pallas_call(
        kernel,
        grid_spec=pltpu.PrefetchScalarGridSpec(
            num_scalar_prefetch=1,
            grid=(),
            in_specs=[VMEM] * len(args),
            out_specs=[pl.BlockSpec(memory_space=pl.ANY)] * 9,
            scratch_shapes=[pltpu.SemaphoreType.DMA((9 * len(columns) + 9,))],
        ),
        out_shape=out_shape,
        compiler_params=pltpu.CompilerParams(vmem_limit_bytes=4 * 2**20),
    )(scalars, *args)


def held(value, *earlier):
    return lax.optimization_barrier((value,) + earlier)[0]


def gather_hops(local, hops):
    ahead, behind, parts = local
    for _ in range(hops):
        ahead, behind = forth(ahead), back(behind)
        parts = parts + [ahead, behind]
    return ahead, behind, parts


def gather_end(state):
    ahead, behind, parts = state
    half = ahead.shape[0] // 32 * 16
    return parts + [forth(ahead[:half]), back(behind[half:])]


def gather_last(scalars, state, columns, hold=None, **options):
    parts = gather_end(state)
    if hold is not None:
        parts[-2:] = [held(part, hold) for part in parts[-2:]]
    return put_in_order(scalars, parts, columns, **options)


def held_hops(state, hold, hops=1):
    ahead, behind = lax.optimization_barrier((state[0], state[1], hold))[:2]
    return gather_hops((ahead, behind, state[2]), hops)


def add(left, right):
    return (left.astype(F32) + right.astype(F32)).astype(left.dtype)


def add_pair(one, two, three, four):
    def kernel(*refs):
        parts, (left, right), held_parts, sems = refs[:4], refs[4:6], refs[6:10], refs[10]
        copies = [pltpu.make_async_copy(x, y, sems.at[i]) for i, (x, y) in enumerate(zip(parts, held_parts))]
        for copy in copies:
            copy.start()
        for copy in copies:
            copy.wait()
        for whole, part, out, low in ((*held_parts[:2], left, False), (*held_parts[2:], right, True)):
            rows, count = whole.shape[0], part.shape[0]
            start = rows - count if low else 0
            out[pl.ds(start, count), :] = add(whole[pl.ds(start, count), :], part[...])
            if count < rows:
                rest = pl.ds(count if not low else 0, rows - count)
                out[rest, :] = whole[rest, :]

    shape = jax.ShapeDtypeStruct(one.shape, one.dtype)
    args = [one, two, three, four]
    return pl.pallas_call(
        kernel,
        in_specs=[pl.BlockSpec(memory_space=pl.ANY)] * 4,
        out_specs=[pl.BlockSpec(memory_space=pltpu.VMEM)] * 2,
        out_shape=[shape, shape],
        scratch_shapes=[pltpu.VMEM(arg.shape, arg.dtype) for arg in args] + [pltpu.SemaphoreType.DMA((4,))],
        compiler_params=pltpu.CompilerParams(vmem_limit_bytes=8 * 2**20),
        cost_estimate=pl.CostEstimate(flops=1, bytes_accessed=1, transcendentals=0),
    )(*args)


class Scatter:
    def __init__(self, pieces):
        self.own, *self.sides, top, low = pieces
        self.ahead, self.behind = forth(top), back(low)
        self.step = 0

    def wait(self, *others):
        self.ahead, self.behind = lax.optimization_barrier((self.ahead, self.behind) + others)[:2]

    def hop(self):
        m1, p1, m2, p2, m3, p3 = self.sides
        up, down = ((p3, m3), (p2, m2), (p1, m1))[self.step]
        ahead, behind = add_pair(up, self.ahead, down, self.behind)
        self.sent = (ahead, behind)
        self.ahead, self.behind = forth(ahead), back(behind)
        self.step += 1

    def total(self):
        return (self.own.astype(F32) + self.ahead.astype(F32) + self.behind.astype(F32)).astype(BF)


def finish(core, own, other, rows, outputs, weights=(), gain=None, down=None):
    widths = [2 * 128 * len(lanes) for lanes, _, _ in outputs]

    def kernel(core, own, other, *refs):
        weights, refs = refs[: len(weights_given)], refs[len(weights_given) :]
        if gain is not None:
            gain_ref, refs = refs[0], refs[1:]
        outs = refs[: len(outputs)]
        for side, source in ((core[0], own), (1 - core[0], other)):
            for out, (lanes, core_step, block_step) in zip(outs, outputs):
                for index, lane in enumerate(lanes):
                    place = pl.multiple_of(side * core_step + index * block_step, 128)
                    out[:, pl.ds(place, 128)] = source[pl.ds(0, rows), pl.ds(lane, 128)].astype(F32)
            if down is not None:
                out = refs[len(outputs)]
                count, width = out.shape[0] // 2, out.shape[1]
                blocks = count * width // (rows * 128)
                tall = jnp.concatenate([source[:, pl.ds(down + j * 128, 128)] for j in range(blocks)], 0)
                start = pl.multiple_of(side * count, 16)
                for j in range(width // 128):
                    out[pl.ds(start, count), pl.ds(j * 128, 128)] = tall[j * count : (j + 1) * count].astype(F32)
        if gain is not None:
            total = jnp.zeros((rows, 1), F32)
            for weight, out in zip(weights, outs):
                total = total + jnp.sum(weight[...].astype(BF).astype(F32) * out[...], 1, keepdims=True)
            refs[-1][...] = jnp.broadcast_to(total / gain_ref[...].astype(BF).astype(F32), (rows, 128))

    weights_given = list(weights)
    args = [own, other] + weights_given + ([] if gain is None else [gain])
    out_shape = [jax.ShapeDtypeStruct((rows, width), F32) for width in widths]
    if down is not None:
        out_shape.append(jax.ShapeDtypeStruct(down_shape(rows, own.shape[1] - down), F32))
    if gain is not None:
        out_shape.append(jax.ShapeDtypeStruct((rows, 128), F32))
    return vmem_call(kernel, core, args, out_shape)


def down_shape(rows, folded):
    return 2 * folded // 8, 8 * rows


def per_device(
    decoder_input,
    memory,
    memory_lengths,
    distance_bucket,
    cotangent,
    self_gain,
    self_query,
    self_key,
    self_value,
    self_output,
    bucket_bias,
    cross_gain,
    cross_query,
    cross_key,
    cross_value,
    cross_output,
    feed_gain,
    gate_weight,
    up_weight,
    down_weight,
):
    shards = lax.axis_size("fsdp")
    rep = lax.axis_index("rep")
    side, core = rep // 2, rep % 2
    first = core == 0
    rows = decoder_input.shape[1]
    width = decoder_input.shape[2]
    slots = memory.shape[1]
    half = width // 2
    heads = half // HEAD
    shard_rows = self_query.shape[0]
    hidden_all = gate_weight.shape[1]
    hidden_rows = down_weight.shape[0]
    hidden_half = hidden_rows // 2

    which = core.reshape(1)
    cot_own = cotangent[0]
    cot_low = cot_own.astype(BF)
    cot_other = core_swap(cot_low)
    places = jnp.stack([rep, 2 * (1 - side) + core, 2 * side + 1 - core, 2 * (1 - side) + 1 - core])

    slot = (places[:, None] * slots + jnp.arange(slots, dtype=jnp.int32)[None]).reshape(-1)
    lane = jnp.arange(128, dtype=jnp.int32)[None]
    ones = jnp.where((lane >= 1) & (lane <= 3), 1.0, 0.0)
    extra_two = (jnp.where((lane == 0) & (slot >= memory_lengths[0])[:, None], NEG, 0.0) + ones).astype(BF)
    extra_one = jnp.broadcast_to(ones, (4 * rows, 128)).astype(BF)
    codes = jnp.arange(BUCKETS, dtype=jnp.int32)
    gaps = (jnp.stack([places[0], places[2]])[None, :] - places[:, None]).reshape(-1)
    starts = gaps * 256 + 768
    below = jnp.sum((distance_bucket[None, :] < codes[:, None]).astype(jnp.int32), 1)[None]
    upto = jnp.sum((distance_bucket[None, :] <= codes[:, None]).astype(jnp.int32), 1)[None]

    ringed = shards == 8 and shard_rows % 32 == 0 and hidden_half % 128 == 0
    wide = hidden_all // 2
    if ringed:
        ring = jnp.concatenate([ring_places(), which])
        gain_columns = [gain.reshape(shard_rows, 1) for gain in (self_gain, cross_gain, feed_gain)]
        early = which
        which, ring, starts, below, upto, extra_two, gain_columns = lax.optimization_barrier(
            (which, ring, starts, below, upto, extra_two, gain_columns)
        )

        def packed(kernel, args, rows, columns):
            return vmem_call(kernel, which, args, [jax.ShapeDtypeStruct((rows, columns), BF)])[0]

        vectors = [v[None] for v in (self_gain, cross_gain, feed_gain, bucket_bias)]
        local = pack_halves(
            pack_kernel,
            early,
            [self_query, self_key, self_value, self_output, cross_output, cross_query, cross_key, cross_value],
            vectors,
            shard_rows,
            60,
        )
        state = gather_hops((local, local, [local]), 1)
    x_own, m_own = decoder_input[0], memory[0]
    x_far, m_far = far_swap(x_own), far_swap(m_own)
    x_core = core_swap(x_own)
    if ringed:
        feed = packed(pack_feed_kernel, [gate_weight, up_weight, down_weight], shard_rows, 3 * wide)
        state = held_hops(state, (feed, starts, below, upto))
        state = held_hops(state, (x_far, x_core, cot_other, extra_two))
    x_diagonal = core_swap(x_far)
    if ringed:
        state = gather_end(held_hops(state, x_diagonal, 0))
        feed = held(feed, *state[-2:])
        feed = gather_hops((feed, feed, [feed]), 1)
        query_one, kv_one, out_one, out_two, query_two, kv_two, extras = put_in_order(
            ring, state, (half, 2 * half, half, half, half, 2 * half, 128), turned=(2, 3)
        )
        gains, line = step(
            prepare_kernel, which, [extras, distance_bucket[None]], [((8, width), F32), ((8, 8 * rows), F32)], near=(0,)
        )
    else:

        def own_columns(weight):
            return lax.dynamic_slice_in_dim(weight, core * half, half, 1).astype(BF)

        def own_hidden(weight):
            parts = weight.reshape(shard_rows, shards, 2, hidden_half)
            own = lax.dynamic_index_in_dim(parts, core, 2, keepdims=False)
            return own.reshape(shard_rows, wide).astype(BF)

        def own_beside(left, right):
            return beside(own_columns(left), own_columns(right))

        query_one = gather_plain(own_columns(self_query))
        kv_one = gather_plain(own_beside(self_key, self_value))
        outs = [gather_plain(own_columns(w)) for w in (self_output, cross_output)]
        out_one, out_two = [jnp.where(first, w, jnp.concatenate([w[half:], w[:half]], 0)) for w in outs]
        query_two = gather_plain(own_columns(cross_query))
        kv_two = gather_plain(own_beside(cross_key, cross_value))
        gate_matrix = gather_plain(own_hidden(gate_weight))
        up_matrix = gather_plain(own_hidden(up_weight))
        down_half = lax.dynamic_slice_in_dim(down_weight, core * hidden_half, hidden_half, 0).astype(BF)
        down_matrix = gather_plain(down_half)
        gains = jnp.stack([gather_plain(g.astype(BF)).astype(F32) for g in (self_gain, cross_gain, feed_gain)])
        table = gather_plain(bucket_bias.astype(BF)).astype(F32)
        table = lax.dynamic_index_in_dim(table.reshape(2, heads, BUCKETS), core, 0, keepdims=False)
        hot = (distance_bucket[None, :] == codes[:, None]).astype(BF)
        line = jnp.einsum("hb,bd->hd", table.astype(BF), hot, preferred_element_type=F32)
        line = jnp.concatenate([jnp.full((heads, 4 * rows), NEG, F32), line], 1)
        line = jnp.pad(line, ((0, 8 - heads), (0, 0)))

    def owners(value):
        value = add(value, far_swap(value))
        return value, core_swap(value)

    pair = 2 * rows
    f32, b16 = (lambda *shape: (shape, F32)), (lambda *shape: (shape, BF))
    blocks = [x_own, x_far, x_core, x_diagonal]
    q1, k1v1, n1_t = step(
        first_kernel,
        which,
        [*blocks, gains, query_one, kv_one],
        [b16(half, pair), b16(4 * rows, 2 * half), b16(width, 4 * rows)],
        near=(5, 6),
        scratch=[pltpu.VMEM((4 * rows, width), BF)],
    )
    out_one_other, out_two_other = core_swap(out_one), core_swap(out_two)
    m_core, m_diagonal = core_swap(m_own), core_swap(m_far)
    k2v2 = project_blocks([m_own, m_far, m_core, m_diagonal], kv_two)
    if ringed:
        q1 = held(q1, k2v2, out_one_other, out_two_other, *feed[:2])
        feed = gather_hops(feed, 1)
    o1, logs_one = attend(q1, k1v1, None, line, starts)
    if ringed:
        o1 = held(o1, *feed[:2])
        feed = held_hops(feed, o1, 1)
    part, low_own, low_other = step(
        mix_kernel, which, [o1, out_one, out_one_other], [f32(pair, width), b16(rows, width), b16(rows, width)], near=(0,)
    )
    low_own, low_other = core_swap(low_other), core_swap(low_own)
    middle, n2, n2_t, q2 = step(
        functools.partial(norm_kernel, 2, 1, 1),
        which,
        [x_own, x_core, part, low_own, low_other, gains, query_two],
        [f32(pair, width), b16(pair, width), b16(width, pair), b16(half, pair)],
        near=(2, 6),
    )
    if ringed:
        q2 = held(q2, *feed[:2])
        feed = gather_end(held_hops(feed, q2, 0))
    o2, logs_two = attend(q2, k2v2, extra_two)
    if ringed:
        o2 = held(o2, *feed[-2:])
        m_own = held(m_own, o2)
    (m_turned,) = step(turn_kernel, which, [m_own, m_far, m_core, m_diagonal], [b16(width, 4 * slots)], 16)
    o1_other, o2_other = core_swap(o1), core_swap(o2)
    part, low_own, low_other = step(
        mix_kernel, which, [o2, out_two, out_two_other], [f32(pair, width), b16(rows, width), b16(rows, width)], near=(0,)
    )
    if ringed:
        low_own, low_other = lax.optimization_barrier((low_own, low_other, *feed[-2:]))[:2]
    low_own, low_other = core_swap(low_other), core_swap(low_own)
    after, n3, n3_t = step(
        functools.partial(norm_kernel, 1, 0, 2),
        which,
        [middle, part, low_own, low_other, gains],
        [f32(pair, width), b16(pair, width), b16(width, pair)],
        near=(1,),
    )
    if ringed:
        feed[-2:] = [held(part, m_turned) for part in feed[-2:]]
        gate_matrix, up_matrix, down_matrix = put_in_order(ring, feed, (wide, wide, wide), fold=width)

    part_low, d_gate_up_w, d_down_w, d_n3, d_low = step(
        feed_kernel,
        which,
        [n3, n3_t, gate_matrix, up_matrix, down_matrix, cot_low, cot_other],
        [b16(pair, width), b16(width, 2 * wide), b16(wide, width), f32(pair, width), b16(pair, width)],
        10,
        near=(0, 1, 2, 3, 4),
    )
    d_after, d_o2, d_out_two = step(
        functools.partial(back_kernel, 2, 2),
        which,
        [d_n3, core_swap(d_low), after, gains, cot_own, cot_other, out_two, out_two_other, o2, o2_other],
        [f32(pair, width), b16(half, pair), b16(width, half)],
    )

    back_two = functools.partial(attend_back, q2, k2v2, extra_two, o2)
    if ringed:
        feed_ring = Scatter(cut_apart(ring, [d_gate_up_w, fold_down(d_down_w, shards, wide)], None))
        feed_ring.wait(d_after)
        d_o2 = held(d_o2, feed_ring.ahead, feed_ring.behind)
        feed_ring.hop()
    d_q2_a, d_kv2 = back_two(d_o2, logs_two, base=0, pairs=1)
    d_q2_b, d_kv2 = back_two(held(d_o2, d_q2_a), logs_two, base=1, pairs=1, earlier=d_kv2)
    if ringed:
        d_q2_b = held(d_q2_b, feed_ring.ahead, feed_ring.behind)
        feed_ring.wait(d_q2_b)
        feed_ring.hop()
    d_q2_c, d_kv2 = back_two(held(d_o2, d_q2_b), logs_two, base=2, pairs=heads // 2 - 2, earlier=d_kv2)
    if ringed:
        d_q2_c, d_kv2 = lax.optimization_barrier((d_q2_c, d_kv2, feed_ring.ahead, feed_ring.behind))[:2]
        feed_ring.wait(d_q2_c)
        feed_ring.hop()
        d_q2_c, d_kv2 = lax.optimization_barrier((d_q2_c, d_kv2, *feed_ring.sent))[:2]
    d_q2 = jnp.concatenate([d_q2_a, d_q2_b, d_q2_c], 0)
    part, low, d_query_two = step(
        query_kernel, which, [d_q2, query_two, n2_t], [f32(pair, width), b16(pair, width), b16(width, half)]
    )
    low = core_swap(low)
    d_middle, d_o1, d_out_one = step(
        functools.partial(back_kernel, 1, 1),
        which,
        [part, low, middle, gains, d_after, out_one, out_one_other, o1, o1_other],
        [f32(pair, width), b16(half, pair), b16(width, half)],
    )
    d_mem_core = core_swap(step(memory_core_kernel, which, [d_kv2, kv_two], [b16(2 * slots, width)], near=(0,))[0])
    (d_kv_two,) = step(memory_weight_kernel, which, [m_turned, d_kv2], [b16(width, 2 * half)], near=(1,))
    d_memory, d_memory_far = step(
        memory_near_kernel, which, [d_kv2, kv_two, d_mem_core], [f32(slots, width), b16(slots, width)], near=(0,)
    )
    d_memory_far_sum = far_swap(d_memory_far)

    cross_parts = [d_query_two, d_kv_two, d_out_two, d_out_one]
    if ringed:
        pieces = list(cut_apart(ring, cross_parts, None, (2, 3)))
        pieces[-2:] = lax.optimization_barrier((*pieces[-2:], feed_ring.ahead, feed_ring.behind))[:2]
        cross_ring = Scatter(pieces)
        feed_ring.wait(d_memory_far)
        feed_own, feed_other = owners(feed_ring.total())
        d_o1 = held(d_o1, d_memory_far)
    back_one = functools.partial(attend_back, q1, k1v1, extra_one, o1)
    d_q1_a, d_kv1, d_far_a = back_one(d_o1, logs_one, line, starts, base=0, pairs=1)
    d_o1_b = held(d_o1, d_q1_a)
    if ringed:
        d_o1_b = held(d_o1_b, cross_ring.ahead, cross_ring.behind)
        cross_ring.wait(d_q1_a)
        cross_ring.hop()
    d_q1_b, d_kv1, d_far_b = back_one(d_o1_b, logs_one, line, starts, base=1, pairs=1, earlier=d_kv1)
    d_q1_c, d_kv1, d_far_c = back_one(
        held(d_o1, d_q1_b), logs_one, line, starts, base=2, pairs=heads // 2 - 2, earlier=d_kv1
    )
    if ringed:
        d_q1_c, d_kv1, d_far_c = lax.optimization_barrier((d_q1_c, d_kv1, d_far_c, cross_ring.ahead, cross_ring.behind))[:3]
        cross_ring.wait(d_q1_c)
        cross_ring.hop()
    d_q1 = jnp.concatenate([d_q1_a, d_q1_b, d_q1_c], 0)
    if ringed:
        (table_rows,) = step(
            table_kernel, (which, starts), [below, upto, d_far_a, d_far_b, d_far_c], [b16(8 * EXTRA, 3 * half)]
        )
        d_kv1 = held(d_kv1, table_rows, d_memory_far_sum)
        d_query_one, d_kv_one = step(
            first_weights_kernel, which, [d_q1, d_kv1, n1_t], [b16(width, half), b16(width, 2 * half)]
        )
        cross_ring.wait(d_q1_c)
        cross_ring.hop()
        pieces = list(cut_apart(ring, [d_query_one, d_kv_one], table_rows))
        pieces[-2:] = lax.optimization_barrier((*pieces[-2:], cross_ring.ahead, cross_ring.behind))[:2]
        self_ring = Scatter(pieces)
        self_ring.hop()
        d_q1 = held(d_q1, *self_ring.sent)
    after_own, output_other = after[:rows], core_swap(part_low[rows:])
    if ringed:
        after_own, d_memory = held(after_own, self_ring.own), held(d_memory, self_ring.own)
    output = after_own + part_low[:rows].astype(F32) + output_other.astype(F32)
    d_memory = d_memory + d_memory_far_sum.astype(F32)
    near, low = step(
        first_back_kernel, which, [d_q1, d_kv1, query_one, kv_one], [f32(pair, width), b16(pair, width)]
    )
    low = core_swap(low)
    d_n1, d_n1_far = step(first_sum_kernel, which, [near, low], [f32(rows, width), b16(rows, width)])
    d_n1_other = far_swap(d_n1_far)
    (d_input,) = step(
        input_kernel, which, [x_own, gains, d_n1, d_n1_other, d_middle[:rows]], [f32(rows, width)]
    )

    blocks = half // 128
    plain = lambda start: ([start + 128 * i for i in range(blocks)], half, 128)
    turns = lambda start: [([start + 256 * i + 128 * t for i in range(blocks)], half, 128) for t in range(2)]
    if ringed:
        self_ring.wait(d_n1_far)
        self_ring.hop()
        hidden = lambda start: ([start + 128 * i for i in range(wide // 128)], 128, 256)
        d_gate_out, d_up_out, d_down_out, d_gain_three = finish(
            which, feed_own, feed_other, shard_rows, [hidden(0), hidden(wide)], (gate_weight, up_weight), gain_columns[2], 2 * wide
        )
        cross_sum = cross_ring.total()
        cross_own, cross_other = owners(cross_sum)
        self_ring.wait(d_down_out, cross_sum)
        self_ring.hop()
        self_ring.wait(d_n1_other)
        d_cross = finish(
            which,
            cross_own,
            cross_other,
            shard_rows,
            [plain(0), *turns(half), plain(3 * half), plain(4 * half)],
            (cross_query,),
            gain_columns[1],
        )
        self_sum = self_ring.total()
        self_own = held(add(self_sum, far_swap(self_sum)), d_input, d_cross[0], output)
        self_other = core_swap(self_own)
        d_self = finish(
            which,
            self_own,
            self_other,
            shard_rows,
            [plain(0), *turns(half)],
            (self_query, self_key, self_value),
            gain_columns[0],
        )
        table_own, table_other = [v[shard_rows, : shard_rows // 2].astype(F32) for v in (self_own, self_other)]
        d_gains = [d_self[3][:, 0], d_cross[5][:, 0], d_gain_three[:, 0]]
        d_output_one_out = d_cross[4]
    else:
        d_query_one, d_kv_one = step(
            first_weights_kernel, which, [d_q1, d_kv1, n1_t], [b16(width, half), b16(width, 2 * half)]
        )

        def whole(both, axis=1):
            own, other = both
            return jnp.concatenate([jnp.where(first, own, other), jnp.where(first, other, own)], axis).astype(F32)

        def plain_owners(value):
            return owners(scatter_plain(value))

        def kv_whole(both):
            pick = lambda v, turn: v.reshape(shard_rows, -1, 2, 128)[:, :, turn].reshape(shard_rows, half)
            return [whole([pick(v, turn) for v in both]) for turn in range(2)]

        def hidden_whole(both):
            both = [v.reshape(shard_rows, shards, 1, hidden_half) for v in both]
            return whole(both, 2).reshape(shard_rows, hidden_all)

        def in_order(value):
            return jnp.where(first, value, jnp.concatenate([value[half:], value[:half]], 0))

        far = (gaps[:, None] * 256 + jnp.arange(512, dtype=jnp.int32)[None] - 255).reshape(-1)
        inside = ((far[None] >= below[0][:, None]) & (far[None] < upto[0][:, None])).astype(F32)
        d_far = jnp.concatenate([d_far_a, d_far_b, d_far_c], 0).reshape(heads, -1)
        d_table = jnp.einsum("hd,bd->hb", d_far, inside, precision=lax.Precision.HIGHEST).reshape(1, -1)
        d_table = jnp.concatenate([jnp.where(first, d_table, 0.0), jnp.where(first, 0.0, d_table)], 1)
        d_table = d_table.reshape(shards, shard_rows // 2).astype(BF)

        def gain_grad(gain, *pairs):
            total = sum(jnp.sum(w.astype(BF).astype(F32) * g, 1) for w, g in pairs)
            return total / gain.astype(BF).astype(F32)

        d_gate_out, d_up_out = [hidden_whole(plain_owners(v)) for v in (d_gate_up_w[:, :wide], d_gate_up_w[:, wide:])]
        d_down_out = whole(plain_owners(d_down_w), 0)
        d_cross = [whole(plain_owners(d_query_two)), *kv_whole(plain_owners(d_kv_two))]
        d_cross.append(whole(plain_owners(in_order(d_out_two))))
        d_output_one_out = whole(plain_owners(in_order(d_out_one)))
        d_self = [whole(plain_owners(d_query_one)), *kv_whole(plain_owners(d_kv_one))]
        table_own, table_other = [v[0].astype(F32) for v in plain_owners(d_table)]
        d_gains = [
            gain_grad(self_gain, (self_query, d_self[0]), (self_key, d_self[1]), (self_value, d_self[2])),
            gain_grad(cross_gain, (cross_query, d_cross[0])),
            gain_grad(feed_gain, (gate_weight, d_gate_out), (up_weight, d_up_out)),
        ]
    d_bucket = table_own + table_other

    return (
        output[None],
        d_input[None],
        d_memory[None],
        d_gains[0],
        d_self[0],
        d_self[1],
        d_self[2],
        d_output_one_out,
        d_bucket,
        d_gains[1],
        d_cross[0],
        d_cross[1],
        d_cross[2],
        d_cross[3],
        d_gains[2],
        d_gate_out,
        d_up_out,
        d_down_out,
    )


def solution(mesh):
    split = P("fsdp", "rep", None)
    vector, matrix = P("fsdp"), P("fsdp", None)
    weights = (
        (vector,)
        + (matrix,) * 4
        + (vector, vector)
        + (matrix,) * 4
        + (vector,)
        + (matrix,) * 3
    )
    return jax.shard_map(
        per_device,
        mesh=mesh,
        in_specs=(split, split, vector, P(), split) + weights,
        out_specs=(split, split, split) + weights,
        check_vma=False,
    )
```

```python
import functools

import jax
import jax.numpy as jnp
from jax import lax
from jax.experimental import pallas as pl
from jax.experimental.pallas import tpu as pltpu
from jax.sharding import PartitionSpec as P

HEAD = 64
BUCKETS = 32
EXTRA = 16
EPS = 1e-06
NEG = -1e30
BF = jnp.bfloat16
F32 = jnp.float32
NN = (((1,), (0,)), ((), ()))
NT = (((1,), (1,)), ((), ()))
TN = (((0,), (0,)), ((), ()))
TT = (((0,), (1,)), ((), ()))

CORE = [(0, 1), (1, 0), (2, 3), (3, 2)]
FAR = [(0, 2), (2, 0), (1, 3), (3, 1)]


def core_swap(value):
    return lax.ppermute(value, "rep", CORE)


def far_swap(value):
    return lax.ppermute(value, "rep", FAR)


def dot(left, right, dims=NN):
    return lax.dot_general(left, right, dims, preferred_element_type=F32)


def half_rows(pair, head):
    row = lax.broadcasted_iota(jnp.int32, pair.shape, 0)
    keep = (row < HEAD) if head == 0 else (row >= HEAD)
    return jnp.where(keep, pair, jnp.zeros_like(pair))


def three_terms(value):
    first = value.astype(BF)
    rest = value - first.astype(F32)
    second = rest.astype(BF)
    third = (rest - second.astype(F32)).astype(BF)
    return first, second, third


def extra_rows(first_row, vector):
    terms = three_terms(-vector)
    row = lax.broadcasted_iota(jnp.int32, (128, vector.shape[1]), 0)
    out = jnp.where(row == 0, first_row, 0.0)
    for place, term in enumerate(terms):
        out = jnp.where(row == place + 1, term.astype(F32), out)
    return out.astype(BF)


def spread(line, starts, head, part, blocks, lanes):
    block = 256
    rows = []
    for j in range(blocks):
        tiles = []
        for i in range(lanes):
            start = pl.multiple_of(starts[(part * blocks + j) * lanes + i], 128)
            row = line[pl.ds(head, 1), pl.ds(start, 2 * block)]
            tile = pltpu.roll(jnp.broadcast_to(row, (block, 2 * block)), 0, 1, stride=1, stride_axis=0)
            tiles.append(tile[:, block:])
        rows.append(jnp.concatenate(tiles, 1))
    return jnp.concatenate(rows, 0)


def attend_kernel(chunk, biased, base, *refs):
    if biased:
        starts, query, keyvalue, line, mixed, log_total = refs
    else:
        query, keyvalue, extra, mixed, log_total = refs
    keys, rows = keyvalue.shape[0], query.shape[1]
    key, value = keyvalue.at[:, pl.ds(0, 128)], keyvalue.at[:, pl.ds(128, 128)]
    pair = query[...]
    row = lax.broadcasted_iota(jnp.int32, (128, rows), 0)
    one = jnp.where(row == 0, 1.0, 0.0).astype(BF)
    wide = [half_rows(pair, h) for h in range(2)]
    if not biased:
        wide = [jnp.concatenate([w, one], 0) for w in wide]

    def score(part, head):
        span = pl.ds(part * chunk, chunk)
        if not biased:
            return dot(jnp.concatenate([key[span, :], extra[span, :]], 1), wide[head])
        full = 2 * (base + pl.program_id(0)) + head
        return dot(key[span, :], wide[head]) + spread(line, starts, full, part, chunk // 256, rows // 256)

    highest = [jnp.full((1, rows), NEG, F32)] * 2
    total = [jnp.zeros((1, rows), F32)] * 2
    acc = [jnp.zeros((HEAD, rows), F32)] * 2
    steps = [(part, head) for part in range(keys // chunk) for head in range(2)]
    ahead = score(*steps[0])
    for index, (part, head) in enumerate(steps):
        scores = ahead
        if index + 1 < len(steps):
            ahead = score(*steps[index + 1])
        span = pl.ds(part * chunk, chunk)
        top = jnp.maximum(highest[head], jnp.max(scores, 0, keepdims=True))
        soft = jnp.exp(scores - top)
        scale = jnp.exp(highest[head] - top)
        total[head] = total[head] * scale + jnp.sum(soft, 0, keepdims=True)
        product = dot(value[span, :], soft.astype(BF), TN)[head * HEAD : (head + 1) * HEAD]
        acc[head] = acc[head] * scale + product
        highest[head] = top
    for head in range(2):
        mixed[pl.ds(head * HEAD, HEAD), :] = (acc[head] / total[head]).astype(BF)
        log_total[0, pl.ds(head, 1), :] = highest[head] + jnp.log(total[head])


def attend(query, keyvalue, extra, line=None, starts=None, chunk=512, base=0, pairs=None, modelled=0.3):
    rows, keys = query.shape[1], keyvalue.shape[0]
    pairs = query.shape[0] // 128 if pairs is None else pairs
    width = pairs * 128
    biased = line is not None
    in_specs = [pl.BlockSpec((128, rows), lambda p, *s: (p + base, 0)), pl.BlockSpec((keys, 256), lambda p, *s: (0, p + base))]
    out_specs = [pl.BlockSpec((128, rows), lambda p, *s: (p, 0)), pl.BlockSpec((1, 8, rows), lambda p, *s: (p, 0, 0))]
    out_shape = [jax.ShapeDtypeStruct((width, rows), BF), jax.ShapeDtypeStruct((pairs, 8, rows), F32)]
    args = [query, keyvalue]
    if biased:
        args = [starts] + args + [line]
        in_specs.append(pl.BlockSpec(line.shape, lambda p, *s: (0, 0)))
    else:
        args.append(extra)
        in_specs.append(pl.BlockSpec((keys, 128), lambda p, *s: (0, 0)))
    return pl.pallas_call(
        functools.partial(attend_kernel, chunk, biased, base),
        grid_spec=pltpu.PrefetchScalarGridSpec(
            num_scalar_prefetch=int(biased), grid=(pairs,), in_specs=in_specs, out_specs=out_specs
        ),
        out_shape=out_shape,
        compiler_params=pltpu.CompilerParams(vmem_limit_bytes=12 * 2**20),
        cost_estimate=pl.CostEstimate(flops=1, bytes_accessed=1 + int(3.7e6 * modelled), transcendentals=0),
    )(*args)


def attend_back_kernel(chunk, biased, chained, base, *refs):
    if biased:
        starts, query, keyvalue, extra, mixed, grad, log_total, line = refs[:8]
        d_query, d_keyvalue, d_far = refs[8 + chained :]
    else:
        query, keyvalue, extra, mixed, grad, log_total = refs[:6]
        d_query, d_keyvalue = refs[6 + chained :]
    keys, rows = keyvalue.shape[0], query.shape[1]
    key, value = keyvalue.at[:, pl.ds(0, 128)], keyvalue.at[:, pl.ds(128, 128)]
    pair, grad_pair = query[...], grad[...]
    product = mixed[...].astype(F32) * grad_pair.astype(F32)
    q_half = [half_rows(pair, h) for h in range(2)]
    g_half = [half_rows(grad_pair, h) for h in range(2)]
    q_wide, g_wide = [], []
    for head in range(2):
        inner = jnp.sum(product[head * HEAD : (head + 1) * HEAD], 0, keepdims=True)
        logs = log_total[0, pl.ds(head, 1), :]
        q_wide.append(jnp.concatenate([q_half[head], extra_rows(1.0, logs)], 0))
        g_wide.append(jnp.concatenate([g_half[head], extra_rows(0.0, inner)], 0))
    if biased:
        block = 256
        down = lax.broadcasted_iota(jnp.int32, (block, block), 0)
        over = lax.broadcasted_iota(jnp.int32, (block, block), 1)
        flip = jnp.where(down + over == block - 1, 1.0, 0.0).astype(BF)
    acc = [jnp.zeros((HEAD, rows), F32) for _ in range(2)]
    for part in range(keys // chunk):
        span = pl.ds(part * chunk, chunk)
        key_wide = jnp.concatenate([key[span, :], extra[span, :]], 1)
        value_wide = jnp.concatenate([value[span, :], extra[span, :]], 1)
        dv, dk = 0.0, 0.0
        for head in range(2):
            scores = dot(key_wide, q_wide[head])
            if biased:
                full = 2 * (base + pl.program_id(0)) + head
                scores = scores + spread(line, starts, full, part, chunk // 256, rows // 256)
            soft = jnp.exp(scores)
            d_scores = (soft * dot(value_wide, g_wide[head])).astype(BF)
            dv = dv + dot(soft.astype(BF), g_half[head], NT)
            dk = dk + dot(d_scores, q_half[head], NT)
            step = dot(key[span, :], d_scores, TN)[head * HEAD : (head + 1) * HEAD]
            acc[head] = acc[head] + step
            if biased:
                for j in range(chunk // block):
                    for i in range(rows // block):
                        tile = d_scores[j * block : (j + 1) * block, i * block : (i + 1) * block]
                        tile = jnp.concatenate([dot(flip, tile), jnp.zeros((block, block), F32)], 1)
                        tile = pltpu.roll(tile, 0, 1, stride=1, stride_axis=0)
                        place = (part * (chunk // block) + j) * (rows // block) + i
                        d_far[0, head, pl.ds(place, 1), :] = jnp.sum(tile, 0, keepdims=True)
        d_keyvalue[span, :] = jnp.concatenate([dk.astype(BF), dv.astype(BF)], 1)
    for head in range(2):
        d_query[pl.ds(head * HEAD, HEAD), :] = acc[head].astype(BF)


def attend_back(
    query, keyvalue, extra, mixed, grad, log_total, line=None, starts=None, chunk=512, base=0, pairs=None, earlier=None, modelled=0.3
):
    rows, keys = query.shape[1], keyvalue.shape[0]
    pairs = query.shape[0] // 128 if pairs is None else pairs
    width = pairs * 128
    biased = line is not None
    across = pl.BlockSpec((128, rows), lambda p, *s: (p + base, 0))
    along = pl.BlockSpec((keys, 256), lambda p, *s: (0, p + base))
    in_specs = [
        across,
        along,
        pl.BlockSpec((keys, 128), lambda p, *s: (0, 0)),
        across,
        across,
        pl.BlockSpec((1, 8, rows), lambda p, *s: (p + base, 0, 0)),
    ]
    args = [query, keyvalue, extra, mixed, grad, log_total]
    out_specs = [pl.BlockSpec((128, rows), lambda p, *s: (p, 0)), along]
    out_shape = [jax.ShapeDtypeStruct((width, rows), BF), jax.ShapeDtypeStruct(keyvalue.shape, BF)]
    if biased:
        in_specs.append(pl.BlockSpec(line.shape, lambda p, *s: (0, 0)))
        args = [starts] + args + [line]
        blocks = (keys // 256) * (rows // 256)
        out_specs.append(pl.BlockSpec((1, 2, blocks, 512), lambda p, *s: (p, 0, 0, 0)))
        out_shape.append(jax.ShapeDtypeStruct((pairs, 2, blocks, 512), F32))
    aliases = {}
    if earlier is not None:
        aliases = {len(args): 1}
        in_specs.append(pl.BlockSpec(memory_space=pl.ANY))
        args.append(earlier)
    return pl.pallas_call(
        functools.partial(attend_back_kernel, chunk, biased, int(earlier is not None), base),
        grid_spec=pltpu.PrefetchScalarGridSpec(
            num_scalar_prefetch=int(biased), grid=(pairs,), in_specs=in_specs, out_specs=out_specs
        ),
        out_shape=out_shape,
        input_output_aliases=aliases,
        compiler_params=pltpu.CompilerParams(vmem_limit_bytes=10 * 2**20),
        cost_estimate=pl.CostEstimate(flops=1, bytes_accessed=1 + int(3.7e6 * modelled), transcendentals=0),
    )(*args)


def project_blocks(blocks, weight):
    def kernel(*refs):
        weight, out = refs[-2:]
        row = 0
        for block in refs[:-2]:
            for part in range(block.shape[0] // blocks[0].shape[0]):
                count = blocks[0].shape[0]
                out[pl.ds(row, count), :] = dot(block[pl.ds(part * count, count), :], weight[...]).astype(BF)
                row += count

    rows = sum(block.shape[0] for block in blocks)
    return pl.pallas_call(
        kernel,
        in_specs=[pl.BlockSpec(block.shape, lambda: (0, 0)) for block in blocks] + [pl.BlockSpec(memory_space=pltpu.VMEM)],
        out_specs=pl.BlockSpec(memory_space=pltpu.VMEM),
        out_shape=jax.ShapeDtypeStruct((rows, weight.shape[1]), BF),
        compiler_params=pltpu.CompilerParams(vmem_limit_bytes=12 * 2**20),
        cost_estimate=pl.CostEstimate(flops=1, bytes_accessed=1, transcendentals=0),
    )(*blocks, weight)


def beside(left, right):
    rows, half = left.shape
    return jnp.stack([left.reshape(rows, -1, 128), right.reshape(rows, -1, 128)], 2).reshape(rows, 2 * half)


VMEM = pl.BlockSpec(memory_space=pltpu.VMEM)


def whole_block(shape):
    return pl.BlockSpec(shape, lambda *i: (0,) * len(shape), pipeline_mode=pl.Buffered(1))


def step(kernel, core, args, shapes, mib=10, near=(), scratch=()):
    scalars = core if isinstance(core, tuple) else (core,)
    return pl.pallas_call(
        kernel,
        grid_spec=pltpu.PrefetchScalarGridSpec(
            num_scalar_prefetch=len(scalars),
            grid=(1,),
            in_specs=[VMEM if i in near else whole_block(arg.shape) for i, arg in enumerate(args)],
            out_specs=[VMEM] * len(shapes),
            scratch_shapes=list(scratch),
        ),
        out_shape=[jax.ShapeDtypeStruct(shape, kind) for shape, kind in shapes],
        compiler_params=pltpu.CompilerParams(vmem_limit_bytes=mib * 2**20),
        cost_estimate=pl.CostEstimate(flops=1, bytes_accessed=1, transcendentals=0),
    )(*scalars, *args)


def inverse_rms(value):
    return lax.rsqrt(jnp.mean(value * value, -1, keepdims=True) + EPS)


def norm_back(value, inverse, gain, grad):
    scaled = grad * gain
    return inverse * (scaled - value * (inverse * inverse) * jnp.mean(scaled * value, -1, keepdims=True))


def rows_turned(ref):
    half = ref.shape[0] // 2
    return jnp.concatenate([ref[pl.ds(half, half), :], ref[pl.ds(0, half), :]], 0)


def lanes_turned(ref):
    half = ref.shape[1] // 2
    return jnp.concatenate([ref[:, pl.ds(half, half)], ref[:, pl.ds(0, half)]], 1)


def halves(core, half):
    return pl.ds(pl.multiple_of(core[0] * half, 128), half), pl.ds(pl.multiple_of((1 - core[0]) * half, 128), half)


def first_kernel(core, own, far, near, diagonal, gain, w_query, w_keyvalue, query, keyvalue, normed_t, normed):
    rows = own.shape[0]
    for place, block in enumerate((own, far, near, diagonal)):
        value = block[...].astype(F32)
        value = value * inverse_rms(value) * gain[pl.ds(0, 1), :]
        normed[pl.ds(place * rows, rows), :] = value.astype(BF)
        normed_t[:, pl.ds(place * rows, rows)] = value.T.astype(BF)
    keyvalue[...] = dot(normed[...], w_keyvalue[...]).astype(BF)
    mine = jnp.concatenate([normed[pl.ds(0, rows), :], normed[pl.ds(2 * rows, rows), :]], 0)
    query[...] = dot(mine, w_query[...]).T.astype(BF)


def prepare_kernel(core, extras, buckets, gains, line):
    count = gains.shape[1] // 8
    lines = extras[...].astype(F32).T
    gains[...] = lines[:8]
    table = jnp.concatenate([lines[3:4, f * count : f * count + count // 2] for f in range(8)], 1)
    entries = table.shape[1]
    heads = entries // BUCKETS // 2
    head = lax.broadcasted_iota(jnp.int32, (8, entries), 0)
    entry = lax.broadcasted_iota(jnp.int32, (8, entries), 1)
    first = (core[0] * heads + head) * BUCKETS
    mine = (entry >= first) & (entry < first + BUCKETS) & (head < heads)
    rows = jnp.where(mine, jnp.broadcast_to(table, (8, entries)), 0.0).astype(BF)
    length = buckets.shape[1]
    code = lax.broadcasted_iota(jnp.int32, (entries, length), 0) & (BUCKETS - 1)
    hot = jnp.where(code == buckets[...], 1.0, 0.0).astype(BF)
    line[:, pl.ds(0, length)] = jnp.full((8, length), NEG, F32)
    line[:, pl.ds(length, length)] = dot(rows, hot)


def table_kernel(core, starts, below, upto, *refs):
    parts, out = refs[:-1], refs[-1]
    heads = sum(2 * far.shape[0] for far in parts)
    total = jnp.zeros((8, BUCKETS), F32)
    for block in range(8):
        rows = [far[p, h, pl.ds(block, 1), :] for far in parts for p in range(far.shape[0]) for h in range(2)]
        rows = jnp.concatenate(rows + [jnp.zeros((8 - heads, 512), F32)], 0)
        distance = lax.broadcasted_iota(jnp.int32, (512, BUCKETS), 0) + (starts[block] - 1023)
        hot = jnp.where((distance >= below[...]) & (distance < upto[...]), 1.0, 0.0).astype(BF)
        for term in three_terms(rows):
            total = total + dot(term, hot)
    entries = 2 * heads * BUCKETS
    spot = lax.broadcasted_iota(jnp.int32, (BUCKETS, entries), 1) - lax.broadcasted_iota(jnp.int32, (BUCKETS, entries), 0)
    line = jnp.zeros((1, entries), F32)
    for head in range(heads):
        pick = jnp.where(spot == (core[0] * heads + head) * BUCKETS, 1.0, 0.0).astype(BF)
        line = line + dot(total[head : head + 1].astype(BF), pick)
    out[...] = jnp.zeros(out.shape, BF)
    count = entries // 8
    for f in range(8):
        out[pl.ds(f * EXTRA, 1), pl.ds(0, count)] = line[:, f * count : (f + 1) * count].astype(BF)


def mix_kernel(core, mixed, weight, w_theirs, part, low_own, low_other):
    half = mixed.shape[0]
    mine, theirs = halves(core, half)
    part[:, mine] = dot(mixed[...], weight[pl.ds(0, half), :], TN)
    part[:, theirs] = dot(mixed[...], w_theirs[pl.ds(half, half), :], TN)
    rows = low_own.shape[0]
    low_own[...] = part[pl.ds(0, rows), :].astype(BF)
    low_other[...] = part[pl.ds(rows, rows), :].astype(BF)


def stacked(refs):
    blocks = [ref[...].astype(F32) for ref in refs]
    return blocks[0] if len(blocks) == 1 else jnp.concatenate(blocks, 0)


def norm_kernel(parts, projected, which, core, *refs):
    base, (part, own, other, gain) = refs[:parts], refs[parts : parts + 4]
    value, normed, normed_t = refs[parts + 4 + projected : parts + 7 + projected]
    whole = stacked(base) + part[...] + stacked((own, other))
    value[...] = whole
    whole = whole * inverse_rms(whole) * gain[pl.ds(which, 1), :]
    normed[...] = whole.astype(BF)
    normed_t[...] = whole.T.astype(BF)
    if projected:
        refs[-1][...] = dot(normed[...], refs[parts + 4][...]).T.astype(BF)


def feed_kernel(core, normed, normed_t, gate, up, down, cot_own, cot_other, own, other, grads, d_down, d_normed, d_low_own, d_low_other):
    wide = gate.shape[1]
    scale, cubic = 0.7978845608028654, 0.044715
    grad_out = jnp.concatenate([cot_own[...], cot_other[...]], 0)
    total, back_total = 0.0, 0.0
    for start in range(0, wide, 256):
        span = pl.ds(start, 256)
        g = dot(normed[...], gate[:, span])
        u = dot(normed[...], up[:, span])
        square = g * g
        t = jnp.tanh(scale * (g + cubic * square * g))
        act = 0.5 * g * (1.0 + t)
        slope = 0.5 * (1.0 + t) + 0.5 * g * (1.0 - t * t) * (scale * (1.0 + 3.0 * cubic * square))
        hidden = (act * u).astype(BF)
        d_hidden = dot(grad_out, down[span, :], NT)
        d_gate = (d_hidden * u * slope).astype(BF)
        d_up = (d_hidden * act).astype(BF)
        total = total + dot(hidden, down[span, :])
        back_total = back_total + dot(d_gate, gate[:, span], NT) + dot(d_up, up[:, span], NT)
        grads[:, span] = dot(normed_t[...], d_gate).astype(BF)
        grads[:, pl.ds(wide + start, 256)] = dot(normed_t[...], d_up).astype(BF)
        d_down[span, :] = dot(hidden, grad_out, TN).astype(BF)
    rows = own.shape[0]
    own[...] = total[:rows]
    other[...] = total[rows:].astype(BF)
    d_normed[...] = back_total
    d_low_own[...] = back_total[:rows].astype(BF)
    d_low_other[...] = back_total[rows:].astype(BF)


def back_kernel(parts, which, core, *refs):
    part, own, other, value, gain = refs[:5]
    base = refs[5 : 5 + parts]
    weight, w_theirs, mixed, mixed_other = refs[5 + parts : 9 + parts]
    d_value, d_mixed, d_weight = refs[9 + parts :]
    half = weight.shape[1]
    grad = part[...] + stacked((own, other))
    whole = value[...]
    d_value[...] = stacked(base) + norm_back(whole, inverse_rms(whole), gain[pl.ds(which, 1), :], grad)
    mine, theirs = halves(core, half)
    d_mine, d_theirs = d_value[:, mine].astype(BF), d_value[:, theirs].astype(BF)
    d_mixed[...] = (dot(weight[pl.ds(0, half), :], d_mine, NT) + dot(w_theirs[pl.ds(half, half), :], d_theirs, NT)).astype(BF)
    d_weight[pl.ds(0, half), :] = dot(mixed[...], d_mine).astype(BF)
    d_weight[pl.ds(half, half), :] = dot(lanes_turned(mixed_other), d_mine).astype(BF)


def query_kernel(core, d_query, weight, normed_t, part, low_own, low_other, d_weight):
    grad = d_query[...].astype(F32).T.astype(BF)
    total = dot(grad, weight[...], NT)
    part[...] = total
    rows = low_own.shape[0]
    low_own[...] = total[:rows].astype(BF)
    low_other[...] = total[rows:].astype(BF)
    d_weight[...] = dot(normed_t[...], d_query[...], NT).astype(BF)


def memory_core_kernel(core, d_keyvalue, weight, out):
    rows = out.shape[0]
    out[...] = dot(d_keyvalue[pl.ds(rows, rows), :], weight[...], NT).astype(BF)


def memory_weight_kernel(core, memory_t, d_keyvalue, out):
    out[...] = dot(memory_t[...], d_keyvalue[...]).astype(BF)


def memory_near_kernel(core, d_keyvalue, weight, other, own, far):
    rows = own.shape[0]
    own[...] = dot(d_keyvalue[pl.ds(0, rows), :], weight[...], NT) + other[pl.ds(0, rows), :].astype(F32)
    total = dot(d_keyvalue[pl.ds(rows, rows), :], weight[...], NT) + other[pl.ds(rows, rows), :].astype(F32)
    far[...] = total.astype(BF)


def turn_kernel(core, *refs):
    blocks, out = refs[:-1], refs[-1]
    for place, block in enumerate(blocks):
        rows = block.shape[0]
        out[:, pl.ds(place * rows, rows)] = block[...].astype(F32).T.astype(BF)


def first_weights_kernel(core, d_query, d_keyvalue, normed_t, d_w_query, d_w_keyvalue):
    rows = d_query.shape[1] // 2
    d_w_query[...] = (
        dot(normed_t[:, pl.ds(0, rows)], d_query[:, pl.ds(0, rows)], NT)
        + dot(normed_t[:, pl.ds(2 * rows, rows)], d_query[:, pl.ds(rows, rows)], NT)
    ).astype(BF)
    d_w_keyvalue[...] = dot(normed_t[...], d_keyvalue[...]).astype(BF)


def first_back_kernel(core, d_query, d_keyvalue, w_query, w_keyvalue, near, low):
    rows = d_query.shape[1] // 2
    grad = d_query[...].astype(F32).T.astype(BF)
    near[...] = dot(d_keyvalue[pl.ds(0, 2 * rows), :], w_keyvalue[...], NT)
    near[pl.ds(0, rows), :] += dot(grad[:rows], w_query[...], NT)
    total = dot(d_keyvalue[pl.ds(2 * rows, 2 * rows), :], w_keyvalue[...], NT)
    low[pl.ds(0, rows), :] = (total[:rows] + dot(grad[rows:], w_query[...], NT)).astype(BF)
    low[pl.ds(rows, rows), :] = total[rows:].astype(BF)


def first_sum_kernel(core, near, other, own, far):
    rows = own.shape[0]
    own[...] = near[pl.ds(0, rows), :] + other[pl.ds(0, rows), :].astype(F32)
    far[...] = (near[pl.ds(rows, rows), :] + other[pl.ds(rows, rows), :].astype(F32)).astype(BF)


def output_kernel(core, after, own, other, out):
    out[...] = after[pl.ds(0, out.shape[0]), :] + own[...] + other[...].astype(F32)


def input_kernel(core, value, gain, own, far, base, out):
    whole = value[...].astype(F32)
    grad = own[...] + far[...].astype(F32)
    start = base[pl.ds(0, out.shape[0]), :]
    out[...] = start + norm_back(whole, inverse_rms(whole), gain[pl.ds(0, 1), :], grad)


def gather_plain(local):
    return lax.all_gather(local, "fsdp", axis=0, tiled=True)


def scatter_plain(whole):
    return lax.psum_scatter(whole, "fsdp", scatter_dimension=0, tiled=True)


RING = (0, 2, 4, 6, 7, 5, 3, 1)
FORTH = [(RING[i], RING[(i + 1) % 8]) for i in range(8)]
BACK = [(after, before) for before, after in FORTH]


def forth(value):
    return lax.ppermute(value, "fsdp", FORTH)


def back(value):
    return lax.ppermute(value, "fsdp", BACK)


def ring_places():
    shard = lax.axis_index("fsdp")
    place = jnp.where(shard % 2 == 0, shard // 2, 7 - shard // 2)
    places = (place + jnp.array([0, -1, 1, -2, 2, -3, 3, 4], jnp.int32)) % 8
    return jnp.where(places < 4, 2 * places, 15 - 2 * places)


def vmem_call(kernel, scalars, args, out_shape, mib=10):
    return pl.pallas_call(
        kernel,
        grid_spec=pltpu.PrefetchScalarGridSpec(
            num_scalar_prefetch=1,
            grid=(1,),
            in_specs=[whole_block(arg.shape) for arg in args],
            out_specs=[whole_block(out.shape) for out in out_shape],
        ),
        out_shape=out_shape,
        compiler_params=pltpu.CompilerParams(vmem_limit_bytes=mib * 2**20),
    )(scalars, *args)


def pack_kernel(place, query, key, value, output_one, output_two, query_two, key_two, value_two, *refs):
    vectors, out = refs[:4], refs[4]
    rows, half = query.shape
    out[:, pl.ds(0, half)] = query[...].astype(BF)
    out[:, pl.ds(3 * half, half)] = jnp.where(place[0] < 2, output_one[...], output_two[...]).astype(BF)
    out[:, pl.ds(4 * half, half)] = query_two[...].astype(BF)
    for base, pair in ((1, (key, value)), (5, (key_two, value_two))):
        for part in range(half // 128):
            for turn, weight in enumerate(pair):
                lane = base * half + part * 256 + turn * 128
                out[:, pl.ds(lane, 128)] = weight[:, pl.ds(part * 128, 128)].astype(BF)
    table = jnp.concatenate([vectors[3][...], jnp.zeros((1, rows - vectors[3].shape[1]), F32)], 1)
    lines = [vector[...] for vector in vectors[:3]] + [table, jnp.zeros((4, rows), F32)]
    lines = jnp.concatenate(lines, 0).astype(BF)
    unit = lax.broadcasted_iota(jnp.int32, (8, 128), 0) == lax.broadcasted_iota(jnp.int32, (8, 128), 1)
    out[:, pl.ds(7 * half, 128)] = dot(lines, jnp.where(unit, 1.0, 0.0).astype(BF), TN).astype(BF)


def pack_halves(kernel, core, weights, vectors, rows, mib):
    half = weights[0].shape[1] // 2
    own = pl.BlockSpec((weights[0].shape[0], half), lambda i, c: (0, lax.rem(c[0], 2)))
    columns = 7 * half + 128
    return pl.pallas_call(
        kernel,
        grid_spec=pltpu.PrefetchScalarGridSpec(
            num_scalar_prefetch=1,
            grid=(1,),
            in_specs=[own] * len(weights) + [pl.BlockSpec(v.shape, lambda i, c: (0, 0)) for v in vectors],
            out_specs=pl.BlockSpec((rows, columns), lambda i, c: (0, 0)),
        ),
        out_shape=jax.ShapeDtypeStruct((rows, columns), BF),
        compiler_params=pltpu.CompilerParams(vmem_limit_bytes=mib * 2**20),
    )(core, *weights, *vectors)


def pack_feed_kernel(core, gate, up, down, out):
    rows, wide = gate.shape[0], gate.shape[1] // 2
    for place, weight in enumerate((gate, up)):
        for part in range(wide // 128):
            start = pl.multiple_of(part * 256 + core[0] * 128, 128)
            out[:, pl.ds(place * wide + part * 128, 128)] = weight[:, pl.ds(start, 128)].astype(BF)
    half = down.shape[0] // 2
    top = pl.multiple_of(core[0] * half, 16)
    own = jnp.concatenate([down[pl.ds(top, half), pl.ds(j * 128, 128)].astype(BF) for j in range(down.shape[1] // 128)], 0)
    for part in range(wide // 128):
        out[:, pl.ds(2 * wide + part * 128, 128)] = own[part * rows : (part + 1) * rows]


def unfold_down(whole, shards, width):
    rows, wide = whole.shape[0] // shards, whole.shape[1]
    count = rows * wide // width

    def kernel(_, whole, out):
        for f in range(shards):
            tall = jnp.concatenate([whole[pl.ds(f * rows, rows), pl.ds(j * 128, 128)] for j in range(wide // 128)], 0)
            for j in range(width // 128):
                out[pl.ds(f * count, count), pl.ds(j * 128, 128)] = tall[j * count : (j + 1) * count]

    return vmem_call(kernel, jnp.zeros((1,), jnp.int32), [whole], [jax.ShapeDtypeStruct((shards * count, width), whole.dtype)])[0]


def fold_down(whole, shards, wide):
    width = whole.shape[1]
    count = whole.shape[0] // shards
    rows = count * width // wide

    def kernel(_, whole, out):
        for f in range(shards):
            tall = jnp.concatenate([whole[pl.ds(f * count, count), pl.ds(j * 128, 128)] for j in range(width // 128)], 0)
            for j in range(wide // 128):
                out[pl.ds(f * rows, rows), pl.ds(j * 128, 128)] = tall[j * rows : (j + 1) * rows]

    return vmem_call(kernel, jnp.zeros((1,), jnp.int32), [whole], [jax.ShapeDtypeStruct((shards * rows, wide), whole.dtype)])[0]


def put_in_order(scalars, parts, columns, extra=0, turned=(), fold=None):
    rows = parts[0].shape[0] - extra
    skip = parts[7].shape[0]
    total = 8 * rows

    def kernel(scalars, *refs):
        parts, outs = refs[:9], list(refs[9 : 9 + len(columns)])
        sems = refs[-1]
        if fold is not None:
            outs[-1] = refs[-2]
        copies = []
        for index, part in enumerate(parts):
            place = scalars[min(index, 7)]
            offset = skip if index == 8 else 0
            count = min(part.shape[0], rows - offset)
            lane = 0
            for turn, (out, width) in enumerate(zip(outs, columns)):
                start = place * rows
                if turn in turned:
                    start = lax.rem(start + scalars[8] * (total // 2), total)
                start = pl.multiple_of(start + offset, 16)
                copies.append((part.at[pl.ds(0, count), pl.ds(lane, width)], out.at[pl.ds(start, count), :]))
                lane += width
            if extra and index != 7:
                start = pl.multiple_of(place * extra, 16)
                copies.append(
                    (part.at[pl.ds(part.shape[0] - extra, extra), pl.ds(0, 128)], refs[9 + len(columns)].at[pl.ds(start, extra), :])
                )
        copies = [pltpu.make_async_copy(x, y, sems.at[i]) for i, (x, y) in enumerate(copies)]
        for copy in copies:
            copy.start()
        for copy in copies:
            copy.wait()
        if fold is not None:
            folded, out = refs[-2], refs[8 + len(columns)]
            wide, count = columns[-1], rows * columns[-1] // fold
            for f in range(8):
                tall = jnp.concatenate([folded[pl.ds(f * rows, rows), pl.ds(j * 128, 128)] for j in range(wide // 128)], 0)
                for j in range(fold // 128):
                    out[pl.ds(f * count, count), pl.ds(j * 128, 128)] = tall[j * count : (j + 1) * count]

    out_shape = [jax.ShapeDtypeStruct((total, width), BF) for width in columns]
    scratch = []
    if fold is not None:
        out_shape[-1] = jax.ShapeDtypeStruct((total * columns[-1] // fold, fold), BF)
        scratch.append(pltpu.VMEM((total, columns[-1]), BF))
    if extra:
        out_shape.append(jax.ShapeDtypeStruct((8 * extra, 128), BF))
    return pl.pallas_call(
        kernel,
        grid_spec=pltpu.PrefetchScalarGridSpec(
            num_scalar_prefetch=1,
            grid=(),
            in_specs=[pl.BlockSpec(memory_space=pltpu.HBM)] * 9,
            out_specs=[VMEM] * len(out_shape),
            scratch_shapes=scratch + [pltpu.SemaphoreType.DMA((9 * len(columns) + 9,))],
        ),
        out_shape=out_shape,
        compiler_params=pltpu.CompilerParams(vmem_limit_bytes=4 * 2**20),
    )(scalars, *parts)


def cut_apart(scalars, columns, extras, turned=()):
    rows = columns[0].shape[0] // 8
    extra = 0 if extras is None else EXTRA
    width = sum(c.shape[1] for c in columns)
    half = (rows + extra) // 32 * 16
    counts = [rows + extra] * 7 + [half, rows + extra - half]

    def kernel(scalars, *refs):
        blocks, outs, sems = refs[: len(columns)], refs[len(refs) - 10 : -1], refs[-1]
        copies = []
        for index, out in enumerate(outs):
            place = scalars[min(index, 7)]
            skip = half if index == 8 else 0
            count = min(out.shape[0], rows - skip)
            lane = 0
            for turn, block in enumerate(blocks):
                start = place * rows
                if turn in turned:
                    start = lax.rem(start + scalars[8] * 4 * rows, 8 * rows)
                start = pl.multiple_of(start + skip, 16)
                copies.append((block.at[pl.ds(start, count), :], out.at[pl.ds(0, count), pl.ds(lane, block.shape[1])]))
                lane += block.shape[1]
            if extra and index != 7:
                start = pl.multiple_of(place * extra, 16)
                copies.append((refs[len(columns)].at[pl.ds(start, extra), :], out.at[pl.ds(count, extra), :]))
        copies = [pltpu.make_async_copy(x, y, sems.at[i]) for i, (x, y) in enumerate(copies)]
        for copy in copies:
            copy.start()
        for copy in copies:
            copy.wait()

    args = list(columns) + ([] if extras is None else [extras])
    out_shape = [jax.ShapeDtypeStruct((count, width), BF) for count in counts]
    return pl.pallas_call(
        kernel,
        grid_spec=pltpu.PrefetchScalarGridSpec(
            num_scalar_prefetch=1,
            grid=(),
            in_specs=[VMEM] * len(args),
            out_specs=[pl.BlockSpec(memory_space=pl.ANY)] * 9,
            scratch_shapes=[pltpu.SemaphoreType.DMA((9 * len(columns) + 9,))],
        ),
        out_shape=out_shape,
        compiler_params=pltpu.CompilerParams(vmem_limit_bytes=4 * 2**20),
    )(scalars, *args)


def held(value, *earlier):
    return lax.optimization_barrier((value,) + earlier)[0]


def gather_hops(local, hops):
    ahead, behind, parts = local
    for _ in range(hops):
        ahead, behind = forth(ahead), back(behind)
        parts = parts + [ahead, behind]
    return ahead, behind, parts


def gather_end(state):
    ahead, behind, parts = state
    half = ahead.shape[0] // 32 * 16
    return parts + [forth(ahead[:half]), back(behind[half:])]


def gather_last(scalars, state, columns, hold=None, **options):
    parts = gather_end(state)
    if hold is not None:
        parts[-2:] = [held(part, hold) for part in parts[-2:]]
    return put_in_order(scalars, parts, columns, **options)


def held_hops(state, hold, hops=1):
    ahead, behind = lax.optimization_barrier((state[0], state[1], hold))[:2]
    return gather_hops((ahead, behind, state[2]), hops)


def add(left, right):
    return (left.astype(F32) + right.astype(F32)).astype(left.dtype)


def add_pair(one, two, three, four):
    def kernel(one, two, three, four, left, right):
        for whole, part, out, low in ((one, two, left, False), (three, four, right, True)):
            rows, count = whole.shape[0], part.shape[0]
            start = rows - count if low else 0
            out[pl.ds(start, count), :] = add(whole[pl.ds(start, count), :], part[...])
            if count < rows:
                rest = pl.ds(count if not low else 0, rows - count)
                out[rest, :] = whole[rest, :]

    shape = jax.ShapeDtypeStruct(one.shape, one.dtype)
    return pl.pallas_call(
        kernel,
        in_specs=[VMEM] * 4,
        out_specs=[VMEM] * 2,
        out_shape=[shape, shape],
        compiler_params=pltpu.CompilerParams(vmem_limit_bytes=4 * 2**20),
        cost_estimate=pl.CostEstimate(flops=1, bytes_accessed=1, transcendentals=0),
    )(one, two, three, four)


class Scatter:
    def __init__(self, pieces):
        self.own, *self.sides, top, low = pieces
        self.ahead, self.behind = forth(top), back(low)
        self.step = 0

    def wait(self, *others):
        self.ahead, self.behind = lax.optimization_barrier((self.ahead, self.behind) + others)[:2]

    def hop(self):
        m1, p1, m2, p2, m3, p3 = self.sides
        up, down = ((p3, m3), (p2, m2), (p1, m1))[self.step]
        ahead, behind = add_pair(up, self.ahead, down, self.behind)
        self.sent = (ahead, behind)
        self.ahead, self.behind = forth(ahead), back(behind)
        self.step += 1

    def total(self):
        return (self.own.astype(F32) + self.ahead.astype(F32) + self.behind.astype(F32)).astype(BF)


def finish(core, own, other, rows, outputs, weights=(), gain=None, down=None):
    widths = [2 * 128 * len(lanes) for lanes, _, _ in outputs]

    def kernel(core, own, other, *refs):
        weights, refs = refs[: len(weights_given)], refs[len(weights_given) :]
        if gain is not None:
            gain_ref, refs = refs[0], refs[1:]
        outs = refs[: len(outputs)]
        for side, source in ((core[0], own), (1 - core[0], other)):
            for out, (lanes, core_step, block_step) in zip(outs, outputs):
                for index, lane in enumerate(lanes):
                    place = pl.multiple_of(side * core_step + index * block_step, 128)
                    out[:, pl.ds(place, 128)] = source[pl.ds(0, rows), pl.ds(lane, 128)].astype(F32)
            if down is not None:
                out = refs[len(outputs)]
                count, width = out.shape[0] // 2, out.shape[1]
                blocks = count * width // (rows * 128)
                tall = jnp.concatenate([source[:, pl.ds(down + j * 128, 128)] for j in range(blocks)], 0)
                start = pl.multiple_of(side * count, 16)
                for j in range(width // 128):
                    out[pl.ds(start, count), pl.ds(j * 128, 128)] = tall[j * count : (j + 1) * count].astype(F32)
        if gain is not None:
            total = jnp.zeros((rows, 1), F32)
            for weight, out in zip(weights, outs):
                total = total + jnp.sum(weight[...].astype(BF).astype(F32) * out[...], 1, keepdims=True)
            line = gain_ref[...].astype(BF).astype(F32)
            spot = lax.broadcasted_iota(jnp.int32, (rows, rows), 0) == lax.broadcasted_iota(jnp.int32, (rows, rows), 1)
            column = jnp.sum(jnp.where(spot, jnp.broadcast_to(line, (rows, rows)), 0.0), 1, keepdims=True)
            refs[-1][...] = jnp.broadcast_to(total / column, (rows, 128))

    weights_given = list(weights)
    args = [own, other] + weights_given + ([] if gain is None else [gain])
    out_shape = [jax.ShapeDtypeStruct((rows, width), F32) for width in widths]
    if down is not None:
        out_shape.append(jax.ShapeDtypeStruct(down_shape(rows, own.shape[1] - down), F32))
    if gain is not None:
        out_shape.append(jax.ShapeDtypeStruct((rows, 128), F32))
    return vmem_call(kernel, core, args, out_shape)


def down_shape(rows, folded):
    return 2 * folded // 8, 8 * rows


def per_device(
    decoder_input,
    memory,
    memory_lengths,
    distance_bucket,
    cotangent,
    self_gain,
    self_query,
    self_key,
    self_value,
    self_output,
    bucket_bias,
    cross_gain,
    cross_query,
    cross_key,
    cross_value,
    cross_output,
    feed_gain,
    gate_weight,
    up_weight,
    down_weight,
):
    shards = lax.axis_size("fsdp")
    rep = lax.axis_index("rep")
    side, core = rep // 2, rep % 2
    first = core == 0
    rows = decoder_input.shape[1]
    width = decoder_input.shape[2]
    slots = memory.shape[1]
    half = width // 2
    heads = half // HEAD
    shard_rows = self_query.shape[0]
    hidden_all = gate_weight.shape[1]
    hidden_rows = down_weight.shape[0]
    hidden_half = hidden_rows // 2

    which = core.reshape(1)
    cot_own = cotangent[0]
    cot_low = cot_own.astype(BF)
    cot_other = core_swap(cot_low)
    places = jnp.stack([rep, 2 * (1 - side) + core, 2 * side + 1 - core, 2 * (1 - side) + 1 - core])

    slot = (places[:, None] * slots + jnp.arange(slots, dtype=jnp.int32)[None]).reshape(-1)
    lane = jnp.arange(128, dtype=jnp.int32)[None]
    ones = jnp.where((lane >= 1) & (lane <= 3), 1.0, 0.0)
    extra_two = (jnp.where((lane == 0) & (slot >= memory_lengths[0])[:, None], NEG, 0.0) + ones).astype(BF)
    extra_one = jnp.broadcast_to(ones, (4 * rows, 128)).astype(BF)
    codes = jnp.arange(BUCKETS, dtype=jnp.int32)
    gaps = (jnp.stack([places[0], places[2]])[None, :] - places[:, None]).reshape(-1)
    starts = gaps * 256 + 768
    below = jnp.sum((distance_bucket[None, :] < codes[:, None]).astype(jnp.int32), 1)[None]
    upto = jnp.sum((distance_bucket[None, :] <= codes[:, None]).astype(jnp.int32), 1)[None]

    ringed = shards == 8 and shard_rows % 32 == 0 and hidden_half % 128 == 0
    wide = hidden_all // 2
    if ringed:
        ring = jnp.concatenate([ring_places(), which])
        gain_rows = [gain[None] for gain in (self_gain, cross_gain, feed_gain)]
        which, ring, starts, below, upto, extra_two, gain_rows, own_side = lax.optimization_barrier(
            (which, ring, starts, below, upto, extra_two, gain_rows, side == 0)
        )

        def packed(kernel, args, rows, columns):
            return vmem_call(kernel, which, args, [jax.ShapeDtypeStruct((rows, columns), BF)])[0]

        vectors = [v[None] for v in (self_gain, cross_gain, feed_gain, bucket_bias)]
        local = pack_halves(
            pack_kernel,
            rep.reshape(1),
            [self_query, self_key, self_value, self_output, cross_output, cross_query, cross_key, cross_value],
            vectors,
            shard_rows,
            60,
        )
        state = gather_hops((local, local, [local]), 1)
    x_own, m_own = decoder_input[0], memory[0]
    x_far, m_far = far_swap(x_own), far_swap(m_own)
    x_core = core_swap(x_own)
    if ringed:
        feed = packed(pack_feed_kernel, [gate_weight, up_weight, down_weight], shard_rows, 3 * wide)
        state = held_hops(state, (feed, starts, below, upto))
        state = held_hops(state, (x_far, x_core, cot_other, extra_two))
    x_diagonal = core_swap(x_far)
    if ringed:
        state = gather_end(held_hops(state, x_diagonal, 0))
        feed = held(feed, *state[-2:])
        feed = gather_hops((feed, feed, [feed]), 1)
        query_one, kv_one, out_part, query_two, kv_two, extras = put_in_order(
            ring, state, (half, 2 * half, half, half, 2 * half, 128), turned=(2,)
        )
        out_far = far_swap(out_part)
        gains, line = step(
            prepare_kernel, which, [extras, distance_bucket[None]], [((8, width), F32), ((8, 8 * rows), F32)], near=(0,)
        )
    else:

        def own_columns(weight):
            return lax.dynamic_slice_in_dim(weight, core * half, half, 1).astype(BF)

        def own_hidden(weight):
            parts = weight.reshape(shard_rows, shards, 2, hidden_half)
            own = lax.dynamic_index_in_dim(parts, core, 2, keepdims=False)
            return own.reshape(shard_rows, wide).astype(BF)

        def own_beside(left, right):
            return beside(own_columns(left), own_columns(right))

        query_one = gather_plain(own_columns(self_query))
        kv_one = gather_plain(own_beside(self_key, self_value))
        outs = [gather_plain(own_columns(w)) for w in (self_output, cross_output)]
        out_one, out_two = [jnp.where(first, w, jnp.concatenate([w[half:], w[:half]], 0)) for w in outs]
        query_two = gather_plain(own_columns(cross_query))
        kv_two = gather_plain(own_beside(cross_key, cross_value))
        gate_matrix = gather_plain(own_hidden(gate_weight))
        up_matrix = gather_plain(own_hidden(up_weight))
        down_half = lax.dynamic_slice_in_dim(down_weight, core * hidden_half, hidden_half, 0).astype(BF)
        down_matrix = gather_plain(down_half)
        gains = jnp.stack([gather_plain(g.astype(BF)).astype(F32) for g in (self_gain, cross_gain, feed_gain)])
        table = gather_plain(bucket_bias.astype(BF)).astype(F32)
        table = lax.dynamic_index_in_dim(table.reshape(2, heads, BUCKETS), core, 0, keepdims=False)
        hot = (distance_bucket[None, :] == codes[:, None]).astype(BF)
        line = jnp.einsum("hb,bd->hd", table.astype(BF), hot, preferred_element_type=F32)
        line = jnp.concatenate([jnp.full((heads, 4 * rows), NEG, F32), line], 1)
        line = jnp.pad(line, ((0, 8 - heads), (0, 0)))

    def owners(value):
        value = add(value, far_swap(value))
        return value, core_swap(value)

    pair = 2 * rows
    f32, b16 = (lambda *shape: (shape, F32)), (lambda *shape: (shape, BF))
    blocks = [x_own, x_far, x_core, x_diagonal]
    q1, k1v1, n1_t = step(
        first_kernel,
        which,
        [*blocks, gains, query_one, kv_one],
        [b16(half, pair), b16(4 * rows, 2 * half), b16(width, 4 * rows)],
        near=(5, 6),
        scratch=[pltpu.VMEM((4 * rows, width), BF)],
    )
    m_core, m_diagonal = core_swap(m_own), core_swap(m_far)
    k2v2 = project_blocks([m_own, m_far, m_core, m_diagonal], kv_two)
    if ringed:
        q1 = held(q1, k2v2, *feed[:2])
        feed = gather_hops(feed, 1)
    o1, logs_one = attend(q1, k1v1, None, line, starts)
    if ringed:
        out_far = held(out_far, o1, *feed[:2])
        out_one, out_two = jnp.where(own_side, out_part, out_far), jnp.where(own_side, out_far, out_part)
        o1 = held(o1, *feed[:2])
        feed = held_hops(feed, o1, 1)
    out_one_other, out_two_other = core_swap(out_one), core_swap(out_two)
    part, low_own, low_other = step(
        mix_kernel, which, [o1, out_one, out_one_other], [f32(pair, width), b16(rows, width), b16(rows, width)], near=(0,)
    )
    low_own, low_other = core_swap(low_other), core_swap(low_own)
    middle, n2, n2_t, q2 = step(
        functools.partial(norm_kernel, 2, 1, 1),
        which,
        [x_own, x_core, part, low_own, low_other, gains, query_two],
        [f32(pair, width), b16(pair, width), b16(width, pair), b16(half, pair)],
        near=(2, 6),
    )
    o2_a, logs_a = attend(q2, k2v2, extra_two, base=0, pairs=1, modelled=0)
    q2_b = held(q2, o2_a)
    if ringed:
        q2_b = held(q2_b, *feed[:2])
        feed = gather_end(held_hops(feed, q2_b, 0))
    o2_b, logs_b = attend(q2_b, k2v2, extra_two, base=1, pairs=heads // 2 - 1)
    if ringed:
        o2_b = held(o2_b, *feed[-2:])
        m_own = held(m_own, o2_b)
    o2, logs_two = jnp.concatenate([o2_a, o2_b], 0), jnp.concatenate([logs_a, logs_b], 0)
    (m_turned,) = step(turn_kernel, which, [m_own, m_far, m_core, m_diagonal], [b16(width, 4 * slots)], 16)
    o1_other, o2_other = core_swap(o1), core_swap(o2)
    part, low_own, low_other = step(
        mix_kernel, which, [o2, out_two, out_two_other], [f32(pair, width), b16(rows, width), b16(rows, width)], near=(0,)
    )
    if ringed:
        low_own, low_other = lax.optimization_barrier((low_own, low_other, *feed[-2:]))[:2]
    low_own, low_other = core_swap(low_other), core_swap(low_own)
    after, n3, n3_t = step(
        functools.partial(norm_kernel, 1, 0, 2),
        which,
        [middle, part, low_own, low_other, gains],
        [f32(pair, width), b16(pair, width), b16(width, pair)],
        near=(1,),
    )
    if ringed:
        feed[-2:] = [held(part, m_turned) for part in feed[-2:]]
        gate_matrix, up_matrix, down_matrix = put_in_order(ring, feed, (wide, wide, wide), fold=width)

    out_own, out_other, d_gate_up_w, d_down_w, d_n3, low_own, low_other = step(
        feed_kernel,
        which,
        [n3, n3_t, gate_matrix, up_matrix, down_matrix, cot_low, cot_other],
        [
            f32(rows, width),
            b16(rows, width),
            b16(width, 2 * wide),
            b16(wide, width),
            f32(pair, width),
            b16(rows, width),
            b16(rows, width),
        ],
        10,
        near=(0, 1, 2, 3, 4),
    )
    d_after, d_o2, d_out_two = step(
        functools.partial(back_kernel, 2, 2),
        which,
        [d_n3, core_swap(low_other), core_swap(low_own), after, gains, cot_own, cot_other, out_two, out_two_other, o2, o2_other],
        [f32(pair, width), b16(half, pair), b16(width, half)],
    )

    back_two = functools.partial(attend_back, q2, k2v2, extra_two, o2)
    if ringed:
        feed_ring = Scatter(cut_apart(ring, [d_gate_up_w, fold_down(d_down_w, shards, wide)], None))
        feed_ring.wait(d_after)
        d_o2 = held(d_o2, feed_ring.ahead, feed_ring.behind)
        feed_ring.hop()
    d_q2_a, d_kv2 = back_two(d_o2, logs_two, base=0, pairs=1)
    d_q2_b, d_kv2 = back_two(held(d_o2, d_q2_a), logs_two, base=1, pairs=1, earlier=d_kv2)
    if ringed:
        d_q2_b = held(d_q2_b, feed_ring.ahead, feed_ring.behind)
        feed_ring.wait(d_q2_b)
        feed_ring.hop()
    d_q2_c, d_kv2 = back_two(held(d_o2, d_q2_b), logs_two, base=2, pairs=heads // 2 - 2, earlier=d_kv2)
    if ringed:
        d_q2_c, d_kv2 = lax.optimization_barrier((d_q2_c, d_kv2, feed_ring.ahead, feed_ring.behind))[:2]
        feed_ring.wait(d_q2_c)
        feed_ring.hop()
        d_q2_c, d_kv2 = lax.optimization_barrier((d_q2_c, d_kv2, *feed_ring.sent))[:2]
    d_q2 = jnp.concatenate([d_q2_a, d_q2_b, d_q2_c], 0)
    part, low_own, low_other, d_query_two = step(
        query_kernel,
        which,
        [d_q2, query_two, n2_t],
        [f32(pair, width), b16(rows, width), b16(rows, width), b16(width, half)],
    )
    low_own, low_other = core_swap(low_other), core_swap(low_own)
    d_middle, d_o1, d_out_one = step(
        functools.partial(back_kernel, 1, 1),
        which,
        [part, low_own, low_other, middle, gains, d_after, out_one, out_one_other, o1, o1_other],
        [f32(pair, width), b16(half, pair), b16(width, half)],
    )
    d_mem_core = core_swap(step(memory_core_kernel, which, [d_kv2, kv_two], [b16(2 * slots, width)], near=(0,))[0])
    (d_kv_two,) = step(memory_weight_kernel, which, [m_turned, d_kv2], [b16(width, 2 * half)], near=(1,))
    d_memory, d_memory_far = step(
        memory_near_kernel, which, [d_kv2, kv_two, d_mem_core], [f32(slots, width), b16(slots, width)], near=(0,)
    )
    d_memory_far_sum = far_swap(d_memory_far)

    cross_parts = [d_query_two, d_kv_two, d_out_two, d_out_one]
    if ringed:
        pieces = list(cut_apart(ring, cross_parts, None, (2, 3)))
        pieces[-2:] = lax.optimization_barrier((*pieces[-2:], feed_ring.ahead, feed_ring.behind))[:2]
        cross_ring = Scatter(pieces)
        feed_ring.wait(d_memory_far)
        feed_own, feed_other = owners(feed_ring.total())
        d_o1 = held(d_o1, d_memory_far)
    back_one = functools.partial(attend_back, q1, k1v1, extra_one, o1)
    d_q1_a, d_kv1, d_far_a = back_one(d_o1, logs_one, line, starts, base=0, pairs=1)
    d_o1_b = held(d_o1, d_q1_a)
    if ringed:
        d_o1_b = held(d_o1_b, cross_ring.ahead, cross_ring.behind)
        cross_ring.wait(d_q1_a)
        cross_ring.hop()
    d_q1_b, d_kv1, d_far_b = back_one(d_o1_b, logs_one, line, starts, base=1, pairs=1, earlier=d_kv1)
    d_q1_c, d_kv1, d_far_c = back_one(
        held(d_o1, d_q1_b), logs_one, line, starts, base=2, pairs=heads // 2 - 2, earlier=d_kv1
    )
    if ringed:
        d_q1_c, d_kv1, d_far_c = lax.optimization_barrier((d_q1_c, d_kv1, d_far_c, cross_ring.ahead, cross_ring.behind))[:3]
        cross_ring.wait(d_q1_c)
        cross_ring.hop()
    d_q1 = jnp.concatenate([d_q1_a, d_q1_b, d_q1_c], 0)
    if ringed:
        (table_rows,) = step(
            table_kernel, (which, starts), [below, upto, d_far_a, d_far_b, d_far_c], [b16(8 * EXTRA, 3 * half)]
        )
        d_kv1 = held(d_kv1, table_rows, d_memory_far_sum)
        d_query_one, d_kv_one = step(
            first_weights_kernel, which, [d_q1, d_kv1, n1_t], [b16(width, half), b16(width, 2 * half)]
        )
        cross_ring.wait(d_q1_c)
        cross_ring.hop()
        pieces = list(cut_apart(ring, [d_query_one, d_kv_one], table_rows))
        pieces[-2:] = lax.optimization_barrier((*pieces[-2:], cross_ring.ahead, cross_ring.behind))[:2]
        self_ring = Scatter(pieces)
        self_ring.hop()
        d_q1 = held(d_q1, self_ring.ahead, self_ring.behind)
        self_ring.hop()
    out_other = core_swap(out_other)
    if ringed:
        after, d_memory = held(after, self_ring.own), held(d_memory, self_ring.own)
    (output,) = step(output_kernel, which, [after, out_own, out_other], [f32(rows, width)])
    d_memory = d_memory + d_memory_far_sum.astype(F32)
    near, low = step(
        first_back_kernel, which, [d_q1, d_kv1, query_one, kv_one], [f32(pair, width), b16(pair, width)]
    )
    low = core_swap(low)
    d_n1, d_n1_far = step(first_sum_kernel, which, [near, low], [f32(rows, width), b16(rows, width)])
    d_n1_other = far_swap(d_n1_far)
    (d_input,) = step(
        input_kernel, which, [x_own, gains, d_n1, d_n1_other, d_middle], [f32(rows, width)]
    )

    blocks = half // 128
    plain = lambda start: ([start + 128 * i for i in range(blocks)], half, 128)
    turns = lambda start: [([start + 256 * i + 128 * t for i in range(blocks)], half, 128) for t in range(2)]
    if ringed:
        self_ring.wait(d_n1_far)
        hidden = lambda start: ([start + 128 * i for i in range(wide // 128)], 128, 256)
        d_gate_out, d_up_out, d_down_out, d_gain_three = finish(
            which, feed_own, feed_other, shard_rows, [hidden(0), hidden(wide)], (gate_weight, up_weight), gain_rows[2], 2 * wide
        )
        cross_sum = cross_ring.total()
        cross_own, cross_other = owners(cross_sum)
        self_ring.wait(d_down_out, cross_sum)
        self_ring.hop()
        self_ring.wait(d_n1_other)
        d_cross = finish(
            which,
            cross_own,
            cross_other,
            shard_rows,
            [plain(0), *turns(half), plain(3 * half), plain(4 * half)],
            (cross_query,),
            gain_rows[1],
        )
        self_sum = self_ring.total()
        self_own = held(add(self_sum, far_swap(self_sum)), d_input, d_cross[0], output, d_memory)
        self_other = core_swap(self_own)
        d_self = finish(
            which,
            self_own,
            self_other,
            shard_rows,
            [plain(0), *turns(half)],
            (self_query, self_key, self_value),
            gain_rows[0],
        )
        table_own, table_other = [v[shard_rows, : shard_rows // 2].astype(F32) for v in (self_own, self_other)]
        d_gains = [d_self[3][:, 0], d_cross[5][:, 0], d_gain_three[:, 0]]
        d_output_one_out = d_cross[4]
    else:
        d_query_one, d_kv_one = step(
            first_weights_kernel, which, [d_q1, d_kv1, n1_t], [b16(width, half), b16(width, 2 * half)]
        )

        def whole(both, axis=1):
            own, other = both
            return jnp.concatenate([jnp.where(first, own, other), jnp.where(first, other, own)], axis).astype(F32)

        def plain_owners(value):
            return owners(scatter_plain(value))

        def kv_whole(both):
            pick = lambda v, turn: v.reshape(shard_rows, -1, 2, 128)[:, :, turn].reshape(shard_rows, half)
            return [whole([pick(v, turn) for v in both]) for turn in range(2)]

        def hidden_whole(both):
            both = [v.reshape(shard_rows, shards, 1, hidden_half) for v in both]
            return whole(both, 2).reshape(shard_rows, hidden_all)

        def in_order(value):
            return jnp.where(first, value, jnp.concatenate([value[half:], value[:half]], 0))

        far = (gaps[:, None] * 256 + jnp.arange(512, dtype=jnp.int32)[None] - 255).reshape(-1)
        inside = ((far[None] >= below[0][:, None]) & (far[None] < upto[0][:, None])).astype(F32)
        d_far = jnp.concatenate([d_far_a, d_far_b, d_far_c], 0).reshape(heads, -1)
        d_table = jnp.einsum("hd,bd->hb", d_far, inside, precision=lax.Precision.HIGHEST).reshape(1, -1)
        d_table = jnp.concatenate([jnp.where(first, d_table, 0.0), jnp.where(first, 0.0, d_table)], 1)
        d_table = d_table.reshape(shards, shard_rows // 2).astype(BF)

        def gain_grad(gain, *pairs):
            total = sum(jnp.sum(w.astype(BF).astype(F32) * g, 1) for w, g in pairs)
            return total / gain.astype(BF).astype(F32)

        d_gate_out, d_up_out = [hidden_whole(plain_owners(v)) for v in (d_gate_up_w[:, :wide], d_gate_up_w[:, wide:])]
        d_down_out = whole(plain_owners(d_down_w), 0)
        d_cross = [whole(plain_owners(d_query_two)), *kv_whole(plain_owners(d_kv_two))]
        d_cross.append(whole(plain_owners(in_order(d_out_two))))
        d_output_one_out = whole(plain_owners(in_order(d_out_one)))
        d_self = [whole(plain_owners(d_query_one)), *kv_whole(plain_owners(d_kv_one))]
        table_own, table_other = [v[0].astype(F32) for v in plain_owners(d_table)]
        d_gains = [
            gain_grad(self_gain, (self_query, d_self[0]), (self_key, d_self[1]), (self_value, d_self[2])),
            gain_grad(cross_gain, (cross_query, d_cross[0])),
            gain_grad(feed_gain, (gate_weight, d_gate_out), (up_weight, d_up_out)),
        ]
    d_bucket = table_own + table_other

    return (
        output[None],
        d_input[None],
        d_memory[None],
        d_gains[0],
        d_self[0],
        d_self[1],
        d_self[2],
        d_output_one_out,
        d_bucket,
        d_gains[1],
        d_cross[0],
        d_cross[1],
        d_cross[2],
        d_cross[3],
        d_gains[2],
        d_gate_out,
        d_up_out,
        d_down_out,
    )


def solution(mesh):
    split = P("fsdp", "rep", None)
    vector, matrix = P("fsdp"), P("fsdp", None)
    weights = (
        (vector,)
        + (matrix,) * 4
        + (vector, vector)
        + (matrix,) * 4
        + (vector,)
        + (matrix,) * 3
    )
    return jax.shard_map(
        per_device,
        mesh=mesh,
        in_specs=(split, split, vector, P(), split) + weights,
        out_specs=(split, split, split) + weights,
        check_vma=False,
    )
```

```python
import functools

import jax
import jax.numpy as jnp
from jax import lax
from jax.experimental import pallas as pl
from jax.experimental.pallas import tpu as pltpu
from jax.sharding import PartitionSpec as P

HEAD = 64
BUCKETS = 32
EXTRA = 16
EPS = 1e-06
NEG = -1e30
BF = jnp.bfloat16
F32 = jnp.float32
NN = (((1,), (0,)), ((), ()))
NT = (((1,), (1,)), ((), ()))
TN = (((0,), (0,)), ((), ()))
TT = (((0,), (1,)), ((), ()))

CORE = [(0, 1), (1, 0), (2, 3), (3, 2)]
FAR = [(0, 2), (2, 0), (1, 3), (3, 1)]


def core_swap(value):
    return lax.ppermute(value, "rep", CORE)


def far_swap(value):
    return lax.ppermute(value, "rep", FAR)


def dot(left, right, dims=NN):
    return lax.dot_general(left, right, dims, preferred_element_type=F32)


def half_rows(pair, head):
    row = lax.broadcasted_iota(jnp.int32, pair.shape, 0)
    keep = (row < HEAD) if head == 0 else (row >= HEAD)
    return jnp.where(keep, pair, jnp.zeros_like(pair))


def three_terms(value):
    first = value.astype(BF)
    rest = value - first.astype(F32)
    second = rest.astype(BF)
    third = (rest - second.astype(F32)).astype(BF)
    return first, second, third


def extra_rows(first_row, vector):
    terms = three_terms(-vector)
    row = lax.broadcasted_iota(jnp.int32, (128, vector.shape[1]), 0)
    out = jnp.where(row == 0, first_row, 0.0)
    for place, term in enumerate(terms):
        out = jnp.where(row == place + 1, term.astype(F32), out)
    return out.astype(BF)


def spread(line, starts, head, part, blocks, lanes):
    block = 256
    rows = []
    for j in range(blocks):
        tiles = []
        for i in range(lanes):
            start = pl.multiple_of(starts[(part * blocks + j) * lanes + i], 128)
            row = line[pl.ds(head, 1), pl.ds(start, 2 * block)]
            tile = pltpu.roll(jnp.broadcast_to(row, (block, 2 * block)), 0, 1, stride=1, stride_axis=0)
            tiles.append(tile[:, block:])
        rows.append(jnp.concatenate(tiles, 1))
    return jnp.concatenate(rows, 0)


def attend_kernel(chunk, biased, base, *refs):
    if biased:
        starts, query, keyvalue, line, mixed, log_total = refs
    else:
        query, keyvalue, extra, mixed, log_total = refs
    keys, rows = keyvalue.shape[0], query.shape[1]
    key, value = keyvalue.at[:, pl.ds(0, 128)], keyvalue.at[:, pl.ds(128, 128)]
    pair = query[...]
    row = lax.broadcasted_iota(jnp.int32, (128, rows), 0)
    one = jnp.where(row == 0, 1.0, 0.0).astype(BF)
    wide = [half_rows(pair, h) for h in range(2)]
    if not biased:
        wide = [jnp.concatenate([w, one], 0) for w in wide]

    def score(part, head):
        span = pl.ds(part * chunk, chunk)
        if not biased:
            return dot(jnp.concatenate([key[span, :], extra[span, :]], 1), wide[head])
        full = 2 * (base + pl.program_id(0)) + head
        return dot(key[span, :], wide[head]) + spread(line, starts, full, part, chunk // 256, rows // 256)

    highest = [jnp.full((1, rows), NEG, F32)] * 2
    total = [jnp.zeros((1, rows), F32)] * 2
    acc = [jnp.zeros((HEAD, rows), F32)] * 2
    steps = [(part, head) for part in range(keys // chunk) for head in range(2)]
    ahead = score(*steps[0])
    for index, (part, head) in enumerate(steps):
        scores = ahead
        if index + 1 < len(steps):
            ahead = score(*steps[index + 1])
        span = pl.ds(part * chunk, chunk)
        top = jnp.maximum(highest[head], jnp.max(scores, 0, keepdims=True))
        soft = jnp.exp(scores - top)
        scale = jnp.exp(highest[head] - top)
        total[head] = total[head] * scale + jnp.sum(soft, 0, keepdims=True)
        product = dot(value[span, :], soft.astype(BF), TN)[head * HEAD : (head + 1) * HEAD]
        acc[head] = acc[head] * scale + product
        highest[head] = top
    for head in range(2):
        mixed[pl.ds(head * HEAD, HEAD), :] = (acc[head] / total[head]).astype(BF)
        log_total[0, pl.ds(head, 1), :] = highest[head] + jnp.log(total[head])


def attend(query, keyvalue, extra, line=None, starts=None, chunk=512, base=0, pairs=None, modelled=0.3):
    rows, keys = query.shape[1], keyvalue.shape[0]
    pairs = query.shape[0] // 128 if pairs is None else pairs
    width = pairs * 128
    biased = line is not None
    in_specs = [pl.BlockSpec((128, rows), lambda p, *s: (p + base, 0)), pl.BlockSpec((keys, 256), lambda p, *s: (0, p + base))]
    out_specs = [pl.BlockSpec((128, rows), lambda p, *s: (p, 0)), pl.BlockSpec((1, 8, rows), lambda p, *s: (p, 0, 0))]
    out_shape = [jax.ShapeDtypeStruct((width, rows), BF), jax.ShapeDtypeStruct((pairs, 8, rows), F32)]
    args = [query, keyvalue]
    if biased:
        args = [starts] + args + [line]
        in_specs.append(pl.BlockSpec(line.shape, lambda p, *s: (0, 0)))
    else:
        args.append(extra)
        in_specs.append(pl.BlockSpec((keys, 128), lambda p, *s: (0, 0)))
    return pl.pallas_call(
        functools.partial(attend_kernel, chunk, biased, base),
        grid_spec=pltpu.PrefetchScalarGridSpec(
            num_scalar_prefetch=int(biased), grid=(pairs,), in_specs=in_specs, out_specs=out_specs
        ),
        out_shape=out_shape,
        compiler_params=pltpu.CompilerParams(vmem_limit_bytes=12 * 2**20),
        cost_estimate=pl.CostEstimate(flops=1, bytes_accessed=1 + int(3.7e6 * modelled), transcendentals=0),
    )(*args)


def attend_back_kernel(chunk, biased, chained, base, *refs):
    if biased:
        starts, query, keyvalue, extra, mixed, grad, log_total, line = refs[:8]
        d_query, d_keyvalue, d_far = refs[8 + chained :]
    else:
        query, keyvalue, extra, mixed, grad, log_total = refs[:6]
        d_query, d_keyvalue = refs[6 + chained :]
    keys, rows = keyvalue.shape[0], query.shape[1]
    key, value = keyvalue.at[:, pl.ds(0, 128)], keyvalue.at[:, pl.ds(128, 128)]
    pair, grad_pair = query[...], grad[...]
    product = mixed[...].astype(F32) * grad_pair.astype(F32)
    q_half = [half_rows(pair, h) for h in range(2)]
    g_half = [half_rows(grad_pair, h) for h in range(2)]
    q_wide, g_wide = [], []
    for head in range(2):
        inner = jnp.sum(product[head * HEAD : (head + 1) * HEAD], 0, keepdims=True)
        logs = log_total[0, pl.ds(head, 1), :]
        q_wide.append(jnp.concatenate([q_half[head], extra_rows(1.0, logs)], 0))
        g_wide.append(jnp.concatenate([g_half[head], extra_rows(0.0, inner)], 0))
    if biased:
        block = 256
        down = lax.broadcasted_iota(jnp.int32, (block, block), 0)
        over = lax.broadcasted_iota(jnp.int32, (block, block), 1)
        flip = jnp.where(down + over == block - 1, 1.0, 0.0).astype(BF)
    acc = [jnp.zeros((HEAD, rows), F32) for _ in range(2)]
    for part in range(keys // chunk):
        span = pl.ds(part * chunk, chunk)
        key_wide = jnp.concatenate([key[span, :], extra[span, :]], 1)
        value_wide = jnp.concatenate([value[span, :], extra[span, :]], 1)
        dv, dk = 0.0, 0.0
        for head in range(2):
            scores = dot(key_wide, q_wide[head])
            if biased:
                full = 2 * (base + pl.program_id(0)) + head
                scores = scores + spread(line, starts, full, part, chunk // 256, rows // 256)
            soft = jnp.exp(scores)
            d_scores = (soft * dot(value_wide, g_wide[head])).astype(BF)
            dv = dv + dot(soft.astype(BF), g_half[head], NT)
            dk = dk + dot(d_scores, q_half[head], NT)
            step = dot(key[span, :], d_scores, TN)[head * HEAD : (head + 1) * HEAD]
            acc[head] = acc[head] + step
            if biased:
                for j in range(chunk // block):
                    for i in range(rows // block):
                        tile = d_scores[j * block : (j + 1) * block, i * block : (i + 1) * block]
                        tile = jnp.concatenate([dot(flip, tile), jnp.zeros((block, block), F32)], 1)
                        tile = pltpu.roll(tile, 0, 1, stride=1, stride_axis=0)
                        place = (part * (chunk // block) + j) * (rows // block) + i
                        d_far[0, head, pl.ds(place, 1), :] = jnp.sum(tile, 0, keepdims=True)
        d_keyvalue[span, :] = jnp.concatenate([dk.astype(BF), dv.astype(BF)], 1)
    for head in range(2):
        d_query[pl.ds(head * HEAD, HEAD), :] = acc[head].astype(BF)


def attend_back(
    query, keyvalue, extra, mixed, grad, log_total, line=None, starts=None, chunk=512, base=0, pairs=None, earlier=None, modelled=0.3
):
    rows, keys = query.shape[1], keyvalue.shape[0]
    pairs = query.shape[0] // 128 if pairs is None else pairs
    width = pairs * 128
    biased = line is not None
    across = pl.BlockSpec((128, rows), lambda p, *s: (p + base, 0))
    along = pl.BlockSpec((keys, 256), lambda p, *s: (0, p + base))
    in_specs = [
        across,
        along,
        pl.BlockSpec((keys, 128), lambda p, *s: (0, 0)),
        across,
        across,
        pl.BlockSpec((1, 8, rows), lambda p, *s: (p + base, 0, 0)),
    ]
    args = [query, keyvalue, extra, mixed, grad, log_total]
    out_specs = [pl.BlockSpec((128, rows), lambda p, *s: (p, 0)), along]
    out_shape = [jax.ShapeDtypeStruct((width, rows), BF), jax.ShapeDtypeStruct(keyvalue.shape, BF)]
    if biased:
        in_specs.append(pl.BlockSpec(line.shape, lambda p, *s: (0, 0)))
        args = [starts] + args + [line]
        blocks = (keys // 256) * (rows // 256)
        out_specs.append(pl.BlockSpec((1, 2, blocks, 512), lambda p, *s: (p, 0, 0, 0)))
        out_shape.append(jax.ShapeDtypeStruct((pairs, 2, blocks, 512), F32))
    aliases = {}
    if earlier is not None:
        aliases = {len(args): 1}
        in_specs.append(pl.BlockSpec(memory_space=pl.ANY))
        args.append(earlier)
    return pl.pallas_call(
        functools.partial(attend_back_kernel, chunk, biased, int(earlier is not None), base),
        grid_spec=pltpu.PrefetchScalarGridSpec(
            num_scalar_prefetch=int(biased), grid=(pairs,), in_specs=in_specs, out_specs=out_specs
        ),
        out_shape=out_shape,
        input_output_aliases=aliases,
        compiler_params=pltpu.CompilerParams(vmem_limit_bytes=10 * 2**20),
        cost_estimate=pl.CostEstimate(flops=1, bytes_accessed=1 + int(3.7e6 * modelled), transcendentals=0),
    )(*args)


def project_blocks(blocks, weight):
    def kernel(*refs):
        weight, out = refs[-2:]
        row = 0
        for block in refs[:-2]:
            for part in range(block.shape[0] // blocks[0].shape[0]):
                count = blocks[0].shape[0]
                out[pl.ds(row, count), :] = dot(block[pl.ds(part * count, count), :], weight[...]).astype(BF)
                row += count

    rows = sum(block.shape[0] for block in blocks)
    return pl.pallas_call(
        kernel,
        in_specs=[pl.BlockSpec(block.shape, lambda: (0, 0)) for block in blocks] + [pl.BlockSpec(memory_space=pltpu.VMEM)],
        out_specs=pl.BlockSpec(memory_space=pltpu.VMEM),
        out_shape=jax.ShapeDtypeStruct((rows, weight.shape[1]), BF),
        compiler_params=pltpu.CompilerParams(vmem_limit_bytes=12 * 2**20),
        cost_estimate=pl.CostEstimate(flops=1, bytes_accessed=1, transcendentals=0),
    )(*blocks, weight)


def beside(left, right):
    rows, half = left.shape
    return jnp.stack([left.reshape(rows, -1, 128), right.reshape(rows, -1, 128)], 2).reshape(rows, 2 * half)


VMEM = pl.BlockSpec(memory_space=pltpu.VMEM)


def whole_block(shape):
    return pl.BlockSpec(shape, lambda *i: (0,) * len(shape), pipeline_mode=pl.Buffered(1))


def step(kernel, core, args, shapes, mib=10, near=(), scratch=()):
    scalars = core if isinstance(core, tuple) else (core,)
    return pl.pallas_call(
        kernel,
        grid_spec=pltpu.PrefetchScalarGridSpec(
            num_scalar_prefetch=len(scalars),
            grid=(1,),
            in_specs=[VMEM if i in near else whole_block(arg.shape) for i, arg in enumerate(args)],
            out_specs=[VMEM] * len(shapes),
            scratch_shapes=list(scratch),
        ),
        out_shape=[jax.ShapeDtypeStruct(shape, kind) for shape, kind in shapes],
        compiler_params=pltpu.CompilerParams(vmem_limit_bytes=mib * 2**20),
        cost_estimate=pl.CostEstimate(flops=1, bytes_accessed=1, transcendentals=0),
    )(*scalars, *args)


def inverse_rms(value):
    return lax.rsqrt(jnp.mean(value * value, -1, keepdims=True) + EPS)


def norm_back(value, inverse, gain, grad):
    scaled = grad * gain
    return inverse * (scaled - value * (inverse * inverse) * jnp.mean(scaled * value, -1, keepdims=True))


def rows_turned(ref):
    half = ref.shape[0] // 2
    return jnp.concatenate([ref[pl.ds(half, half), :], ref[pl.ds(0, half), :]], 0)


def lanes_turned(ref):
    half = ref.shape[1] // 2
    return jnp.concatenate([ref[:, pl.ds(half, half)], ref[:, pl.ds(0, half)]], 1)


def halves(core, half):
    return pl.ds(pl.multiple_of(core[0] * half, 128), half), pl.ds(pl.multiple_of((1 - core[0]) * half, 128), half)


def first_kernel(core, own, far, near, diagonal, gain, w_query, w_keyvalue, query, keyvalue, normed_t, normed):
    rows = own.shape[0]
    for place, block in enumerate((own, far, near, diagonal)):
        value = block[...].astype(F32)
        value = value * inverse_rms(value) * gain[pl.ds(0, 1), :]
        normed[pl.ds(place * rows, rows), :] = value.astype(BF)
        normed_t[:, pl.ds(place * rows, rows)] = value.T.astype(BF)
    keyvalue[...] = dot(normed[...], w_keyvalue[...]).astype(BF)
    mine = jnp.concatenate([normed[pl.ds(0, rows), :], normed[pl.ds(2 * rows, rows), :]], 0)
    query[...] = dot(mine, w_query[...]).T.astype(BF)


def prepare_kernel(core, extras, buckets, gains, line):
    count = gains.shape[1] // 8
    lines = extras[...].astype(F32).T
    gains[...] = lines[:8]
    table = jnp.concatenate([lines[3:4, f * count : f * count + count // 2] for f in range(8)], 1)
    entries = table.shape[1]
    heads = entries // BUCKETS // 2
    head = lax.broadcasted_iota(jnp.int32, (8, entries), 0)
    entry = lax.broadcasted_iota(jnp.int32, (8, entries), 1)
    first = (core[0] * heads + head) * BUCKETS
    mine = (entry >= first) & (entry < first + BUCKETS) & (head < heads)
    rows = jnp.where(mine, jnp.broadcast_to(table, (8, entries)), 0.0).astype(BF)
    length = buckets.shape[1]
    code = lax.broadcasted_iota(jnp.int32, (entries, length), 0) & (BUCKETS - 1)
    hot = jnp.where(code == buckets[...], 1.0, 0.0).astype(BF)
    line[:, pl.ds(0, length)] = jnp.full((8, length), NEG, F32)
    line[:, pl.ds(length, length)] = dot(rows, hot)


def table_kernel(core, starts, below, upto, *refs):
    parts, out = refs[:-1], refs[-1]
    heads = sum(2 * far.shape[0] for far in parts)
    total = jnp.zeros((8, BUCKETS), F32)
    for block in range(8):
        rows = [far[p, h, pl.ds(block, 1), :] for far in parts for p in range(far.shape[0]) for h in range(2)]
        rows = jnp.concatenate(rows + [jnp.zeros((8 - heads, 512), F32)], 0)
        distance = lax.broadcasted_iota(jnp.int32, (512, BUCKETS), 0) + (starts[block] - 1023)
        hot = jnp.where((distance >= below[...]) & (distance < upto[...]), 1.0, 0.0).astype(BF)
        for term in three_terms(rows):
            total = total + dot(term, hot)
    entries = 2 * heads * BUCKETS
    spot = lax.broadcasted_iota(jnp.int32, (BUCKETS, entries), 1) - lax.broadcasted_iota(jnp.int32, (BUCKETS, entries), 0)
    line = jnp.zeros((1, entries), F32)
    for head in range(heads):
        pick = jnp.where(spot == (core[0] * heads + head) * BUCKETS, 1.0, 0.0).astype(BF)
        line = line + dot(total[head : head + 1].astype(BF), pick)
    out[...] = jnp.zeros(out.shape, BF)
    count = entries // 8
    for f in range(8):
        out[pl.ds(f * EXTRA, 1), pl.ds(0, count)] = line[:, f * count : (f + 1) * count].astype(BF)


def mix_kernel(core, mixed, weight, w_theirs, part, low_own, low_other):
    half = mixed.shape[0]
    mine, theirs = halves(core, half)
    part[:, mine] = dot(mixed[...], weight[pl.ds(0, half), :], TN)
    part[:, theirs] = dot(mixed[...], w_theirs[pl.ds(half, half), :], TN)
    rows = low_own.shape[0]
    low_own[...] = part[pl.ds(0, rows), :].astype(BF)
    low_other[...] = part[pl.ds(rows, rows), :].astype(BF)


def stacked(refs):
    blocks = [ref[...].astype(F32) for ref in refs]
    return blocks[0] if len(blocks) == 1 else jnp.concatenate(blocks, 0)


def norm_kernel(parts, projected, which, core, *refs):
    base, (part, own, other, gain) = refs[:parts], refs[parts : parts + 4]
    value, normed, normed_t = refs[parts + 4 + projected : parts + 7 + projected]
    whole = stacked(base) + part[...] + stacked((own, other))
    value[...] = whole
    whole = whole * inverse_rms(whole) * gain[pl.ds(which, 1), :]
    normed[...] = whole.astype(BF)
    normed_t[...] = whole.T.astype(BF)
    if projected:
        refs[-1][...] = dot(normed[...], refs[parts + 4][...]).T.astype(BF)


def feed_kernel(core, normed, normed_t, gate, up, down, cot_own, cot_other, own, other, grads, d_down, d_normed, d_low_own, d_low_other):
    wide = gate.shape[1]
    scale, cubic = 0.7978845608028654, 0.044715
    grad_out = jnp.concatenate([cot_own[...], cot_other[...]], 0)
    total, back_total = 0.0, 0.0
    for start in range(0, wide, 256):
        span = pl.ds(start, 256)
        g = dot(normed[...], gate[:, span])
        u = dot(normed[...], up[:, span])
        square = g * g
        t = jnp.tanh(scale * (g + cubic * square * g))
        act = 0.5 * g * (1.0 + t)
        slope = 0.5 * (1.0 + t) + 0.5 * g * (1.0 - t * t) * (scale * (1.0 + 3.0 * cubic * square))
        hidden = (act * u).astype(BF)
        d_hidden = dot(grad_out, down[span, :], NT)
        d_gate = (d_hidden * u * slope).astype(BF)
        d_up = (d_hidden * act).astype(BF)
        total = total + dot(hidden, down[span, :])
        back_total = back_total + dot(d_gate, gate[:, span], NT) + dot(d_up, up[:, span], NT)
        grads[:, span] = dot(normed_t[...], d_gate).astype(BF)
        grads[:, pl.ds(wide + start, 256)] = dot(normed_t[...], d_up).astype(BF)
        d_down[span, :] = dot(hidden, grad_out, TN).astype(BF)
    rows = own.shape[0]
    own[...] = total[:rows]
    other[...] = total[rows:].astype(BF)
    d_normed[...] = back_total
    d_low_own[...] = back_total[:rows].astype(BF)
    d_low_other[...] = back_total[rows:].astype(BF)


def back_kernel(parts, which, core, *refs):
    part, own, other, value, gain = refs[:5]
    base = refs[5 : 5 + parts]
    weight, w_theirs, mixed, mixed_other = refs[5 + parts : 9 + parts]
    d_value, d_mixed, d_weight = refs[9 + parts :]
    half = weight.shape[1]
    grad = part[...] + stacked((own, other))
    whole = value[...]
    d_value[...] = stacked(base) + norm_back(whole, inverse_rms(whole), gain[pl.ds(which, 1), :], grad)
    mine, theirs = halves(core, half)
    d_mine, d_theirs = d_value[:, mine].astype(BF), d_value[:, theirs].astype(BF)
    d_mixed[...] = (dot(weight[pl.ds(0, half), :], d_mine, NT) + dot(w_theirs[pl.ds(half, half), :], d_theirs, NT)).astype(BF)
    d_weight[pl.ds(0, half), :] = dot(mixed[...], d_mine).astype(BF)
    d_weight[pl.ds(half, half), :] = dot(lanes_turned(mixed_other), d_mine).astype(BF)


def query_kernel(core, d_query, weight, normed_t, part, low_own, low_other, d_weight):
    grad = d_query[...].astype(F32).T.astype(BF)
    total = dot(grad, weight[...], NT)
    part[...] = total
    rows = low_own.shape[0]
    low_own[...] = total[:rows].astype(BF)
    low_other[...] = total[rows:].astype(BF)
    d_weight[...] = dot(normed_t[...], d_query[...], NT).astype(BF)


def memory_core_kernel(core, d_keyvalue, weight, out):
    rows = out.shape[0]
    out[...] = dot(d_keyvalue[pl.ds(rows, rows), :], weight[...], NT).astype(BF)


def memory_weight_kernel(core, memory_t, d_keyvalue, out):
    out[...] = dot(memory_t[...], d_keyvalue[...]).astype(BF)


def memory_near_kernel(core, d_keyvalue, weight, other, own, far):
    rows = own.shape[0]
    own[...] = dot(d_keyvalue[pl.ds(0, rows), :], weight[...], NT) + other[pl.ds(0, rows), :].astype(F32)
    total = dot(d_keyvalue[pl.ds(rows, rows), :], weight[...], NT) + other[pl.ds(rows, rows), :].astype(F32)
    far[...] = total.astype(BF)


def turn_kernel(core, *refs):
    blocks, out = refs[:-1], refs[-1]
    for place, block in enumerate(blocks):
        rows = block.shape[0]
        out[:, pl.ds(place * rows, rows)] = block[...].astype(F32).T.astype(BF)


def first_weights_kernel(core, d_query, d_keyvalue, normed_t, d_w_query, d_w_keyvalue):
    rows = d_query.shape[1] // 2
    d_w_query[...] = (
        dot(normed_t[:, pl.ds(0, rows)], d_query[:, pl.ds(0, rows)], NT)
        + dot(normed_t[:, pl.ds(2 * rows, rows)], d_query[:, pl.ds(rows, rows)], NT)
    ).astype(BF)
    d_w_keyvalue[...] = dot(normed_t[...], d_keyvalue[...]).astype(BF)


def first_back_kernel(core, d_query, d_keyvalue, w_query, w_keyvalue, near, low):
    rows = d_query.shape[1] // 2
    grad = d_query[...].astype(F32).T.astype(BF)
    near[...] = dot(d_keyvalue[pl.ds(0, 2 * rows), :], w_keyvalue[...], NT)
    near[pl.ds(0, rows), :] += dot(grad[:rows], w_query[...], NT)
    total = dot(d_keyvalue[pl.ds(2 * rows, 2 * rows), :], w_keyvalue[...], NT)
    low[pl.ds(0, rows), :] = (total[:rows] + dot(grad[rows:], w_query[...], NT)).astype(BF)
    low[pl.ds(rows, rows), :] = total[rows:].astype(BF)


def first_sum_kernel(core, near, other, own, far):
    rows = own.shape[0]
    own[...] = near[pl.ds(0, rows), :] + other[pl.ds(0, rows), :].astype(F32)
    far[...] = (near[pl.ds(rows, rows), :] + other[pl.ds(rows, rows), :].astype(F32)).astype(BF)


def output_kernel(core, after, own, other, out):
    out[...] = after[pl.ds(0, out.shape[0]), :] + own[...] + other[...].astype(F32)


def input_kernel(core, value, gain, own, far, base, out):
    whole = value[...].astype(F32)
    grad = own[...] + far[...].astype(F32)
    start = base[pl.ds(0, out.shape[0]), :]
    out[...] = start + norm_back(whole, inverse_rms(whole), gain[pl.ds(0, 1), :], grad)


def gather_plain(local):
    return lax.all_gather(local, "fsdp", axis=0, tiled=True)


def scatter_plain(whole):
    return lax.psum_scatter(whole, "fsdp", scatter_dimension=0, tiled=True)


RING = (0, 2, 4, 6, 7, 5, 3, 1)
FORTH = [(RING[i], RING[(i + 1) % 8]) for i in range(8)]
BACK = [(after, before) for before, after in FORTH]


def forth(value):
    return lax.ppermute(value, "fsdp", FORTH)


def back(value):
    return lax.ppermute(value, "fsdp", BACK)


def ring_places():
    shard = lax.axis_index("fsdp")
    place = jnp.where(shard % 2 == 0, shard // 2, 7 - shard // 2)
    places = (place + jnp.array([0, -1, 1, -2, 2, -3, 3, 4], jnp.int32)) % 8
    return jnp.where(places < 4, 2 * places, 15 - 2 * places)


def vmem_call(kernel, scalars, args, out_shape, mib=10):
    return pl.pallas_call(
        kernel,
        grid_spec=pltpu.PrefetchScalarGridSpec(
            num_scalar_prefetch=1,
            grid=(1,),
            in_specs=[whole_block(arg.shape) for arg in args],
            out_specs=[whole_block(out.shape) for out in out_shape],
        ),
        out_shape=out_shape,
        compiler_params=pltpu.CompilerParams(vmem_limit_bytes=mib * 2**20),
    )(scalars, *args)


def pack_kernel(place, query, key, value, output_one, output_two, query_two, key_two, value_two, *refs):
    vectors, out = refs[:4], refs[4]
    rows, half = query.shape
    out[:, pl.ds(0, half)] = query[...].astype(BF)
    out[:, pl.ds(3 * half, half)] = jnp.where(place[0] < 2, output_one[...], output_two[...]).astype(BF)
    out[:, pl.ds(4 * half, half)] = query_two[...].astype(BF)
    for base, pair in ((1, (key, value)), (5, (key_two, value_two))):
        for part in range(half // 128):
            for turn, weight in enumerate(pair):
                lane = base * half + part * 256 + turn * 128
                out[:, pl.ds(lane, 128)] = weight[:, pl.ds(part * 128, 128)].astype(BF)
    table = jnp.concatenate([vectors[3][...], jnp.zeros((1, rows - vectors[3].shape[1]), F32)], 1)
    lines = [vector[...] for vector in vectors[:3]] + [table, jnp.zeros((4, rows), F32)]
    lines = jnp.concatenate(lines, 0).astype(BF)
    unit = lax.broadcasted_iota(jnp.int32, (8, 128), 0) == lax.broadcasted_iota(jnp.int32, (8, 128), 1)
    out[:, pl.ds(7 * half, 128)] = dot(lines, jnp.where(unit, 1.0, 0.0).astype(BF), TN).astype(BF)


def pack_halves(kernel, core, weights, vectors, rows, mib):
    half = weights[0].shape[1] // 2
    own = pl.BlockSpec((weights[0].shape[0], half), lambda i, c: (0, lax.rem(c[0], 2)))
    columns = 7 * half + 128
    return pl.pallas_call(
        kernel,
        grid_spec=pltpu.PrefetchScalarGridSpec(
            num_scalar_prefetch=1,
            grid=(1,),
            in_specs=[own] * len(weights) + [pl.BlockSpec(v.shape, lambda i, c: (0, 0)) for v in vectors],
            out_specs=pl.BlockSpec((rows, columns), lambda i, c: (0, 0)),
        ),
        out_shape=jax.ShapeDtypeStruct((rows, columns), BF),
        compiler_params=pltpu.CompilerParams(vmem_limit_bytes=mib * 2**20),
    )(core, *weights, *vectors)


def pack_feed_kernel(core, gate, up, down, out):
    rows, wide = gate.shape[0], gate.shape[1] // 2
    for place, weight in enumerate((gate, up)):
        for part in range(wide // 128):
            start = pl.multiple_of(part * 256 + core[0] * 128, 128)
            out[:, pl.ds(place * wide + part * 128, 128)] = weight[:, pl.ds(start, 128)].astype(BF)
    half = down.shape[0] // 2
    top = pl.multiple_of(core[0] * half, 16)
    own = jnp.concatenate([down[pl.ds(top, half), pl.ds(j * 128, 128)].astype(BF) for j in range(down.shape[1] // 128)], 0)
    for part in range(wide // 128):
        out[:, pl.ds(2 * wide + part * 128, 128)] = own[part * rows : (part + 1) * rows]


def unfold_down(whole, shards, width):
    rows, wide = whole.shape[0] // shards, whole.shape[1]
    count = rows * wide // width

    def kernel(_, whole, out):
        for f in range(shards):
            tall = jnp.concatenate([whole[pl.ds(f * rows, rows), pl.ds(j * 128, 128)] for j in range(wide // 128)], 0)
            for j in range(width // 128):
                out[pl.ds(f * count, count), pl.ds(j * 128, 128)] = tall[j * count : (j + 1) * count]

    return vmem_call(kernel, jnp.zeros((1,), jnp.int32), [whole], [jax.ShapeDtypeStruct((shards * count, width), whole.dtype)])[0]


def fold_down(whole, shards, wide):
    width = whole.shape[1]
    count = whole.shape[0] // shards
    rows = count * width // wide

    def kernel(_, whole, out):
        for f in range(shards):
            tall = jnp.concatenate([whole[pl.ds(f * count, count), pl.ds(j * 128, 128)] for j in range(width // 128)], 0)
            for j in range(wide // 128):
                out[pl.ds(f * rows, rows), pl.ds(j * 128, 128)] = tall[j * rows : (j + 1) * rows]

    return vmem_call(kernel, jnp.zeros((1,), jnp.int32), [whole], [jax.ShapeDtypeStruct((shards * rows, wide), whole.dtype)])[0]


def put_in_order(scalars, parts, columns, extra=0, turned=(), fold=None):
    rows = parts[0].shape[0] - extra
    skip = parts[7].shape[0]
    total = 8 * rows

    def kernel(scalars, *refs):
        parts, outs = refs[:9], list(refs[9 : 9 + len(columns)])
        sems = refs[-1]
        if fold is not None:
            outs[-1] = refs[-2]
        copies = []
        for index, part in enumerate(parts):
            place = scalars[min(index, 7)]
            offset = skip if index == 8 else 0
            count = min(part.shape[0], rows - offset)
            lane = 0
            for turn, (out, width) in enumerate(zip(outs, columns)):
                start = place * rows
                if turn in turned:
                    start = lax.rem(start + scalars[8] * (total // 2), total)
                start = pl.multiple_of(start + offset, 16)
                copies.append((part.at[pl.ds(0, count), pl.ds(lane, width)], out.at[pl.ds(start, count), :]))
                lane += width
            if extra and index != 7:
                start = pl.multiple_of(place * extra, 16)
                copies.append(
                    (part.at[pl.ds(part.shape[0] - extra, extra), pl.ds(0, 128)], refs[9 + len(columns)].at[pl.ds(start, extra), :])
                )
        copies = [pltpu.make_async_copy(x, y, sems.at[i]) for i, (x, y) in enumerate(copies)]
        for copy in copies:
            copy.start()
        for copy in copies:
            copy.wait()
        if fold is not None:
            folded, out = refs[-2], refs[8 + len(columns)]
            wide, count = columns[-1], rows * columns[-1] // fold
            for f in range(8):
                tall = jnp.concatenate([folded[pl.ds(f * rows, rows), pl.ds(j * 128, 128)] for j in range(wide // 128)], 0)
                for j in range(fold // 128):
                    out[pl.ds(f * count, count), pl.ds(j * 128, 128)] = tall[j * count : (j + 1) * count]

    out_shape = [jax.ShapeDtypeStruct((total, width), BF) for width in columns]
    scratch = []
    if fold is not None:
        out_shape[-1] = jax.ShapeDtypeStruct((total * columns[-1] // fold, fold), BF)
        scratch.append(pltpu.VMEM((total, columns[-1]), BF))
    if extra:
        out_shape.append(jax.ShapeDtypeStruct((8 * extra, 128), BF))
    return pl.pallas_call(
        kernel,
        grid_spec=pltpu.PrefetchScalarGridSpec(
            num_scalar_prefetch=1,
            grid=(),
            in_specs=[pl.BlockSpec(memory_space=pltpu.HBM)] * 9,
            out_specs=[VMEM] * len(out_shape),
            scratch_shapes=scratch + [pltpu.SemaphoreType.DMA((9 * len(columns) + 9,))],
        ),
        out_shape=out_shape,
        compiler_params=pltpu.CompilerParams(vmem_limit_bytes=4 * 2**20),
    )(scalars, *parts)


def cut_apart(scalars, columns, extras, turned=()):
    rows = columns[0].shape[0] // 8
    extra = 0 if extras is None else EXTRA
    width = sum(c.shape[1] for c in columns)
    half = (rows + extra) // 32 * 16
    counts = [rows + extra] * 7 + [half, rows + extra - half]

    def kernel(scalars, *refs):
        blocks, outs, sems = refs[: len(columns)], refs[len(refs) - 10 : -1], refs[-1]
        copies = []
        for index, out in enumerate(outs):
            place = scalars[min(index, 7)]
            skip = half if index == 8 else 0
            count = min(out.shape[0], rows - skip)
            lane = 0
            for turn, block in enumerate(blocks):
                start = place * rows
                if turn in turned:
                    start = lax.rem(start + scalars[8] * 4 * rows, 8 * rows)
                start = pl.multiple_of(start + skip, 16)
                copies.append((block.at[pl.ds(start, count), :], out.at[pl.ds(0, count), pl.ds(lane, block.shape[1])]))
                lane += block.shape[1]
            if extra and index != 7:
                start = pl.multiple_of(place * extra, 16)
                copies.append((refs[len(columns)].at[pl.ds(start, extra), :], out.at[pl.ds(count, extra), :]))
        copies = [pltpu.make_async_copy(x, y, sems.at[i]) for i, (x, y) in enumerate(copies)]
        for copy in copies:
            copy.start()
        for copy in copies:
            copy.wait()

    args = list(columns) + ([] if extras is None else [extras])
    out_shape = [jax.ShapeDtypeStruct((count, width), BF) for count in counts]
    return pl.pallas_call(
        kernel,
        grid_spec=pltpu.PrefetchScalarGridSpec(
            num_scalar_prefetch=1,
            grid=(),
            in_specs=[VMEM] * len(args),
            out_specs=[pl.BlockSpec(memory_space=pl.ANY)] * 9,
            scratch_shapes=[pltpu.SemaphoreType.DMA((9 * len(columns) + 9,))],
        ),
        out_shape=out_shape,
        compiler_params=pltpu.CompilerParams(vmem_limit_bytes=4 * 2**20),
    )(scalars, *args)


def held(value, *earlier):
    return lax.optimization_barrier((value,) + earlier)[0]


def gather_hops(local, hops):
    ahead, behind, parts = local
    for _ in range(hops):
        ahead, behind = forth(ahead), back(behind)
        parts = parts + [ahead, behind]
    return ahead, behind, parts


def gather_end(state):
    ahead, behind, parts = state
    half = ahead.shape[0] // 32 * 16
    return parts + [forth(ahead[:half]), back(behind[half:])]


def gather_last(scalars, state, columns, hold=None, **options):
    parts = gather_end(state)
    if hold is not None:
        parts[-2:] = [held(part, hold) for part in parts[-2:]]
    return put_in_order(scalars, parts, columns, **options)


def held_hops(state, hold, hops=1):
    ahead, behind = lax.optimization_barrier((state[0], state[1], hold))[:2]
    return gather_hops((ahead, behind, state[2]), hops)


def add(left, right):
    return (left.astype(F32) + right.astype(F32)).astype(left.dtype)


def add_pair(one, two, three, four):
    def kernel(one, two, three, four, left, right):
        for whole, part, out, low in ((one, two, left, False), (three, four, right, True)):
            rows, count = whole.shape[0], part.shape[0]
            start = rows - count if low else 0
            out[pl.ds(start, count), :] = add(whole[pl.ds(start, count), :], part[...])
            if count < rows:
                rest = pl.ds(count if not low else 0, rows - count)
                out[rest, :] = whole[rest, :]

    shape = jax.ShapeDtypeStruct(one.shape, one.dtype)
    return pl.pallas_call(
        kernel,
        in_specs=[VMEM] * 4,
        out_specs=[VMEM] * 2,
        out_shape=[shape, shape],
        compiler_params=pltpu.CompilerParams(vmem_limit_bytes=4 * 2**20),
        cost_estimate=pl.CostEstimate(flops=1, bytes_accessed=1, transcendentals=0),
    )(one, two, three, four)


class Scatter:
    def __init__(self, pieces):
        self.own, *self.sides, top, low = pieces
        self.ahead, self.behind = forth(top), back(low)
        self.step = 0

    def wait(self, *others):
        self.ahead, self.behind = lax.optimization_barrier((self.ahead, self.behind) + others)[:2]

    def hop(self):
        m1, p1, m2, p2, m3, p3 = self.sides
        up, down = ((p3, m3), (p2, m2), (p1, m1))[self.step]
        ahead, behind = add_pair(up, self.ahead, down, self.behind)
        self.sent = (ahead, behind)
        self.ahead, self.behind = forth(ahead), back(behind)
        self.step += 1

    def total(self):
        return (self.own.astype(F32) + self.ahead.astype(F32) + self.behind.astype(F32)).astype(BF)


def finish(core, own, other, rows, outputs, weights=(), gain=None, down=None):
    widths = [2 * 128 * len(lanes) for lanes, _, _ in outputs]

    def kernel(core, own, other, *refs):
        weights, refs = refs[: len(weights_given)], refs[len(weights_given) :]
        if gain is not None:
            gain_ref, refs = refs[0], refs[1:]
        outs = refs[: len(outputs)]
        for side, source in ((core[0], own), (1 - core[0], other)):
            for out, (lanes, core_step, block_step) in zip(outs, outputs):
                for index, lane in enumerate(lanes):
                    place = pl.multiple_of(side * core_step + index * block_step, 128)
                    out[:, pl.ds(place, 128)] = source[pl.ds(0, rows), pl.ds(lane, 128)].astype(F32)
            if down is not None:
                out = refs[len(outputs)]
                count, width = out.shape[0] // 2, out.shape[1]
                blocks = count * width // (rows * 128)
                tall = jnp.concatenate([source[:, pl.ds(down + j * 128, 128)] for j in range(blocks)], 0)
                start = pl.multiple_of(side * count, 16)
                for j in range(width // 128):
                    out[pl.ds(start, count), pl.ds(j * 128, 128)] = tall[j * count : (j + 1) * count].astype(F32)
        if gain is not None:
            total = jnp.zeros((rows, 1), F32)
            for weight, out in zip(weights, outs):
                total = total + jnp.sum(weight[...].astype(BF).astype(F32) * out[...], 1, keepdims=True)
            line = gain_ref[...].astype(BF).astype(F32)
            spot = lax.broadcasted_iota(jnp.int32, (rows, rows), 0) == lax.broadcasted_iota(jnp.int32, (rows, rows), 1)
            column = jnp.sum(jnp.where(spot, jnp.broadcast_to(line, (rows, rows)), 0.0), 1, keepdims=True)
            refs[-1][...] = jnp.broadcast_to(total / column, (rows, 128))

    weights_given = list(weights)
    args = [own, other] + weights_given + ([] if gain is None else [gain])
    out_shape = [jax.ShapeDtypeStruct((rows, width), F32) for width in widths]
    if down is not None:
        out_shape.append(jax.ShapeDtypeStruct(down_shape(rows, own.shape[1] - down), F32))
    if gain is not None:
        out_shape.append(jax.ShapeDtypeStruct((rows, 128), F32))
    return vmem_call(kernel, core, args, out_shape)


def down_shape(rows, folded):
    return 2 * folded // 8, 8 * rows


def per_device(
    decoder_input,
    memory,
    memory_lengths,
    distance_bucket,
    cotangent,
    self_gain,
    self_query,
    self_key,
    self_value,
    self_output,
    bucket_bias,
    cross_gain,
    cross_query,
    cross_key,
    cross_value,
    cross_output,
    feed_gain,
    gate_weight,
    up_weight,
    down_weight,
):
    shards = lax.axis_size("fsdp")
    rep = lax.axis_index("rep")
    side, core = rep // 2, rep % 2
    first = core == 0
    rows = decoder_input.shape[1]
    width = decoder_input.shape[2]
    slots = memory.shape[1]
    half = width // 2
    heads = half // HEAD
    shard_rows = self_query.shape[0]
    hidden_all = gate_weight.shape[1]
    hidden_rows = down_weight.shape[0]
    hidden_half = hidden_rows // 2

    which = core.reshape(1)
    cot_own = cotangent[0]
    cot_low = cot_own.astype(BF)
    cot_other = core_swap(cot_low)
    places = jnp.stack([rep, 2 * (1 - side) + core, 2 * side + 1 - core, 2 * (1 - side) + 1 - core])

    slot = (places[:, None] * slots + jnp.arange(slots, dtype=jnp.int32)[None]).reshape(-1)
    lane = jnp.arange(128, dtype=jnp.int32)[None]
    ones = jnp.where((lane >= 1) & (lane <= 3), 1.0, 0.0)
    extra_two = (jnp.where((lane == 0) & (slot >= memory_lengths[0])[:, None], NEG, 0.0) + ones).astype(BF)
    extra_one = jnp.broadcast_to(ones, (4 * rows, 128)).astype(BF)
    codes = jnp.arange(BUCKETS, dtype=jnp.int32)
    gaps = (jnp.stack([places[0], places[2]])[None, :] - places[:, None]).reshape(-1)
    starts = gaps * 256 + 768
    below = jnp.sum((distance_bucket[None, :] < codes[:, None]).astype(jnp.int32), 1)[None]
    upto = jnp.sum((distance_bucket[None, :] <= codes[:, None]).astype(jnp.int32), 1)[None]

    ringed = shards == 8 and shard_rows % 32 == 0 and hidden_half % 128 == 0
    wide = hidden_all // 2
    if ringed:
        ring = jnp.concatenate([ring_places(), which])
        gain_rows = [gain[None] for gain in (self_gain, cross_gain, feed_gain)]
        which, ring, starts, below, upto, extra_two, gain_rows, own_side = lax.optimization_barrier(
            (which, ring, starts, below, upto, extra_two, gain_rows, side == 0)
        )

        def packed(kernel, args, rows, columns):
            return vmem_call(kernel, which, args, [jax.ShapeDtypeStruct((rows, columns), BF)])[0]

        vectors = [v[None] for v in (self_gain, cross_gain, feed_gain, bucket_bias)]
        local = pack_halves(
            pack_kernel,
            rep.reshape(1),
            [self_query, self_key, self_value, self_output, cross_output, cross_query, cross_key, cross_value],
            vectors,
            shard_rows,
            60,
        )
        state = gather_hops((local, local, [local]), 1)
    x_own, m_own = decoder_input[0], memory[0]
    x_far, m_far = far_swap(x_own), far_swap(m_own)
    x_core = core_swap(x_own)
    if ringed:
        feed = packed(pack_feed_kernel, [gate_weight, up_weight, down_weight], shard_rows, 3 * wide)
        state = held_hops(state, (feed, starts, below, upto))
        state = held_hops(state, (x_far, x_core, cot_other, extra_two))
    x_diagonal = core_swap(x_far)
    if ringed:
        state = gather_end(held_hops(state, x_diagonal, 0))
        feed = held(feed, *state[-2:])
        feed = gather_hops((feed, feed, [feed]), 1)
        query_one, kv_one, out_part, query_two, kv_two, extras = put_in_order(
            ring, state, (half, 2 * half, half, half, 2 * half, 128), turned=(2,)
        )
        out_far = far_swap(out_part)
        gains, line = step(
            prepare_kernel, which, [extras, distance_bucket[None]], [((8, width), F32), ((8, 8 * rows), F32)], near=(0,)
        )
    else:

        def own_columns(weight):
            return lax.dynamic_slice_in_dim(weight, core * half, half, 1).astype(BF)

        def own_hidden(weight):
            parts = weight.reshape(shard_rows, shards, 2, hidden_half)
            own = lax.dynamic_index_in_dim(parts, core, 2, keepdims=False)
            return own.reshape(shard_rows, wide).astype(BF)

        def own_beside(left, right):
            return beside(own_columns(left), own_columns(right))

        query_one = gather_plain(own_columns(self_query))
        kv_one = gather_plain(own_beside(self_key, self_value))
        outs = [gather_plain(own_columns(w)) for w in (self_output, cross_output)]
        out_one, out_two = [jnp.where(first, w, jnp.concatenate([w[half:], w[:half]], 0)) for w in outs]
        query_two = gather_plain(own_columns(cross_query))
        kv_two = gather_plain(own_beside(cross_key, cross_value))
        gate_matrix = gather_plain(own_hidden(gate_weight))
        up_matrix = gather_plain(own_hidden(up_weight))
        down_half = lax.dynamic_slice_in_dim(down_weight, core * hidden_half, hidden_half, 0).astype(BF)
        down_matrix = gather_plain(down_half)
        gains = jnp.stack([gather_plain(g.astype(BF)).astype(F32) for g in (self_gain, cross_gain, feed_gain)])
        table = gather_plain(bucket_bias.astype(BF)).astype(F32)
        table = lax.dynamic_index_in_dim(table.reshape(2, heads, BUCKETS), core, 0, keepdims=False)
        hot = (distance_bucket[None, :] == codes[:, None]).astype(BF)
        line = jnp.einsum("hb,bd->hd", table.astype(BF), hot, preferred_element_type=F32)
        line = jnp.concatenate([jnp.full((heads, 4 * rows), NEG, F32), line], 1)
        line = jnp.pad(line, ((0, 8 - heads), (0, 0)))

    def owners(value):
        value = add(value, far_swap(value))
        return value, core_swap(value)

    pair = 2 * rows
    f32, b16 = (lambda *shape: (shape, F32)), (lambda *shape: (shape, BF))
    blocks = [x_own, x_far, x_core, x_diagonal]
    q1, k1v1, n1_t = step(
        first_kernel,
        which,
        [*blocks, gains, query_one, kv_one],
        [b16(half, pair), b16(4 * rows, 2 * half), b16(width, 4 * rows)],
        near=(5, 6),
        scratch=[pltpu.VMEM((4 * rows, width), BF)],
    )
    m_core, m_diagonal = core_swap(m_own), core_swap(m_far)
    k2v2 = project_blocks([m_own, m_far, m_core, m_diagonal], kv_two)
    if ringed:
        q1 = held(q1, k2v2, *feed[:2])
        feed = gather_hops(feed, 1)
    o1, logs_one = attend(q1, k1v1, None, line, starts)
    if ringed:
        out_far = held(out_far, o1, *feed[:2])
        out_one, out_two = jnp.where(own_side, out_part, out_far), jnp.where(own_side, out_far, out_part)
        o1 = held(o1, *feed[:2])
        feed = held_hops(feed, o1, 1)
    out_one_other, out_two_other = core_swap(out_one), core_swap(out_two)
    part, low_own, low_other = step(
        mix_kernel, which, [o1, out_one, out_one_other], [f32(pair, width), b16(rows, width), b16(rows, width)], near=(0,)
    )
    low_own, low_other = core_swap(low_other), core_swap(low_own)
    middle, n2, n2_t, q2 = step(
        functools.partial(norm_kernel, 2, 1, 1),
        which,
        [x_own, x_core, part, low_own, low_other, gains, query_two],
        [f32(pair, width), b16(pair, width), b16(width, pair), b16(half, pair)],
        near=(2, 6),
    )
    o2_a, logs_a = attend(q2, k2v2, extra_two, base=0, pairs=1, modelled=0)
    q2_b = held(q2, o2_a)
    if ringed:
        q2_b = held(q2_b, *feed[:2])
        feed = gather_end(held_hops(feed, q2_b, 0))
    o2_b, logs_b = attend(q2_b, k2v2, extra_two, base=1, pairs=heads // 2 - 1)
    if ringed:
        o2_b = held(o2_b, *feed[-2:])
        m_own = held(m_own, o2_b)
    o2, logs_two = jnp.concatenate([o2_a, o2_b], 0), jnp.concatenate([logs_a, logs_b], 0)
    (m_turned,) = step(turn_kernel, which, [m_own, m_far, m_core, m_diagonal], [b16(width, 4 * slots)], 16)
    o1_other, o2_other = core_swap(o1), core_swap(o2)
    part, low_own, low_other = step(
        mix_kernel, which, [o2, out_two, out_two_other], [f32(pair, width), b16(rows, width), b16(rows, width)], near=(0,)
    )
    if ringed:
        low_own, low_other = lax.optimization_barrier((low_own, low_other, *feed[-2:]))[:2]
    low_own, low_other = core_swap(low_other), core_swap(low_own)
    after, n3, n3_t = step(
        functools.partial(norm_kernel, 1, 0, 2),
        which,
        [middle, part, low_own, low_other, gains],
        [f32(pair, width), b16(pair, width), b16(width, pair)],
        near=(1,),
    )
    if ringed:
        feed[-2:] = [held(part, m_turned) for part in feed[-2:]]
        gate_matrix, up_matrix, down_matrix = put_in_order(ring, feed, (wide, wide, wide), fold=width)

    out_own, out_other, d_gate_up_w, d_down_w, d_n3, low_own, low_other = step(
        feed_kernel,
        which,
        [n3, n3_t, gate_matrix, up_matrix, down_matrix, cot_low, cot_other],
        [
            f32(rows, width),
            b16(rows, width),
            b16(width, 2 * wide),
            b16(wide, width),
            f32(pair, width),
            b16(rows, width),
            b16(rows, width),
        ],
        10,
        near=(0, 1, 2, 3, 4),
    )
    d_after, d_o2, d_out_two = step(
        functools.partial(back_kernel, 2, 2),
        which,
        [d_n3, core_swap(low_other), core_swap(low_own), after, gains, cot_own, cot_other, out_two, out_two_other, o2, o2_other],
        [f32(pair, width), b16(half, pair), b16(width, half)],
    )

    back_two = functools.partial(attend_back, q2, k2v2, extra_two, o2)
    if ringed:
        feed_ring = Scatter(cut_apart(ring, [d_gate_up_w, fold_down(d_down_w, shards, wide)], None))
        feed_ring.wait(d_after)
        d_o2 = held(d_o2, feed_ring.ahead, feed_ring.behind)
        feed_ring.hop()
    d_q2_a, d_kv2 = back_two(d_o2, logs_two, base=0, pairs=1)
    d_q2_b, d_kv2 = back_two(held(d_o2, d_q2_a), logs_two, base=1, pairs=1, earlier=d_kv2)
    if ringed:
        d_q2_b = held(d_q2_b, feed_ring.ahead, feed_ring.behind)
        feed_ring.wait(d_q2_b)
        feed_ring.hop()
    d_q2_c, d_kv2 = back_two(held(d_o2, d_q2_b), logs_two, base=2, pairs=heads // 2 - 2, earlier=d_kv2)
    if ringed:
        d_q2_c, d_kv2 = lax.optimization_barrier((d_q2_c, d_kv2, feed_ring.ahead, feed_ring.behind))[:2]
        feed_ring.wait(d_q2_c)
        feed_ring.hop()
        d_q2_c, d_kv2 = lax.optimization_barrier((d_q2_c, d_kv2, *feed_ring.sent))[:2]
    d_q2 = jnp.concatenate([d_q2_a, d_q2_b, d_q2_c], 0)
    part, low_own, low_other, d_query_two = step(
        query_kernel,
        which,
        [d_q2, query_two, n2_t],
        [f32(pair, width), b16(rows, width), b16(rows, width), b16(width, half)],
    )
    low_own, low_other = core_swap(low_other), core_swap(low_own)
    d_middle, d_o1, d_out_one = step(
        functools.partial(back_kernel, 1, 1),
        which,
        [part, low_own, low_other, middle, gains, d_after, out_one, out_one_other, o1, o1_other],
        [f32(pair, width), b16(half, pair), b16(width, half)],
    )
    d_mem_core = core_swap(step(memory_core_kernel, which, [d_kv2, kv_two], [b16(2 * slots, width)], near=(0,))[0])
    (d_kv_two,) = step(memory_weight_kernel, which, [m_turned, d_kv2], [b16(width, 2 * half)], near=(1,))
    d_memory, d_memory_far = step(
        memory_near_kernel, which, [d_kv2, kv_two, d_mem_core], [f32(slots, width), b16(slots, width)], near=(0,)
    )
    d_memory_far_sum = far_swap(d_memory_far)

    cross_parts = [d_query_two, d_kv_two, d_out_two, d_out_one]
    if ringed:
        pieces = list(cut_apart(ring, cross_parts, None, (2, 3)))
        pieces[-2:] = lax.optimization_barrier((*pieces[-2:], feed_ring.ahead, feed_ring.behind))[:2]
        cross_ring = Scatter(pieces)
        feed_ring.wait(d_memory_far)
        feed_own, feed_other = owners(feed_ring.total())
        d_o1 = held(d_o1, d_memory_far)
    back_one = functools.partial(attend_back, q1, k1v1, extra_one, o1)
    d_q1_a, d_kv1, d_far_a = back_one(d_o1, logs_one, line, starts, base=0, pairs=1)
    d_o1_b = held(d_o1, d_q1_a)
    if ringed:
        d_o1_b = held(d_o1_b, cross_ring.ahead, cross_ring.behind)
        cross_ring.wait(d_q1_a)
        cross_ring.hop()
    d_q1_b, d_kv1, d_far_b = back_one(d_o1_b, logs_one, line, starts, base=1, pairs=1, earlier=d_kv1)
    d_q1_c, d_kv1, d_far_c = back_one(
        held(d_o1, d_q1_b), logs_one, line, starts, base=2, pairs=heads // 2 - 2, earlier=d_kv1
    )
    if ringed:
        d_q1_c, d_kv1, d_far_c = lax.optimization_barrier((d_q1_c, d_kv1, d_far_c, cross_ring.ahead, cross_ring.behind))[:3]
        cross_ring.wait(d_q1_c)
        cross_ring.hop()
    d_q1 = jnp.concatenate([d_q1_a, d_q1_b, d_q1_c], 0)
    if ringed:
        (table_rows,) = step(
            table_kernel, (which, starts), [below, upto, d_far_a, d_far_b, d_far_c], [b16(8 * EXTRA, 3 * half)]
        )
        d_kv1 = held(d_kv1, table_rows)
        d_query_one, d_kv_one = step(
            first_weights_kernel, which, [d_q1, d_kv1, n1_t], [b16(width, half), b16(width, 2 * half)]
        )
        cross_ring.wait(d_q1_c)
        cross_ring.hop()
        pieces = list(cut_apart(ring, [d_query_one, d_kv_one], table_rows))
        pieces[-2:] = lax.optimization_barrier((*pieces[-2:], *cross_ring.sent))[:2]
        self_ring = Scatter(pieces)
        self_ring.wait(d_memory_far_sum)
        self_ring.hop()
        d_q1 = held(d_q1, self_ring.ahead, self_ring.behind)
        self_ring.hop()
    out_other = core_swap(out_other)
    if ringed:
        after, d_memory = held(after, self_ring.own), held(d_memory, self_ring.own)
    (output,) = step(output_kernel, which, [after, out_own, out_other], [f32(rows, width)])
    d_memory = d_memory + d_memory_far_sum.astype(F32)
    near, low = step(
        first_back_kernel, which, [d_q1, d_kv1, query_one, kv_one], [f32(pair, width), b16(pair, width)]
    )
    low = core_swap(low)
    d_n1, d_n1_far = step(first_sum_kernel, which, [near, low], [f32(rows, width), b16(rows, width)])
    d_n1_other = far_swap(d_n1_far)
    (d_input,) = step(
        input_kernel, which, [x_own, gains, d_n1, d_n1_other, d_middle], [f32(rows, width)]
    )

    blocks = half // 128
    plain = lambda start: ([start + 128 * i for i in range(blocks)], half, 128)
    turns = lambda start: [([start + 256 * i + 128 * t for i in range(blocks)], half, 128) for t in range(2)]
    if ringed:
        self_ring.wait(d_n1_far)
        hidden = lambda start: ([start + 128 * i for i in range(wide // 128)], 128, 256)
        d_gate_out, d_up_out, d_down_out, d_gain_three = finish(
            which, feed_own, feed_other, shard_rows, [hidden(0), hidden(wide)], (gate_weight, up_weight), gain_rows[2], 2 * wide
        )
        cross_sum = cross_ring.total()
        cross_own, cross_other = owners(cross_sum)
        self_ring.wait(d_down_out, cross_sum)
        self_ring.hop()
        self_ring.wait(d_n1_other)
        d_cross = finish(
            which,
            cross_own,
            cross_other,
            shard_rows,
            [plain(0), *turns(half), plain(3 * half), plain(4 * half)],
            (cross_query,),
            gain_rows[1],
        )
        self_sum = self_ring.total()
        self_own = held(add(self_sum, far_swap(self_sum)), d_input, d_cross[0], output, d_memory)
        self_other = core_swap(self_own)
        d_self = finish(
            which,
            self_own,
            self_other,
            shard_rows,
            [plain(0), *turns(half)],
            (self_query, self_key, self_value),
            gain_rows[0],
        )
        table_own, table_other = [v[shard_rows, : shard_rows // 2].astype(F32) for v in (self_own, self_other)]
        d_gains = [d_self[3][:, 0], d_cross[5][:, 0], d_gain_three[:, 0]]
        d_output_one_out = d_cross[4]
    else:
        d_query_one, d_kv_one = step(
            first_weights_kernel, which, [d_q1, d_kv1, n1_t], [b16(width, half), b16(width, 2 * half)]
        )

        def whole(both, axis=1):
            own, other = both
            return jnp.concatenate([jnp.where(first, own, other), jnp.where(first, other, own)], axis).astype(F32)

        def plain_owners(value):
            return owners(scatter_plain(value))

        def kv_whole(both):
            pick = lambda v, turn: v.reshape(shard_rows, -1, 2, 128)[:, :, turn].reshape(shard_rows, half)
            return [whole([pick(v, turn) for v in both]) for turn in range(2)]

        def hidden_whole(both):
            both = [v.reshape(shard_rows, shards, 1, hidden_half) for v in both]
            return whole(both, 2).reshape(shard_rows, hidden_all)

        def in_order(value):
            return jnp.where(first, value, jnp.concatenate([value[half:], value[:half]], 0))

        far = (gaps[:, None] * 256 + jnp.arange(512, dtype=jnp.int32)[None] - 255).reshape(-1)
        inside = ((far[None] >= below[0][:, None]) & (far[None] < upto[0][:, None])).astype(F32)
        d_far = jnp.concatenate([d_far_a, d_far_b, d_far_c], 0).reshape(heads, -1)
        d_table = jnp.einsum("hd,bd->hb", d_far, inside, precision=lax.Precision.HIGHEST).reshape(1, -1)
        d_table = jnp.concatenate([jnp.where(first, d_table, 0.0), jnp.where(first, 0.0, d_table)], 1)
        d_table = d_table.reshape(shards, shard_rows // 2).astype(BF)

        def gain_grad(gain, *pairs):
            total = sum(jnp.sum(w.astype(BF).astype(F32) * g, 1) for w, g in pairs)
            return total / gain.astype(BF).astype(F32)

        d_gate_out, d_up_out = [hidden_whole(plain_owners(v)) for v in (d_gate_up_w[:, :wide], d_gate_up_w[:, wide:])]
        d_down_out = whole(plain_owners(d_down_w), 0)
        d_cross = [whole(plain_owners(d_query_two)), *kv_whole(plain_owners(d_kv_two))]
        d_cross.append(whole(plain_owners(in_order(d_out_two))))
        d_output_one_out = whole(plain_owners(in_order(d_out_one)))
        d_self = [whole(plain_owners(d_query_one)), *kv_whole(plain_owners(d_kv_one))]
        table_own, table_other = [v[0].astype(F32) for v in plain_owners(d_table)]
        d_gains = [
            gain_grad(self_gain, (self_query, d_self[0]), (self_key, d_self[1]), (self_value, d_self[2])),
            gain_grad(cross_gain, (cross_query, d_cross[0])),
            gain_grad(feed_gain, (gate_weight, d_gate_out), (up_weight, d_up_out)),
        ]
    d_bucket = table_own + table_other

    return (
        output[None],
        d_input[None],
        d_memory[None],
        d_gains[0],
        d_self[0],
        d_self[1],
        d_self[2],
        d_output_one_out,
        d_bucket,
        d_gains[1],
        d_cross[0],
        d_cross[1],
        d_cross[2],
        d_cross[3],
        d_gains[2],
        d_gate_out,
        d_up_out,
        d_down_out,
    )


def solution(mesh):
    split = P("fsdp", "rep", None)
    vector, matrix = P("fsdp"), P("fsdp", None)
    weights = (
        (vector,)
        + (matrix,) * 4
        + (vector, vector)
        + (matrix,) * 4
        + (vector,)
        + (matrix,) * 3
    )
    return jax.shard_map(
        per_device,
        mesh=mesh,
        in_specs=(split, split, vector, P(), split) + weights,
        out_specs=(split, split, split) + weights,
        check_vma=False,
    )
```

```python
import functools

import jax
import jax.numpy as jnp
from jax import lax
from jax.experimental import pallas as pl
from jax.experimental.pallas import tpu as pltpu
from jax.sharding import PartitionSpec as P

HEAD = 64
BUCKETS = 32
EXTRA = 16
EPS = 1e-06
NEG = -1e30
BF = jnp.bfloat16
F32 = jnp.float32
NN = (((1,), (0,)), ((), ()))
NT = (((1,), (1,)), ((), ()))
TN = (((0,), (0,)), ((), ()))
TT = (((0,), (1,)), ((), ()))

CORE = [(0, 1), (1, 0), (2, 3), (3, 2)]
FAR = [(0, 2), (2, 0), (1, 3), (3, 1)]


def core_swap(value):
    return lax.ppermute(value, "rep", CORE)


def far_swap(value):
    return lax.ppermute(value, "rep", FAR)


def dot(left, right, dims=NN):
    return lax.dot_general(left, right, dims, preferred_element_type=F32)


def half_rows(pair, head):
    row = lax.broadcasted_iota(jnp.int32, pair.shape, 0)
    keep = (row < HEAD) if head == 0 else (row >= HEAD)
    return jnp.where(keep, pair, jnp.zeros_like(pair))


def three_terms(value):
    first = value.astype(BF)
    rest = value - first.astype(F32)
    second = rest.astype(BF)
    third = (rest - second.astype(F32)).astype(BF)
    return first, second, third


def extra_rows(first_row, vector):
    terms = three_terms(-vector)
    row = lax.broadcasted_iota(jnp.int32, (128, vector.shape[1]), 0)
    out = jnp.where(row == 0, first_row, 0.0)
    for place, term in enumerate(terms):
        out = jnp.where(row == place + 1, term.astype(F32), out)
    return out.astype(BF)


def spread(line, starts, head, part, blocks, lanes):
    block = 256
    rows = []
    for j in range(blocks):
        tiles = []
        for i in range(lanes):
            start = pl.multiple_of(starts[(part * blocks + j) * lanes + i], 128)
            row = line[pl.ds(head, 1), pl.ds(start, 2 * block)]
            tile = pltpu.roll(jnp.broadcast_to(row, (block, 2 * block)), 0, 1, stride=1, stride_axis=0)
            tiles.append(tile[:, block:])
        rows.append(jnp.concatenate(tiles, 1))
    return jnp.concatenate(rows, 0)


def attend_kernel(chunk, biased, base, *refs):
    if biased:
        starts, query, keyvalue, line, mixed, log_total = refs
    else:
        query, keyvalue, extra, mixed, log_total = refs
    keys, rows = keyvalue.shape[0], query.shape[1]
    key, value = keyvalue.at[:, pl.ds(0, 128)], keyvalue.at[:, pl.ds(128, 128)]
    pair = query[...]
    row = lax.broadcasted_iota(jnp.int32, (128, rows), 0)
    one = jnp.where(row == 0, 1.0, 0.0).astype(BF)
    wide = [half_rows(pair, h) for h in range(2)]
    if not biased:
        wide = [jnp.concatenate([w, one], 0) for w in wide]

    def score(part, head):
        span = pl.ds(part * chunk, chunk)
        if not biased:
            return dot(jnp.concatenate([key[span, :], extra[span, :]], 1), wide[head])
        full = 2 * (base + pl.program_id(0)) + head
        return dot(key[span, :], wide[head]) + spread(line, starts, full, part, chunk // 256, rows // 256)

    highest = [jnp.full((1, rows), NEG, F32)] * 2
    total = [jnp.zeros((1, rows), F32)] * 2
    acc = [jnp.zeros((HEAD, rows), F32)] * 2
    steps = [(part, head) for part in range(keys // chunk) for head in range(2)]
    ahead = score(*steps[0])
    for index, (part, head) in enumerate(steps):
        scores = ahead
        if index + 1 < len(steps):
            ahead = score(*steps[index + 1])
        span = pl.ds(part * chunk, chunk)
        top = jnp.maximum(highest[head], jnp.max(scores, 0, keepdims=True))
        soft = jnp.exp(scores - top)
        scale = jnp.exp(highest[head] - top)
        total[head] = total[head] * scale + jnp.sum(soft, 0, keepdims=True)
        product = dot(value[span, :], soft.astype(BF), TN)[head * HEAD : (head + 1) * HEAD]
        acc[head] = acc[head] * scale + product
        highest[head] = top
    for head in range(2):
        mixed[pl.ds(head * HEAD, HEAD), :] = (acc[head] / total[head]).astype(BF)
        log_total[0, pl.ds(head, 1), :] = highest[head] + jnp.log(total[head])


def attend(query, keyvalue, extra, line=None, starts=None, chunk=512, base=0, pairs=None, modelled=0.3):
    rows, keys = query.shape[1], keyvalue.shape[0]
    pairs = query.shape[0] // 128 if pairs is None else pairs
    width = pairs * 128
    biased = line is not None
    in_specs = [pl.BlockSpec((128, rows), lambda p, *s: (p + base, 0)), pl.BlockSpec((keys, 256), lambda p, *s: (0, p + base))]
    out_specs = [pl.BlockSpec((128, rows), lambda p, *s: (p, 0)), pl.BlockSpec((1, 8, rows), lambda p, *s: (p, 0, 0))]
    out_shape = [jax.ShapeDtypeStruct((width, rows), BF), jax.ShapeDtypeStruct((pairs, 8, rows), F32)]
    args = [query, keyvalue]
    if biased:
        args = [starts] + args + [line]
        in_specs.append(pl.BlockSpec(line.shape, lambda p, *s: (0, 0)))
    else:
        args.append(extra)
        in_specs.append(pl.BlockSpec((keys, 128), lambda p, *s: (0, 0)))
    return pl.pallas_call(
        functools.partial(attend_kernel, chunk, biased, base),
        grid_spec=pltpu.PrefetchScalarGridSpec(
            num_scalar_prefetch=int(biased), grid=(pairs,), in_specs=in_specs, out_specs=out_specs
        ),
        out_shape=out_shape,
        compiler_params=pltpu.CompilerParams(vmem_limit_bytes=12 * 2**20),
        cost_estimate=pl.CostEstimate(flops=1, bytes_accessed=1 + int(3.7e6 * modelled), transcendentals=0),
    )(*args)


def attend_back_kernel(chunk, biased, chained, base, *refs):
    if biased:
        starts, query, keyvalue, extra, mixed, grad, log_total, line = refs[:8]
        d_query, d_keyvalue, d_far = refs[8 + chained :]
    else:
        query, keyvalue, extra, mixed, grad, log_total = refs[:6]
        d_query, d_keyvalue = refs[6 + chained :]
    keys, rows = keyvalue.shape[0], query.shape[1]
    key, value = keyvalue.at[:, pl.ds(0, 128)], keyvalue.at[:, pl.ds(128, 128)]
    pair, grad_pair = query[...], grad[...]
    product = mixed[...].astype(F32) * grad_pair.astype(F32)
    q_half = [half_rows(pair, h) for h in range(2)]
    g_half = [half_rows(grad_pair, h) for h in range(2)]
    q_wide, g_wide = [], []
    for head in range(2):
        inner = jnp.sum(product[head * HEAD : (head + 1) * HEAD], 0, keepdims=True)
        logs = log_total[0, pl.ds(head, 1), :]
        q_wide.append(jnp.concatenate([q_half[head], extra_rows(1.0, logs)], 0))
        g_wide.append(jnp.concatenate([g_half[head], extra_rows(0.0, inner)], 0))
    if biased:
        block = 256
        down = lax.broadcasted_iota(jnp.int32, (block, block), 0)
        over = lax.broadcasted_iota(jnp.int32, (block, block), 1)
        flip = jnp.where(down + over == block - 1, 1.0, 0.0).astype(BF)
    acc = [jnp.zeros((HEAD, rows), F32) for _ in range(2)]
    for part in range(keys // chunk):
        span = pl.ds(part * chunk, chunk)
        key_wide = jnp.concatenate([key[span, :], extra[span, :]], 1)
        value_wide = jnp.concatenate([value[span, :], extra[span, :]], 1)
        dv, dk = 0.0, 0.0
        for head in range(2):
            scores = dot(key_wide, q_wide[head])
            if biased:
                full = 2 * (base + pl.program_id(0)) + head
                scores = scores + spread(line, starts, full, part, chunk // 256, rows // 256)
            soft = jnp.exp(scores)
            d_scores = (soft * dot(value_wide, g_wide[head])).astype(BF)
            dv = dv + dot(soft.astype(BF), g_half[head], NT)
            dk = dk + dot(d_scores, q_half[head], NT)
            step = dot(key[span, :], d_scores, TN)[head * HEAD : (head + 1) * HEAD]
            acc[head] = acc[head] + step
            if biased:
                for j in range(chunk // block):
                    for i in range(rows // block):
                        tile = d_scores[j * block : (j + 1) * block, i * block : (i + 1) * block]
                        tile = jnp.concatenate([dot(flip, tile), jnp.zeros((block, block), F32)], 1)
                        tile = pltpu.roll(tile, 0, 1, stride=1, stride_axis=0)
                        place = (part * (chunk // block) + j) * (rows // block) + i
                        d_far[0, head, pl.ds(place, 1), :] = jnp.sum(tile, 0, keepdims=True)
        d_keyvalue[span, :] = jnp.concatenate([dk.astype(BF), dv.astype(BF)], 1)
    for head in range(2):
        d_query[pl.ds(head * HEAD, HEAD), :] = acc[head].astype(BF)


def attend_back(
    query, keyvalue, extra, mixed, grad, log_total, line=None, starts=None, chunk=512, base=0, pairs=None, earlier=None, modelled=0.3
):
    rows, keys = query.shape[1], keyvalue.shape[0]
    pairs = query.shape[0] // 128 if pairs is None else pairs
    width = pairs * 128
    biased = line is not None
    across = pl.BlockSpec((128, rows), lambda p, *s: (p + base, 0))
    along = pl.BlockSpec((keys, 256), lambda p, *s: (0, p + base))
    in_specs = [
        across,
        along,
        pl.BlockSpec((keys, 128), lambda p, *s: (0, 0)),
        across,
        across,
        pl.BlockSpec((1, 8, rows), lambda p, *s: (p + base, 0, 0)),
    ]
    args = [query, keyvalue, extra, mixed, grad, log_total]
    out_specs = [pl.BlockSpec((128, rows), lambda p, *s: (p, 0)), along]
    out_shape = [jax.ShapeDtypeStruct((width, rows), BF), jax.ShapeDtypeStruct(keyvalue.shape, BF)]
    if biased:
        in_specs.append(pl.BlockSpec(line.shape, lambda p, *s: (0, 0)))
        args = [starts] + args + [line]
        blocks = (keys // 256) * (rows // 256)
        out_specs.append(pl.BlockSpec((1, 2, blocks, 512), lambda p, *s: (p, 0, 0, 0)))
        out_shape.append(jax.ShapeDtypeStruct((pairs, 2, blocks, 512), F32))
    aliases = {}
    if earlier is not None:
        aliases = {len(args): 1}
        in_specs.append(pl.BlockSpec(memory_space=pl.ANY))
        args.append(earlier)
    return pl.pallas_call(
        functools.partial(attend_back_kernel, chunk, biased, int(earlier is not None), base),
        grid_spec=pltpu.PrefetchScalarGridSpec(
            num_scalar_prefetch=int(biased), grid=(pairs,), in_specs=in_specs, out_specs=out_specs
        ),
        out_shape=out_shape,
        input_output_aliases=aliases,
        compiler_params=pltpu.CompilerParams(vmem_limit_bytes=10 * 2**20),
        cost_estimate=pl.CostEstimate(flops=1, bytes_accessed=1 + int(3.7e6 * modelled), transcendentals=0),
    )(*args)


def project_blocks(blocks, weight):
    def kernel(*refs):
        weight, out = refs[-2:]
        row = 0
        for block in refs[:-2]:
            for part in range(block.shape[0] // blocks[0].shape[0]):
                count = blocks[0].shape[0]
                out[pl.ds(row, count), :] = dot(block[pl.ds(part * count, count), :], weight[...]).astype(BF)
                row += count

    rows = sum(block.shape[0] for block in blocks)
    return pl.pallas_call(
        kernel,
        in_specs=[pl.BlockSpec(block.shape, lambda: (0, 0)) for block in blocks] + [pl.BlockSpec(memory_space=pltpu.VMEM)],
        out_specs=pl.BlockSpec(memory_space=pltpu.VMEM),
        out_shape=jax.ShapeDtypeStruct((rows, weight.shape[1]), BF),
        compiler_params=pltpu.CompilerParams(vmem_limit_bytes=12 * 2**20),
        cost_estimate=pl.CostEstimate(flops=1, bytes_accessed=1, transcendentals=0),
    )(*blocks, weight)


def beside(left, right):
    rows, half = left.shape
    return jnp.stack([left.reshape(rows, -1, 128), right.reshape(rows, -1, 128)], 2).reshape(rows, 2 * half)


VMEM = pl.BlockSpec(memory_space=pltpu.VMEM)


def whole_block(shape):
    return pl.BlockSpec(shape, lambda *i: (0,) * len(shape), pipeline_mode=pl.Buffered(1))


def step(kernel, core, args, shapes, mib=10, near=(), scratch=()):
    scalars = core if isinstance(core, tuple) else (core,)
    return pl.pallas_call(
        kernel,
        grid_spec=pltpu.PrefetchScalarGridSpec(
            num_scalar_prefetch=len(scalars),
            grid=(1,),
            in_specs=[VMEM if i in near else whole_block(arg.shape) for i, arg in enumerate(args)],
            out_specs=[VMEM] * len(shapes),
            scratch_shapes=list(scratch),
        ),
        out_shape=[jax.ShapeDtypeStruct(shape, kind) for shape, kind in shapes],
        compiler_params=pltpu.CompilerParams(vmem_limit_bytes=mib * 2**20),
        cost_estimate=pl.CostEstimate(flops=1, bytes_accessed=1, transcendentals=0),
    )(*scalars, *args)


def inverse_rms(value):
    return lax.rsqrt(jnp.mean(value * value, -1, keepdims=True) + EPS)


def norm_back(value, inverse, gain, grad):
    scaled = grad * gain
    return inverse * (scaled - value * (inverse * inverse) * jnp.mean(scaled * value, -1, keepdims=True))


def rows_turned(ref):
    half = ref.shape[0] // 2
    return jnp.concatenate([ref[pl.ds(half, half), :], ref[pl.ds(0, half), :]], 0)


def lanes_turned(ref):
    half = ref.shape[1] // 2
    return jnp.concatenate([ref[:, pl.ds(half, half)], ref[:, pl.ds(0, half)]], 1)


def halves(core, half):
    return pl.ds(pl.multiple_of(core[0] * half, 128), half), pl.ds(pl.multiple_of((1 - core[0]) * half, 128), half)


def first_kernel(core, own, far, near, diagonal, gain, w_query, w_keyvalue, query, keyvalue, normed_t, normed):
    rows = own.shape[0]
    for place, block in enumerate((own, far, near, diagonal)):
        value = block[...].astype(F32)
        value = value * inverse_rms(value) * gain[pl.ds(0, 1), :]
        normed[pl.ds(place * rows, rows), :] = value.astype(BF)
        normed_t[:, pl.ds(place * rows, rows)] = value.T.astype(BF)
    keyvalue[...] = dot(normed[...], w_keyvalue[...]).astype(BF)
    mine = jnp.concatenate([normed[pl.ds(0, rows), :], normed[pl.ds(2 * rows, rows), :]], 0)
    query[...] = dot(mine, w_query[...]).T.astype(BF)


def prepare_kernel(core, extras, buckets, gains, line):
    count = gains.shape[1] // 8
    lines = extras[...].astype(F32).T
    gains[...] = lines[:8]
    table = jnp.concatenate([lines[3:4, f * count : f * count + count // 2] for f in range(8)], 1)
    entries = table.shape[1]
    heads = entries // BUCKETS // 2
    head = lax.broadcasted_iota(jnp.int32, (8, entries), 0)
    entry = lax.broadcasted_iota(jnp.int32, (8, entries), 1)
    first = (core[0] * heads + head) * BUCKETS
    mine = (entry >= first) & (entry < first + BUCKETS) & (head < heads)
    rows = jnp.where(mine, jnp.broadcast_to(table, (8, entries)), 0.0).astype(BF)
    length = buckets.shape[1]
    code = lax.broadcasted_iota(jnp.int32, (entries, length), 0) & (BUCKETS - 1)
    hot = jnp.where(code == buckets[...], 1.0, 0.0).astype(BF)
    line[:, pl.ds(0, length)] = jnp.full((8, length), NEG, F32)
    line[:, pl.ds(length, length)] = dot(rows, hot)


def table_kernel(core, starts, below, upto, *refs):
    parts, out = refs[:-1], refs[-1]
    heads = sum(2 * far.shape[0] for far in parts)
    total = jnp.zeros((8, BUCKETS), F32)
    for block in range(8):
        rows = [far[p, h, pl.ds(block, 1), :] for far in parts for p in range(far.shape[0]) for h in range(2)]
        rows = jnp.concatenate(rows + [jnp.zeros((8 - heads, 512), F32)], 0)
        distance = lax.broadcasted_iota(jnp.int32, (512, BUCKETS), 0) + (starts[block] - 1023)
        hot = jnp.where((distance >= below[...]) & (distance < upto[...]), 1.0, 0.0).astype(BF)
        for term in three_terms(rows):
            total = total + dot(term, hot)
    entries = 2 * heads * BUCKETS
    spot = lax.broadcasted_iota(jnp.int32, (BUCKETS, entries), 1) - lax.broadcasted_iota(jnp.int32, (BUCKETS, entries), 0)
    line = jnp.zeros((1, entries), F32)
    for head in range(heads):
        pick = jnp.where(spot == (core[0] * heads + head) * BUCKETS, 1.0, 0.0).astype(BF)
        line = line + dot(total[head : head + 1].astype(BF), pick)
    out[...] = jnp.zeros(out.shape, BF)
    count = entries // 8
    for f in range(8):
        out[pl.ds(f * EXTRA, 1), pl.ds(0, count)] = line[:, f * count : (f + 1) * count].astype(BF)


def mix_kernel(core, mixed, weight, w_theirs, part, low_own, low_other):
    half = mixed.shape[0]
    mine, theirs = halves(core, half)
    part[:, mine] = dot(mixed[...], weight[pl.ds(0, half), :], TN)
    part[:, theirs] = dot(mixed[...], w_theirs[pl.ds(half, half), :], TN)
    rows = low_own.shape[0]
    low_own[...] = part[pl.ds(0, rows), :].astype(BF)
    low_other[...] = part[pl.ds(rows, rows), :].astype(BF)


def stacked(refs):
    blocks = [ref[...].astype(F32) for ref in refs]
    return blocks[0] if len(blocks) == 1 else jnp.concatenate(blocks, 0)


def norm_kernel(parts, projected, which, core, *refs):
    base, (part, own, other, gain) = refs[:parts], refs[parts : parts + 4]
    value, normed, normed_t = refs[parts + 4 + projected : parts + 7 + projected]
    whole = stacked(base) + part[...] + stacked((own, other))
    value[...] = whole
    whole = whole * inverse_rms(whole) * gain[pl.ds(which, 1), :]
    normed[...] = whole.astype(BF)
    normed_t[...] = whole.T.astype(BF)
    if projected:
        refs[-1][...] = dot(normed[...], refs[parts + 4][...]).T.astype(BF)


def feed_kernel(core, normed, normed_t, gate, up, down, cot_own, cot_other, own, other, grads, d_down, d_normed, d_low_own, d_low_other):
    wide = gate.shape[1]
    scale, cubic = 0.7978845608028654, 0.044715
    grad_out = jnp.concatenate([cot_own[...], cot_other[...]], 0)
    total, back_total = 0.0, 0.0
    for start in range(0, wide, 256):
        span = pl.ds(start, 256)
        g = dot(normed[...], gate[:, span])
        u = dot(normed[...], up[:, span])
        square = g * g
        t = jnp.tanh(scale * (g + cubic * square * g))
        act = 0.5 * g * (1.0 + t)
        slope = 0.5 * (1.0 + t) + 0.5 * g * (1.0 - t * t) * (scale * (1.0 + 3.0 * cubic * square))
        hidden = (act * u).astype(BF)
        d_hidden = dot(grad_out, down[span, :], NT)
        d_gate = (d_hidden * u * slope).astype(BF)
        d_up = (d_hidden * act).astype(BF)
        total = total + dot(hidden, down[span, :])
        back_total = back_total + dot(d_gate, gate[:, span], NT) + dot(d_up, up[:, span], NT)
        grads[:, span] = dot(normed_t[...], d_gate).astype(BF)
        grads[:, pl.ds(wide + start, 256)] = dot(normed_t[...], d_up).astype(BF)
        d_down[span, :] = dot(hidden, grad_out, TN).astype(BF)
    rows = own.shape[0]
    own[...] = total[:rows]
    other[...] = total[rows:].astype(BF)
    d_normed[...] = back_total
    d_low_own[...] = back_total[:rows].astype(BF)
    d_low_other[...] = back_total[rows:].astype(BF)


def back_kernel(parts, which, core, *refs):
    part, own, other, value, gain = refs[:5]
    base = refs[5 : 5 + parts]
    weight, w_theirs, mixed, mixed_other = refs[5 + parts : 9 + parts]
    d_value, d_mixed, d_weight = refs[9 + parts :]
    half = weight.shape[1]
    grad = part[...] + stacked((own, other))
    whole = value[...]
    d_value[...] = stacked(base) + norm_back(whole, inverse_rms(whole), gain[pl.ds(which, 1), :], grad)
    mine, theirs = halves(core, half)
    d_mine, d_theirs = d_value[:, mine].astype(BF), d_value[:, theirs].astype(BF)
    d_mixed[...] = (dot(weight[pl.ds(0, half), :], d_mine, NT) + dot(w_theirs[pl.ds(half, half), :], d_theirs, NT)).astype(BF)
    d_weight[pl.ds(0, half), :] = dot(mixed[...], d_mine).astype(BF)
    d_weight[pl.ds(half, half), :] = dot(lanes_turned(mixed_other), d_mine).astype(BF)


def query_kernel(core, d_query, weight, normed_t, part, low_own, low_other, d_weight):
    grad = d_query[...].astype(F32).T.astype(BF)
    total = dot(grad, weight[...], NT)
    part[...] = total
    rows = low_own.shape[0]
    low_own[...] = total[:rows].astype(BF)
    low_other[...] = total[rows:].astype(BF)
    d_weight[...] = dot(normed_t[...], d_query[...], NT).astype(BF)


def memory_core_kernel(core, d_keyvalue, weight, out):
    rows = out.shape[0]
    out[...] = dot(d_keyvalue[pl.ds(rows, rows), :], weight[...], NT).astype(BF)


def memory_weight_kernel(core, memory_t, d_keyvalue, out):
    out[...] = dot(memory_t[...], d_keyvalue[...]).astype(BF)


def memory_near_kernel(core, d_keyvalue, weight, other, own, far):
    rows = own.shape[0]
    own[...] = dot(d_keyvalue[pl.ds(0, rows), :], weight[...], NT) + other[pl.ds(0, rows), :].astype(F32)
    total = dot(d_keyvalue[pl.ds(rows, rows), :], weight[...], NT) + other[pl.ds(rows, rows), :].astype(F32)
    far[...] = total.astype(BF)


def turn_kernel(core, *refs):
    blocks, out = refs[:-1], refs[-1]
    for place, block in enumerate(blocks):
        rows = block.shape[0]
        out[:, pl.ds(place * rows, rows)] = block[...].astype(F32).T.astype(BF)


def first_weights_kernel(core, d_query, d_keyvalue, normed_t, d_w_query, d_w_keyvalue):
    rows = d_query.shape[1] // 2
    d_w_query[...] = (
        dot(normed_t[:, pl.ds(0, rows)], d_query[:, pl.ds(0, rows)], NT)
        + dot(normed_t[:, pl.ds(2 * rows, rows)], d_query[:, pl.ds(rows, rows)], NT)
    ).astype(BF)
    d_w_keyvalue[...] = dot(normed_t[...], d_keyvalue[...]).astype(BF)


def first_back_kernel(core, d_query, d_keyvalue, w_query, w_keyvalue, near, low):
    rows = d_query.shape[1] // 2
    grad = d_query[...].astype(F32).T.astype(BF)
    near[...] = dot(d_keyvalue[pl.ds(0, 2 * rows), :], w_keyvalue[...], NT)
    near[pl.ds(0, rows), :] += dot(grad[:rows], w_query[...], NT)
    total = dot(d_keyvalue[pl.ds(2 * rows, 2 * rows), :], w_keyvalue[...], NT)
    low[pl.ds(0, rows), :] = (total[:rows] + dot(grad[rows:], w_query[...], NT)).astype(BF)
    low[pl.ds(rows, rows), :] = total[rows:].astype(BF)


def first_sum_kernel(core, near, other, own, far):
    rows = own.shape[0]
    own[...] = near[pl.ds(0, rows), :] + other[pl.ds(0, rows), :].astype(F32)
    far[...] = (near[pl.ds(rows, rows), :] + other[pl.ds(rows, rows), :].astype(F32)).astype(BF)


def output_kernel(core, after, own, other, out):
    out[...] = after[pl.ds(0, out.shape[0]), :] + own[...] + other[...].astype(F32)


def input_kernel(core, value, gain, own, far, base, out):
    whole = value[...].astype(F32)
    grad = own[...] + far[...].astype(F32)
    start = base[pl.ds(0, out.shape[0]), :]
    out[...] = start + norm_back(whole, inverse_rms(whole), gain[pl.ds(0, 1), :], grad)


def gather_plain(local):
    return lax.all_gather(local, "fsdp", axis=0, tiled=True)


def scatter_plain(whole):
    return lax.psum_scatter(whole, "fsdp", scatter_dimension=0, tiled=True)


RING = (0, 2, 4, 6, 7, 5, 3, 1)
FORTH = [(RING[i], RING[(i + 1) % 8]) for i in range(8)]
BACK = [(after, before) for before, after in FORTH]


def forth(value):
    return lax.ppermute(value, "fsdp", FORTH)


def back(value):
    return lax.ppermute(value, "fsdp", BACK)


def ring_places():
    shard = lax.axis_index("fsdp")
    place = jnp.where(shard % 2 == 0, shard // 2, 7 - shard // 2)
    places = (place + jnp.array([0, -1, 1, -2, 2, -3, 3, 4], jnp.int32)) % 8
    return jnp.where(places < 4, 2 * places, 15 - 2 * places)


def vmem_call(kernel, scalars, args, out_shape, mib=10):
    return pl.pallas_call(
        kernel,
        grid_spec=pltpu.PrefetchScalarGridSpec(
            num_scalar_prefetch=1,
            grid=(1,),
            in_specs=[whole_block(arg.shape) for arg in args],
            out_specs=[whole_block(out.shape) for out in out_shape],
        ),
        out_shape=out_shape,
        compiler_params=pltpu.CompilerParams(vmem_limit_bytes=mib * 2**20),
    )(scalars, *args)


def pack_kernel(place, query, key, value, output_one, output_two, query_two, key_two, value_two, *refs):
    vectors, out = refs[:4], refs[4]
    rows, half = query.shape
    out[:, pl.ds(0, half)] = query[...].astype(BF)
    out[:, pl.ds(3 * half, half)] = jnp.where(place[0] < 2, output_one[...], output_two[...]).astype(BF)
    out[:, pl.ds(4 * half, half)] = query_two[...].astype(BF)
    for base, pair in ((1, (key, value)), (5, (key_two, value_two))):
        for part in range(half // 128):
            for turn, weight in enumerate(pair):
                lane = base * half + part * 256 + turn * 128
                out[:, pl.ds(lane, 128)] = weight[:, pl.ds(part * 128, 128)].astype(BF)
    table = jnp.concatenate([vectors[3][...], jnp.zeros((1, rows - vectors[3].shape[1]), F32)], 1)
    lines = [vector[...] for vector in vectors[:3]] + [table, jnp.zeros((4, rows), F32)]
    lines = jnp.concatenate(lines, 0).astype(BF)
    unit = lax.broadcasted_iota(jnp.int32, (8, 128), 0) == lax.broadcasted_iota(jnp.int32, (8, 128), 1)
    out[:, pl.ds(7 * half, 128)] = dot(lines, jnp.where(unit, 1.0, 0.0).astype(BF), TN).astype(BF)


def pack_halves(kernel, core, weights, vectors, rows, mib):
    half = weights[0].shape[1] // 2
    own = pl.BlockSpec((weights[0].shape[0], half), lambda i, c: (0, lax.rem(c[0], 2)))
    columns = 7 * half + 128
    return pl.pallas_call(
        kernel,
        grid_spec=pltpu.PrefetchScalarGridSpec(
            num_scalar_prefetch=1,
            grid=(1,),
            in_specs=[own] * len(weights) + [pl.BlockSpec(v.shape, lambda i, c: (0, 0)) for v in vectors],
            out_specs=pl.BlockSpec((rows, columns), lambda i, c: (0, 0)),
        ),
        out_shape=jax.ShapeDtypeStruct((rows, columns), BF),
        compiler_params=pltpu.CompilerParams(vmem_limit_bytes=mib * 2**20),
    )(core, *weights, *vectors)


def pack_feed_kernel(core, gate, up, down, out):
    rows, wide = gate.shape[0], gate.shape[1] // 2
    for place, weight in enumerate((gate, up)):
        for part in range(wide // 128):
            start = pl.multiple_of(part * 256 + core[0] * 128, 128)
            out[:, pl.ds(place * wide + part * 128, 128)] = weight[:, pl.ds(start, 128)].astype(BF)
    half = down.shape[0] // 2
    top = pl.multiple_of(core[0] * half, 16)
    own = jnp.concatenate([down[pl.ds(top, half), pl.ds(j * 128, 128)].astype(BF) for j in range(down.shape[1] // 128)], 0)
    for part in range(wide // 128):
        out[:, pl.ds(2 * wide + part * 128, 128)] = own[part * rows : (part + 1) * rows]


def unfold_down(whole, shards, width):
    rows, wide = whole.shape[0] // shards, whole.shape[1]
    count = rows * wide // width

    def kernel(_, whole, out):
        for f in range(shards):
            tall = jnp.concatenate([whole[pl.ds(f * rows, rows), pl.ds(j * 128, 128)] for j in range(wide // 128)], 0)
            for j in range(width // 128):
                out[pl.ds(f * count, count), pl.ds(j * 128, 128)] = tall[j * count : (j + 1) * count]

    return vmem_call(kernel, jnp.zeros((1,), jnp.int32), [whole], [jax.ShapeDtypeStruct((shards * count, width), whole.dtype)])[0]


def fold_down(whole, shards, wide):
    width = whole.shape[1]
    count = whole.shape[0] // shards
    rows = count * width // wide

    def kernel(_, whole, out):
        for f in range(shards):
            tall = jnp.concatenate([whole[pl.ds(f * count, count), pl.ds(j * 128, 128)] for j in range(width // 128)], 0)
            for j in range(wide // 128):
                out[pl.ds(f * rows, rows), pl.ds(j * 128, 128)] = tall[j * rows : (j + 1) * rows]

    return vmem_call(kernel, jnp.zeros((1,), jnp.int32), [whole], [jax.ShapeDtypeStruct((shards * rows, wide), whole.dtype)])[0]


def put_in_order(scalars, parts, columns, extra=0, turned=(), fold=None):
    rows = parts[0].shape[0] - extra
    skip = parts[7].shape[0]
    total = 8 * rows

    def kernel(scalars, *refs):
        parts, outs = refs[:9], list(refs[9 : 9 + len(columns)])
        sems = refs[-1]
        if fold is not None:
            outs[-1] = refs[-2]
        copies = []
        for index, part in enumerate(parts):
            place = scalars[min(index, 7)]
            offset = skip if index == 8 else 0
            count = min(part.shape[0], rows - offset)
            lane = 0
            for turn, (out, width) in enumerate(zip(outs, columns)):
                start = place * rows
                if turn in turned:
                    start = lax.rem(start + scalars[8] * (total // 2), total)
                start = pl.multiple_of(start + offset, 16)
                copies.append((part.at[pl.ds(0, count), pl.ds(lane, width)], out.at[pl.ds(start, count), :]))
                lane += width
            if extra and index != 7:
                start = pl.multiple_of(place * extra, 16)
                copies.append(
                    (part.at[pl.ds(part.shape[0] - extra, extra), pl.ds(0, 128)], refs[9 + len(columns)].at[pl.ds(start, extra), :])
                )
        copies = [pltpu.make_async_copy(x, y, sems.at[i]) for i, (x, y) in enumerate(copies)]
        for copy in copies:
            copy.start()
        for copy in copies:
            copy.wait()
        if fold is not None:
            folded, out = refs[-2], refs[8 + len(columns)]
            wide, count = columns[-1], rows * columns[-1] // fold
            for f in range(8):
                tall = jnp.concatenate([folded[pl.ds(f * rows, rows), pl.ds(j * 128, 128)] for j in range(wide // 128)], 0)
                for j in range(fold // 128):
                    out[pl.ds(f * count, count), pl.ds(j * 128, 128)] = tall[j * count : (j + 1) * count]

    out_shape = [jax.ShapeDtypeStruct((total, width), BF) for width in columns]
    scratch = []
    if fold is not None:
        out_shape[-1] = jax.ShapeDtypeStruct((total * columns[-1] // fold, fold), BF)
        scratch.append(pltpu.VMEM((total, columns[-1]), BF))
    if extra:
        out_shape.append(jax.ShapeDtypeStruct((8 * extra, 128), BF))
    return pl.pallas_call(
        kernel,
        grid_spec=pltpu.PrefetchScalarGridSpec(
            num_scalar_prefetch=1,
            grid=(),
            in_specs=[pl.BlockSpec(memory_space=pltpu.HBM)] * 9,
            out_specs=[VMEM] * len(out_shape),
            scratch_shapes=scratch + [pltpu.SemaphoreType.DMA((9 * len(columns) + 9,))],
        ),
        out_shape=out_shape,
        compiler_params=pltpu.CompilerParams(vmem_limit_bytes=4 * 2**20),
    )(scalars, *parts)


def cut_apart(scalars, columns, extras, turned=()):
    rows = columns[0].shape[0] // 8
    extra = 0 if extras is None else EXTRA
    width = sum(c.shape[1] for c in columns)
    half = (rows + extra) // 32 * 16
    counts = [rows + extra] * 7 + [half, rows + extra - half]

    def kernel(scalars, *refs):
        blocks, outs, sems = refs[: len(columns)], refs[len(refs) - 10 : -1], refs[-1]
        copies = []
        for index, out in enumerate(outs):
            place = scalars[min(index, 7)]
            skip = half if index == 8 else 0
            count = min(out.shape[0], rows - skip)
            lane = 0
            for turn, block in enumerate(blocks):
                start = place * rows
                if turn in turned:
                    start = lax.rem(start + scalars[8] * 4 * rows, 8 * rows)
                start = pl.multiple_of(start + skip, 16)
                copies.append((block.at[pl.ds(start, count), :], out.at[pl.ds(0, count), pl.ds(lane, block.shape[1])]))
                lane += block.shape[1]
            if extra and index != 7:
                start = pl.multiple_of(place * extra, 16)
                copies.append((refs[len(columns)].at[pl.ds(start, extra), :], out.at[pl.ds(count, extra), :]))
        copies = [pltpu.make_async_copy(x, y, sems.at[i]) for i, (x, y) in enumerate(copies)]
        for copy in copies:
            copy.start()
        for copy in copies:
            copy.wait()

    args = list(columns) + ([] if extras is None else [extras])
    out_shape = [jax.ShapeDtypeStruct((count, width), BF) for count in counts]
    return pl.pallas_call(
        kernel,
        grid_spec=pltpu.PrefetchScalarGridSpec(
            num_scalar_prefetch=1,
            grid=(),
            in_specs=[VMEM] * len(args),
            out_specs=[pl.BlockSpec(memory_space=pl.ANY)] * 9,
            scratch_shapes=[pltpu.SemaphoreType.DMA((9 * len(columns) + 9,))],
        ),
        out_shape=out_shape,
        compiler_params=pltpu.CompilerParams(vmem_limit_bytes=4 * 2**20),
    )(scalars, *args)


def held(value, *earlier):
    return lax.optimization_barrier((value,) + earlier)[0]


def gather_hops(local, hops):
    ahead, behind, parts = local
    for _ in range(hops):
        ahead, behind = forth(ahead), back(behind)
        parts = parts + [ahead, behind]
    return ahead, behind, parts


def gather_end(state):
    ahead, behind, parts = state
    half = ahead.shape[0] // 32 * 16
    return parts + [forth(ahead[:half]), back(behind[half:])]


def gather_last(scalars, state, columns, hold=None, **options):
    parts = gather_end(state)
    if hold is not None:
        parts[-2:] = [held(part, hold) for part in parts[-2:]]
    return put_in_order(scalars, parts, columns, **options)


def held_hops(state, hold, hops=1):
    ahead, behind = lax.optimization_barrier((state[0], state[1], hold))[:2]
    return gather_hops((ahead, behind, state[2]), hops)


def add(left, right):
    return (left.astype(F32) + right.astype(F32)).astype(left.dtype)


def add_pair(one, two, three, four):
    def kernel(one, two, three, four, left, right):
        for whole, part, out, low in ((one, two, left, False), (three, four, right, True)):
            rows, count = whole.shape[0], part.shape[0]
            start = rows - count if low else 0
            out[pl.ds(start, count), :] = add(whole[pl.ds(start, count), :], part[...])
            if count < rows:
                rest = pl.ds(count if not low else 0, rows - count)
                out[rest, :] = whole[rest, :]

    shape = jax.ShapeDtypeStruct(one.shape, one.dtype)
    return pl.pallas_call(
        kernel,
        in_specs=[VMEM] * 4,
        out_specs=[VMEM] * 2,
        out_shape=[shape, shape],
        compiler_params=pltpu.CompilerParams(vmem_limit_bytes=4 * 2**20),
        cost_estimate=pl.CostEstimate(flops=1, bytes_accessed=1, transcendentals=0),
    )(one, two, three, four)


class Scatter:
    def __init__(self, pieces):
        self.own, *self.sides, top, low = pieces
        self.ahead, self.behind = forth(top), back(low)
        self.step = 0

    def wait(self, *others):
        self.ahead, self.behind = lax.optimization_barrier((self.ahead, self.behind) + others)[:2]

    def hop(self):
        m1, p1, m2, p2, m3, p3 = self.sides
        up, down = ((p3, m3), (p2, m2), (p1, m1))[self.step]
        ahead, behind = add_pair(up, self.ahead, down, self.behind)
        self.sent = (ahead, behind)
        self.ahead, self.behind = forth(ahead), back(behind)
        self.step += 1

    def total(self):
        return (self.own.astype(F32) + self.ahead.astype(F32) + self.behind.astype(F32)).astype(BF)


def finish(core, own, other, rows, outputs, weights=(), gain=None, down=None):
    widths = [2 * 128 * len(lanes) for lanes, _, _ in outputs]

    def kernel(core, own, other, *refs):
        weights, refs = refs[: len(weights_given)], refs[len(weights_given) :]
        if gain is not None:
            gain_ref, refs = refs[0], refs[1:]
        outs = refs[: len(outputs)]
        for side, source in ((core[0], own), (1 - core[0], other)):
            for out, (lanes, core_step, block_step) in zip(outs, outputs):
                for index, lane in enumerate(lanes):
                    place = pl.multiple_of(side * core_step + index * block_step, 128)
                    out[:, pl.ds(place, 128)] = source[pl.ds(0, rows), pl.ds(lane, 128)].astype(F32)
            if down is not None:
                out = refs[len(outputs)]
                count, width = out.shape[0] // 2, out.shape[1]
                blocks = count * width // (rows * 128)
                tall = jnp.concatenate([source[:, pl.ds(down + j * 128, 128)] for j in range(blocks)], 0)
                start = pl.multiple_of(side * count, 16)
                for j in range(width // 128):
                    out[pl.ds(start, count), pl.ds(j * 128, 128)] = tall[j * count : (j + 1) * count].astype(F32)
        if gain is not None:
            total = jnp.zeros((rows, 1), F32)
            for weight, out in zip(weights, outs):
                total = total + jnp.sum(weight[...].astype(BF).astype(F32) * out[...], 1, keepdims=True)
            line = gain_ref[...].astype(BF).astype(F32)
            spot = lax.broadcasted_iota(jnp.int32, (rows, rows), 0) == lax.broadcasted_iota(jnp.int32, (rows, rows), 1)
            column = jnp.sum(jnp.where(spot, jnp.broadcast_to(line, (rows, rows)), 0.0), 1, keepdims=True)
            refs[-1][...] = jnp.broadcast_to(total / column, (rows, 128))

    weights_given = list(weights)
    args = [own, other] + weights_given + ([] if gain is None else [gain])
    out_shape = [jax.ShapeDtypeStruct((rows, width), F32) for width in widths]
    if down is not None:
        out_shape.append(jax.ShapeDtypeStruct(down_shape(rows, own.shape[1] - down), F32))
    if gain is not None:
        out_shape.append(jax.ShapeDtypeStruct((rows, 128), F32))
    return vmem_call(kernel, core, args, out_shape)


def down_shape(rows, folded):
    return 2 * folded // 8, 8 * rows


def per_device(
    decoder_input,
    memory,
    memory_lengths,
    distance_bucket,
    cotangent,
    self_gain,
    self_query,
    self_key,
    self_value,
    self_output,
    bucket_bias,
    cross_gain,
    cross_query,
    cross_key,
    cross_value,
    cross_output,
    feed_gain,
    gate_weight,
    up_weight,
    down_weight,
):
    shards = lax.axis_size("fsdp")
    rep = lax.axis_index("rep")
    side, core = rep // 2, rep % 2
    first = core == 0
    rows = decoder_input.shape[1]
    width = decoder_input.shape[2]
    slots = memory.shape[1]
    half = width // 2
    heads = half // HEAD
    shard_rows = self_query.shape[0]
    hidden_all = gate_weight.shape[1]
    hidden_rows = down_weight.shape[0]
    hidden_half = hidden_rows // 2

    which = core.reshape(1)
    cot_own = cotangent[0]
    cot_low = cot_own.astype(BF)
    cot_other = core_swap(cot_low)
    places = jnp.stack([rep, 2 * (1 - side) + core, 2 * side + 1 - core, 2 * (1 - side) + 1 - core])

    slot = (places[:, None] * slots + jnp.arange(slots, dtype=jnp.int32)[None]).reshape(-1)
    lane = jnp.arange(128, dtype=jnp.int32)[None]
    ones = jnp.where((lane >= 1) & (lane <= 3), 1.0, 0.0)
    extra_two = (jnp.where((lane == 0) & (slot >= memory_lengths[0])[:, None], NEG, 0.0) + ones).astype(BF)
    extra_one = jnp.broadcast_to(ones, (4 * rows, 128)).astype(BF)
    codes = jnp.arange(BUCKETS, dtype=jnp.int32)
    gaps = (jnp.stack([places[0], places[2]])[None, :] - places[:, None]).reshape(-1)
    starts = gaps * 256 + 768
    below = jnp.sum((distance_bucket[None, :] < codes[:, None]).astype(jnp.int32), 1)[None]
    upto = jnp.sum((distance_bucket[None, :] <= codes[:, None]).astype(jnp.int32), 1)[None]

    ringed = shards == 8 and shard_rows % 32 == 0 and hidden_half % 128 == 0
    wide = hidden_all // 2
    if ringed:
        ring = jnp.concatenate([ring_places(), which])
        gain_rows = [gain[None] for gain in (self_gain, cross_gain, feed_gain)]
        which, ring, starts, below, upto, extra_two, gain_rows, own_side = lax.optimization_barrier(
            (which, ring, starts, below, upto, extra_two, gain_rows, side == 0)
        )

        def packed(kernel, args, rows, columns):
            return vmem_call(kernel, which, args, [jax.ShapeDtypeStruct((rows, columns), BF)])[0]

        vectors = [v[None] for v in (self_gain, cross_gain, feed_gain, bucket_bias)]
        local = pack_halves(
            pack_kernel,
            rep.reshape(1),
            [self_query, self_key, self_value, self_output, cross_output, cross_query, cross_key, cross_value],
            vectors,
            shard_rows,
            60,
        )
        state = gather_hops((local, local, [local]), 1)
    x_own, m_own = decoder_input[0], memory[0]
    x_far, m_far = far_swap(x_own), far_swap(m_own)
    x_core = core_swap(x_own)
    if ringed:
        feed = packed(pack_feed_kernel, [gate_weight, up_weight, down_weight], shard_rows, 3 * wide)
        state = held_hops(state, (feed, starts, below, upto))
        state = held_hops(state, (x_far, x_core, cot_other, extra_two))
    x_diagonal = core_swap(x_far)
    if ringed:
        state = gather_end(held_hops(state, x_diagonal, 0))
        feed = held(feed, *state[-2:])
        feed = gather_hops((feed, feed, [feed]), 1)
        query_one, kv_one, out_part, query_two, kv_two, extras = put_in_order(
            ring, state, (half, 2 * half, half, half, 2 * half, 128), turned=(2,)
        )
        out_far = far_swap(out_part)
        gains, line = step(
            prepare_kernel, which, [extras, distance_bucket[None]], [((8, width), F32), ((8, 8 * rows), F32)], near=(0,)
        )
    else:

        def own_columns(weight):
            return lax.dynamic_slice_in_dim(weight, core * half, half, 1).astype(BF)

        def own_hidden(weight):
            parts = weight.reshape(shard_rows, shards, 2, hidden_half)
            own = lax.dynamic_index_in_dim(parts, core, 2, keepdims=False)
            return own.reshape(shard_rows, wide).astype(BF)

        def own_beside(left, right):
            return beside(own_columns(left), own_columns(right))

        query_one = gather_plain(own_columns(self_query))
        kv_one = gather_plain(own_beside(self_key, self_value))
        outs = [gather_plain(own_columns(w)) for w in (self_output, cross_output)]
        out_one, out_two = [jnp.where(first, w, jnp.concatenate([w[half:], w[:half]], 0)) for w in outs]
        query_two = gather_plain(own_columns(cross_query))
        kv_two = gather_plain(own_beside(cross_key, cross_value))
        gate_matrix = gather_plain(own_hidden(gate_weight))
        up_matrix = gather_plain(own_hidden(up_weight))
        down_half = lax.dynamic_slice_in_dim(down_weight, core * hidden_half, hidden_half, 0).astype(BF)
        down_matrix = gather_plain(down_half)
        gains = jnp.stack([gather_plain(g.astype(BF)).astype(F32) for g in (self_gain, cross_gain, feed_gain)])
        table = gather_plain(bucket_bias.astype(BF)).astype(F32)
        table = lax.dynamic_index_in_dim(table.reshape(2, heads, BUCKETS), core, 0, keepdims=False)
        hot = (distance_bucket[None, :] == codes[:, None]).astype(BF)
        line = jnp.einsum("hb,bd->hd", table.astype(BF), hot, preferred_element_type=F32)
        line = jnp.concatenate([jnp.full((heads, 4 * rows), NEG, F32), line], 1)
        line = jnp.pad(line, ((0, 8 - heads), (0, 0)))

    def owners(value):
        value = add(value, far_swap(value))
        return value, core_swap(value)

    pair = 2 * rows
    f32, b16 = (lambda *shape: (shape, F32)), (lambda *shape: (shape, BF))
    blocks = [x_own, x_far, x_core, x_diagonal]
    q1, k1v1, n1_t = step(
        first_kernel,
        which,
        [*blocks, gains, query_one, kv_one],
        [b16(half, pair), b16(4 * rows, 2 * half), b16(width, 4 * rows)],
        near=(5, 6),
        scratch=[pltpu.VMEM((4 * rows, width), BF)],
    )
    m_core, m_diagonal = core_swap(m_own), core_swap(m_far)
    k2v2 = project_blocks([m_own, m_far, m_core, m_diagonal], kv_two)
    if ringed:
        q1 = held(q1, k2v2, *feed[:2])
        feed = gather_hops(feed, 1)
    o1, logs_one = attend(q1, k1v1, None, line, starts)
    if ringed:
        out_far = held(out_far, o1, *feed[:2])
        out_one, out_two = jnp.where(own_side, out_part, out_far), jnp.where(own_side, out_far, out_part)
        o1 = held(o1, *feed[:2])
        feed = held_hops(feed, o1, 1)
    out_one_other, out_two_other = core_swap(out_one), core_swap(out_two)
    part, low_own, low_other = step(
        mix_kernel, which, [o1, out_one, out_one_other], [f32(pair, width), b16(rows, width), b16(rows, width)], near=(0,)
    )
    low_own, low_other = core_swap(low_other), core_swap(low_own)
    middle, n2, n2_t, q2 = step(
        functools.partial(norm_kernel, 2, 1, 1),
        which,
        [x_own, x_core, part, low_own, low_other, gains, query_two],
        [f32(pair, width), b16(pair, width), b16(width, pair), b16(half, pair)],
        near=(2, 6),
    )
    o2_a, logs_a = attend(q2, k2v2, extra_two, base=0, pairs=1, modelled=0)
    q2_b = held(q2, o2_a)
    if ringed:
        q2_b = held(q2_b, *feed[:2])
        feed = gather_end(held_hops(feed, q2_b, 0))
    o2_b, logs_b = attend(q2_b, k2v2, extra_two, base=1, pairs=heads // 2 - 1)
    if ringed:
        o2_b = held(o2_b, *feed[-2:])
        m_own = held(m_own, o2_b)
    o2, logs_two = jnp.concatenate([o2_a, o2_b], 0), jnp.concatenate([logs_a, logs_b], 0)
    (m_turned,) = step(turn_kernel, which, [m_own, m_far, m_core, m_diagonal], [b16(width, 4 * slots)], 16)
    o1_other, o2_other = core_swap(o1), core_swap(o2)
    part, low_own, low_other = step(
        mix_kernel, which, [o2, out_two, out_two_other], [f32(pair, width), b16(rows, width), b16(rows, width)], near=(0,)
    )
    if ringed:
        low_own, low_other = lax.optimization_barrier((low_own, low_other, *feed[-2:]))[:2]
    low_own, low_other = core_swap(low_other), core_swap(low_own)
    after, n3, n3_t = step(
        functools.partial(norm_kernel, 1, 0, 2),
        which,
        [middle, part, low_own, low_other, gains],
        [f32(pair, width), b16(pair, width), b16(width, pair)],
        near=(1,),
    )
    if ringed:
        feed[-2:] = [held(part, m_turned) for part in feed[-2:]]
        gate_matrix, up_matrix, down_matrix = put_in_order(ring, feed, (wide, wide, wide), fold=width)

    out_own, out_other, d_gate_up_w, d_down_w, d_n3, low_own, low_other = step(
        feed_kernel,
        which,
        [n3, n3_t, gate_matrix, up_matrix, down_matrix, cot_low, cot_other],
        [
            f32(rows, width),
            b16(rows, width),
            b16(width, 2 * wide),
            b16(wide, width),
            f32(pair, width),
            b16(rows, width),
            b16(rows, width),
        ],
        10,
        near=(0, 1, 2, 3, 4),
    )
    d_after, d_o2, d_out_two = step(
        functools.partial(back_kernel, 2, 2),
        which,
        [d_n3, core_swap(low_other), core_swap(low_own), after, gains, cot_own, cot_other, out_two, out_two_other, o2, o2_other],
        [f32(pair, width), b16(half, pair), b16(width, half)],
    )

    back_two = functools.partial(attend_back, q2, k2v2, extra_two, o2)
    if ringed:
        feed_ring = Scatter(cut_apart(ring, [d_gate_up_w, fold_down(d_down_w, shards, wide)], None))
        feed_ring.wait(d_after)
        d_o2 = held(d_o2, feed_ring.ahead, feed_ring.behind)
        feed_ring.hop()
    d_q2_a, d_kv2 = back_two(d_o2, logs_two, base=0, pairs=1)
    d_q2_b, d_kv2 = back_two(held(d_o2, d_q2_a), logs_two, base=1, pairs=1, earlier=d_kv2)
    if ringed:
        d_q2_b = held(d_q2_b, feed_ring.ahead, feed_ring.behind)
        feed_ring.wait(d_q2_b)
        feed_ring.hop()
    d_q2_c, d_kv2 = back_two(held(d_o2, d_q2_b), logs_two, base=2, pairs=heads // 2 - 2, earlier=d_kv2)
    if ringed:
        d_q2_c, d_kv2 = lax.optimization_barrier((d_q2_c, d_kv2, feed_ring.ahead, feed_ring.behind))[:2]
        feed_ring.wait(d_q2_c)
        feed_ring.hop()
        d_q2_c, d_kv2 = lax.optimization_barrier((d_q2_c, d_kv2, *feed_ring.sent))[:2]
    d_q2 = jnp.concatenate([d_q2_a, d_q2_b, d_q2_c], 0)
    part, low_own, low_other, d_query_two = step(
        query_kernel,
        which,
        [d_q2, query_two, n2_t],
        [f32(pair, width), b16(rows, width), b16(rows, width), b16(width, half)],
    )
    low_own, low_other = core_swap(low_other), core_swap(low_own)
    d_middle, d_o1, d_out_one = step(
        functools.partial(back_kernel, 1, 1),
        which,
        [part, low_own, low_other, middle, gains, d_after, out_one, out_one_other, o1, o1_other],
        [f32(pair, width), b16(half, pair), b16(width, half)],
    )
    d_mem_core = core_swap(step(memory_core_kernel, which, [d_kv2, kv_two], [b16(2 * slots, width)], near=(0,))[0])
    (d_kv_two,) = step(memory_weight_kernel, which, [m_turned, d_kv2], [b16(width, 2 * half)], near=(1,))
    d_memory, d_memory_far = step(
        memory_near_kernel, which, [d_kv2, kv_two, d_mem_core], [f32(slots, width), b16(slots, width)], near=(0,)
    )
    d_memory_far_sum = far_swap(d_memory_far)

    cross_parts = [d_query_two, d_kv_two, d_out_two, d_out_one]
    if ringed:
        pieces = list(cut_apart(ring, cross_parts, None, (2, 3)))
        pieces[-2:] = lax.optimization_barrier((*pieces[-2:], feed_ring.ahead, feed_ring.behind))[:2]
        cross_ring = Scatter(pieces)
        feed_ring.wait(d_memory_far)
        feed_own, feed_other = owners(feed_ring.total())
        d_o1 = held(d_o1, d_memory_far)
    back_one = functools.partial(attend_back, q1, k1v1, extra_one, o1)
    d_q1_a, d_kv1, d_far_a = back_one(d_o1, logs_one, line, starts, base=0, pairs=1)
    d_o1_b = held(d_o1, d_q1_a)
    if ringed:
        d_o1_b = held(d_o1_b, cross_ring.ahead, cross_ring.behind)
        cross_ring.wait(d_q1_a)
        cross_ring.hop()
    d_q1_b, d_kv1, d_far_b = back_one(d_o1_b, logs_one, line, starts, base=1, pairs=1, earlier=d_kv1)
    if ringed:
        d_q1_b = held(d_q1_b, cross_ring.ahead, cross_ring.behind)
        cross_ring.wait(d_q1_b)
        cross_ring.hop()
    d_q1_c, d_kv1, d_far_c = back_one(
        held(d_o1, d_q1_b), logs_one, line, starts, base=2, pairs=heads // 2 - 2, earlier=d_kv1
    )
    d_q1 = jnp.concatenate([d_q1_a, d_q1_b, d_q1_c], 0)
    if ringed:
        (table_rows,) = step(
            table_kernel, (which, starts), [below, upto, d_far_a, d_far_b, d_far_c], [b16(8 * EXTRA, 3 * half)]
        )
        d_kv1 = held(d_kv1, table_rows)
        d_query_one, d_kv_one = step(
            first_weights_kernel, which, [d_q1, d_kv1, n1_t], [b16(width, half), b16(width, 2 * half)]
        )
        cross_ring.wait(d_q1_c)
        cross_ring.hop()
        pieces = list(cut_apart(ring, [d_query_one, d_kv_one], table_rows))
        pieces[-2:] = lax.optimization_barrier((*pieces[-2:], *cross_ring.sent))[:2]
        self_ring = Scatter(pieces)
        self_ring.wait(d_memory_far_sum)
        self_ring.hop()
        d_q1 = held(d_q1, self_ring.ahead, self_ring.behind)
        self_ring.hop()
    out_other = core_swap(out_other)
    if ringed:
        after, d_memory = held(after, self_ring.own), held(d_memory, self_ring.own)
    (output,) = step(output_kernel, which, [after, out_own, out_other], [f32(rows, width)])
    d_memory = d_memory + d_memory_far_sum.astype(F32)
    near, low = step(
        first_back_kernel, which, [d_q1, d_kv1, query_one, kv_one], [f32(pair, width), b16(pair, width)]
    )
    low = core_swap(low)
    d_n1, d_n1_far = step(first_sum_kernel, which, [near, low], [f32(rows, width), b16(rows, width)])
    d_n1_other = far_swap(d_n1_far)
    (d_input,) = step(
        input_kernel, which, [x_own, gains, d_n1, d_n1_other, d_middle], [f32(rows, width)]
    )

    blocks = half // 128
    plain = lambda start: ([start + 128 * i for i in range(blocks)], half, 128)
    turns = lambda start: [([start + 256 * i + 128 * t for i in range(blocks)], half, 128) for t in range(2)]
    if ringed:
        self_ring.wait(d_n1_far)
        hidden = lambda start: ([start + 128 * i for i in range(wide // 128)], 128, 256)
        d_gate_out, d_up_out, d_down_out, d_gain_three = finish(
            which, feed_own, feed_other, shard_rows, [hidden(0), hidden(wide)], (gate_weight, up_weight), gain_rows[2], 2 * wide
        )
        cross_sum = cross_ring.total()
        cross_own, cross_other = owners(cross_sum)
        self_ring.wait(d_down_out, cross_sum)
        self_ring.hop()
        self_ring.wait(d_n1_other)
        d_cross = finish(
            which,
            cross_own,
            cross_other,
            shard_rows,
            [plain(0), *turns(half), plain(3 * half), plain(4 * half)],
            (cross_query,),
            gain_rows[1],
        )
        self_sum = self_ring.total()
        self_own = held(add(self_sum, far_swap(self_sum)), d_input, d_cross[0], output, d_memory)
        self_other = core_swap(self_own)
        d_self = finish(
            which,
            self_own,
            self_other,
            shard_rows,
            [plain(0), *turns(half)],
            (self_query, self_key, self_value),
            gain_rows[0],
        )
        table_own, table_other = [v[shard_rows, : shard_rows // 2].astype(F32) for v in (self_own, self_other)]
        d_gains = [d_self[3][:, 0], d_cross[5][:, 0], d_gain_three[:, 0]]
        d_output_one_out = d_cross[4]
    else:
        d_query_one, d_kv_one = step(
            first_weights_kernel, which, [d_q1, d_kv1, n1_t], [b16(width, half), b16(width, 2 * half)]
        )

        def whole(both, axis=1):
            own, other = both
            return jnp.concatenate([jnp.where(first, own, other), jnp.where(first, other, own)], axis).astype(F32)

        def plain_owners(value):
            return owners(scatter_plain(value))

        def kv_whole(both):
            pick = lambda v, turn: v.reshape(shard_rows, -1, 2, 128)[:, :, turn].reshape(shard_rows, half)
            return [whole([pick(v, turn) for v in both]) for turn in range(2)]

        def hidden_whole(both):
            both = [v.reshape(shard_rows, shards, 1, hidden_half) for v in both]
            return whole(both, 2).reshape(shard_rows, hidden_all)

        def in_order(value):
            return jnp.where(first, value, jnp.concatenate([value[half:], value[:half]], 0))

        far = (gaps[:, None] * 256 + jnp.arange(512, dtype=jnp.int32)[None] - 255).reshape(-1)
        inside = ((far[None] >= below[0][:, None]) & (far[None] < upto[0][:, None])).astype(F32)
        d_far = jnp.concatenate([d_far_a, d_far_b, d_far_c], 0).reshape(heads, -1)
        d_table = jnp.einsum("hd,bd->hb", d_far, inside, precision=lax.Precision.HIGHEST).reshape(1, -1)
        d_table = jnp.concatenate([jnp.where(first, d_table, 0.0), jnp.where(first, 0.0, d_table)], 1)
        d_table = d_table.reshape(shards, shard_rows // 2).astype(BF)

        def gain_grad(gain, *pairs):
            total = sum(jnp.sum(w.astype(BF).astype(F32) * g, 1) for w, g in pairs)
            return total / gain.astype(BF).astype(F32)

        d_gate_out, d_up_out = [hidden_whole(plain_owners(v)) for v in (d_gate_up_w[:, :wide], d_gate_up_w[:, wide:])]
        d_down_out = whole(plain_owners(d_down_w), 0)
        d_cross = [whole(plain_owners(d_query_two)), *kv_whole(plain_owners(d_kv_two))]
        d_cross.append(whole(plain_owners(in_order(d_out_two))))
        d_output_one_out = whole(plain_owners(in_order(d_out_one)))
        d_self = [whole(plain_owners(d_query_one)), *kv_whole(plain_owners(d_kv_one))]
        table_own, table_other = [v[0].astype(F32) for v in plain_owners(d_table)]
        d_gains = [
            gain_grad(self_gain, (self_query, d_self[0]), (self_key, d_self[1]), (self_value, d_self[2])),
            gain_grad(cross_gain, (cross_query, d_cross[0])),
            gain_grad(feed_gain, (gate_weight, d_gate_out), (up_weight, d_up_out)),
        ]
    d_bucket = table_own + table_other

    return (
        output[None],
        d_input[None],
        d_memory[None],
        d_gains[0],
        d_self[0],
        d_self[1],
        d_self[2],
        d_output_one_out,
        d_bucket,
        d_gains[1],
        d_cross[0],
        d_cross[1],
        d_cross[2],
        d_cross[3],
        d_gains[2],
        d_gate_out,
        d_up_out,
        d_down_out,
    )


def solution(mesh):
    split = P("fsdp", "rep", None)
    vector, matrix = P("fsdp"), P("fsdp", None)
    weights = (
        (vector,)
        + (matrix,) * 4
        + (vector, vector)
        + (matrix,) * 4
        + (vector,)
        + (matrix,) * 3
    )
    return jax.shard_map(
        per_device,
        mesh=mesh,
        in_specs=(split, split, vector, P(), split) + weights,
        out_specs=(split, split, split) + weights,
        check_vma=False,
    )
```
